32 devices in a mesh: ctx: 16 (over z, y, x), head: 2 (over core).
Axes of the slice: x: 2, y: 2, z: 4, core: 2. Of those that a mesh axis runs over, the one named last changes fastest.
Arguments:
- queries: bfloat16 [2048, 1024], P('ctx', 'head'), may hold values from -6 to 6
- keys_values: bfloat16 [2, 2048, 1024], P(None, 'ctx', 'head'), may hold values from -6 to 6
- attn_cot: bfloat16 [2048, 1024], P('ctx', 'head'), may hold values from -768 to 768
- event_rows: bfloat16 [2048, 1024], P('ctx'), may hold values from -0.15625 to 0.15625
- adapter: bfloat16 [1024, 1024], P(None, 'head'), may hold values from -0.1875 to 0.1875
- qkv_weight: bfloat16 [3, 1024, 1024], P(None, None, 'head'), may hold values from -0.1875 to 0.1875
- starts: int32 [16], P('ctx'), may hold values from 0 to 1920, as said below
- owners: int32 [2048, 1], P('ctx'), may hold values from 0 to 15; in each aligned block of 128 rows (0 to 127, 128 to 255, ...) at most 16 rows name the same one
- slots: int32 [2048], P('ctx'), may hold values from 0 to 255
- table: float32 [4096, 1024], P('ctx', 'head'), may hold values from -0.625 to 0.625
- moment_m: float32 [4096, 1024], P('ctx', 'head'), may hold values from -0.625 to 0.625
- moment_v: float32 [4096, 1024], P('ctx', 'head'), may hold values from 0.01 to 1
Outputs:
- adapter_grad: float32 [1024, 1024], P('ctx', 'head')
- new_table: float32 [4096, 1024], P('ctx', 'head')
- new_m: float32 [4096, 1024], P('ctx', 'head')
- new_v: float32 [4096, 1024], P('ctx', 'head')
The draws below stay inside these ranges and needn't reach their ends.
Inputs may be any that keep to these rules, and one draw needn't show every extreme that they name: starts[b] lies between 0 and b * 128; the last block's start is its own first event. `owners`: among the 128 events of one index of ctx at most 16 name the same owner, and in some such block one owner is named exactly 16 times.
All inputs are finite; a program needn't handle non-finite values.
Results may differ from the reference program's by a relative error of at most 0.014.
Values may be sent and summed in bfloat16 or wider, within the bound.
No kernel may reach another device: no remote copies, remote signals or barrier semaphores. Data moves between devices by JAX's collectives and lax.ppermute only.
A program may use at most 64 MiB of HBM per device.

```python
import math
import jax
import jax.numpy as jnp
import numpy as np
from jax import lax

D = 1024
HEADS = 8
HD = 128
TOK_DEV = 128
SEQ = 2048
QBLK = 128
ROWS_DEV = 256
ROWS = 4096
CAP = 16
N_CTX = 16


def draw_starts(key, part):
    total = SEQ // QBLK
    index = jnp.arange(total, dtype=jnp.int32)
    limit = index * QBLK + 1
    picks = jax.random.randint(key, (total,), 0, limit, dtype=jnp.int32)
    return jnp.where(index == total - 1, (total - 1) * QBLK, picks).astype(jnp.int32)


def place_ends(values, rng, smallest, largest):
    place = [jax.random.randint(jax.random.fold_in(rng, axis), (), 0, length) for axis, length in enumerate(values.shape)]
    main_axis = values.shape.index(max(values.shape))
    next_to = place[:main_axis] + [(place[main_axis] + 1) % values.shape[main_axis]] + place[main_axis + 1:]
    return values.at[tuple(place)].set(smallest).at[tuple(next_to)].set(largest)


def strengthened(result, rng, source, target, blocks, factor):
    def block_of(axis_at):
        return (jnp.arange(result.shape[axis_at]) // (result.shape[axis_at] // blocks)).reshape((-1,) + (1,) * (result.ndim - 1 - axis_at))

    one_side = jax.random.permutation(rng, blocks)[block_of(target)]
    second = (block_of(target) + blocks // 2) % blocks
    return jnp.where((block_of(source) == one_side) | (block_of(source) == second), factor * result, result)


def block_levels(key, extent, cuts, smallest, high):
    loudness = 1.0
    for dim, parts in cuts:
        draws = jax.random.uniform(jax.random.fold_in(jax.random.fold_in(key, 6), dim), (parts,), jnp.float32, smallest / len(cuts), high / len(cuts))
        loudness = loudness * jnp.repeat(jnp.exp(draws), extent[dim] // parts).reshape((-1,) + (1,) * (len(extent) - 1 - dim))
    return loudness


def assign_block(own_key, own, number, rows, count, top, reach, skew):
    ranking = jax.random.permutation(own_key, count)
    crowded, ordinary = portions_of(count, rows * top, reach, skew, True), portions_of(count, rows * top, reach, skew, False)
    places = jnp.arange(count)

    def named(tallies, turn):
        used = int((tallies > 0).sum())
        fixed = max(1, used // 4)
        moved = fixed + (places - fixed + turn * (used - fixed)) % max(1, count - fixed)
        return jnp.zeros((count,), jnp.int32).at[ranking[jnp.where(places < fixed, places, moved)]].set(jnp.asarray(tallies, jnp.int32))

    tallies = jnp.where(number % 4 == 0, named(crowded, number // 4), named(ordinary, number - number // 4 - 1))
    mixed = jax.random.permutation(jax.random.fold_in(own, 3), count)
    donor, receiver = mixed[0:count // 2 * 2:2], mixed[1:count // 2 * 2:2]
    margin = jnp.minimum(tallies[donor] - 1, reach - tallies[receiver]) // 2
    margin = jnp.where((donor == ranking[0]) | (receiver == ranking[0]) | (tallies[receiver] == 0), 0, jnp.maximum(margin, 0))
    moved = jax.random.randint(jax.random.fold_in(own, 4), (count // 2,), 0, 1 << 20) % (margin + 1)
    tallies = tallies.at[donor].add(-moved).at[receiver].add(moved)
    members = jnp.searchsorted(jnp.cumsum(tallies), jnp.arange(rows * top), side="right").astype(jnp.int32)
    grid = members.reshape(top, rows).T
    grid = grid[jax.random.permutation(jax.random.fold_in(own, 1), rows)]
    turn = jax.random.randint(jax.random.fold_in(own, 2), (rows, 1), 0, top)
    return jnp.take_along_axis(grid, (jnp.arange(top)[None, :] + turn) % top, axis=1)


def portions_of(number_of, total, most, lean, full):
    weights = [(1 << 20) // math.isqrt(rank ** lean) + 1 for rank in range(1, number_of + 1)]
    largest = most if full else min(most, max(-(-total // number_of), total * weights[0] // sum(weights)))
    least = 1 if total - largest >= number_of - 1 else 0
    given, spare = [largest] + [least] * (number_of - 1), total - largest - least * (number_of - 1)
    while spare > 0:
        candidates = [i for i in range(1, number_of) if given[i] < largest] or [i for i in range(1, number_of) if given[i] < most]
        mass, left = sum([weights[i] for i in candidates]), spare
        for i in candidates:
            extra = min(most - given[i], max(1, left * weights[i] // mass), spare)
            given[i] = given[i] + extra
            spare = spare - extra
    return np.array(given)


def noise(key, extent, spread, bound, cuts=(), held_as=jnp.bfloat16):
    gain = block_levels(key, extent, cuts, -0.22, 0.18) if cuts else 1.0
    values = jax.random.normal(key, extent, jnp.float32) * spread * gain
    return jnp.minimum(jnp.maximum(values, -bound), bound).astype(held_as)


def bell_draw_with(stream_key, shape, scale, reach, cuts, heavy, kind=jnp.bfloat16):
    drawn = scale * jax.random.normal(stream_key, shape, jnp.float32)
    if cuts:
        drawn = drawn * block_levels(stream_key, shape, cuts, -0.22, 0.18)
    return jnp.clip(strengthened(drawn, jax.random.fold_in(stream_key, 3), *heavy), -reach, reach).astype(kind)


def setup_inputs(seed: int = 0) -> dict:
    key_list = jax.random.split(jax.random.key(seed), 13)
    queries = noise(key_list[0], (SEQ, D), 1.0, 6.0, ((0, 16), (1, 2)))
    keys_values = noise(key_list[1], (2, SEQ, D), 1.0, 6.0, ((1, 16), (2, 2)))
    attn_cot = noise(key_list[2], (SEQ, D), 128.0, 768.0, ((0, 16), (1, 2)))
    event_rows = bell_draw_with(key_list[3], (SEQ, D), 0.02, 0.15625, ((0, 16),), (0, 1, 16, 2.0))
    adapter = noise(key_list[4], (D, D), D ** -0.5, 0.1875, ((1, 2),))
    qkv_weight = noise(key_list[5], (3, D, D), D ** -0.5, 0.1875, ((2, 2),))
    starts = draw_starts(jax.random.fold_in(key_list[12], 71), 0)
    owners_keys = jax.random.split(jax.random.fold_in(key_list[7], 1), SEQ // TOK_DEV)
    owners_turns = jax.random.permutation(jax.random.fold_in(key_list[7], 3), SEQ // TOK_DEV)
    owners = jax.vmap(lambda own, number: assign_block(jax.random.fold_in(key_list[7], 2), own, number, TOK_DEV, N_CTX, 1, CAP, 2))(owners_keys, owners_turns).reshape((SEQ, 1))
    slots = place_ends(jax.random.randint(key_list[8], (SEQ,), 0, ROWS_DEV), jax.random.fold_in(key_list[8], 1), 0, ROWS_DEV - 1).astype(jnp.int32)
    table = noise(key_list[9], (ROWS, D), 0.1, 0.625, ((0, 16), (1, 2)), jnp.float32)
    moment_m = noise(key_list[10], (ROWS, D), 0.1, 0.625, ((0, 16), (1, 2)), jnp.float32)
    moment_v = jnp.clip(jnp.exp(math.log(1.0) - 4.6051702 * jax.random.uniform(key_list[11], (ROWS, D), jnp.float32) ** block_levels(key_list[11], (ROWS, D), ((0, 16), (1, 2)), -0.2, 0.2)), 0.01, 1.0)
    return dict(queries=queries, keys_values=keys_values, attn_cot=attn_cot, event_rows=event_rows, adapter=adapter, qkv_weight=qkv_weight, starts=starts, owners=owners, slots=slots, table=table, moment_m=moment_m, moment_v=moment_v)


beta_first = 0.9
beta_second = 0.999
learn_rate = 0.01
epsilon = 1e-08
first_fix = 1.0 - beta_first ** 10.0
second_fix = 1.0 - beta_second ** 10.0

def adam_rows(summed, touched, table, moment_m, moment_v):
    fresh_m = beta_first * moment_m + (1.0 - beta_first) * summed
    fresh_v = beta_second * moment_v + (1.0 - beta_second) * summed * summed
    update = learn_rate * (fresh_m / first_fix) / (jnp.sqrt(fresh_v / second_fix) + epsilon)
    keep = touched[:, None]
    return (jnp.where(keep, table - update, table), jnp.where(keep, fresh_m, moment_m), jnp.where(keep, fresh_v, moment_v))

def head_backward(operands, lower):
    query, key_rows, value_rows, cotangent = operands
    block_span = math.gcd(SEQ, 1024)
    count = SEQ // block_span
    scale = 1.0 / math.sqrt(HD)
    places = jnp.arange(SEQ, dtype=jnp.int32)
    zeros = jnp.zeros((SEQ, HD), jnp.float32)
    high = lax.Precision.HIGHEST

    def query_step(carry, index):
        first = index * block_span
        q_part = lax.dynamic_slice_in_dim(query, first, block_span, 0)
        c_part = lax.dynamic_slice_in_dim(cotangent, first, block_span, 0)
        q_place = lax.dynamic_slice_in_dim(places, first, block_span, 0)
        q_lower = lax.dynamic_slice_in_dim(lower, first, block_span, 0)
        least = jnp.min(q_lower)

        def key_block_step(inner_loop, key_block_index):
            key_start_row = key_block_index * block_span

            def active(values):
                query_grad, key_grad, value_grad = values
                k_part = lax.dynamic_slice_in_dim(key_rows, key_start_row, block_span, 0)
                v_part = lax.dynamic_slice_in_dim(value_rows, key_start_row, block_span, 0)
                k_place = lax.dynamic_slice_in_dim(places, key_start_row, block_span, 0)
                scores = jnp.dot(q_part, k_part.T, precision=high) * scale
                seen = (k_place[None, :] <= q_place[:, None]) & (k_place[None, :] >= q_lower[:, None])
                squash = jax.nn.sigmoid(scores)
                weights = jnp.where(seen, scores * squash / SEQ, 0.0).astype(jnp.bfloat16).astype(jnp.float32)
                dprod = jnp.dot(c_part, v_part.T, precision=high)
                dscore = jnp.where(seen, dprod * squash * (1.0 + scores * (1.0 - squash)) / SEQ, 0.0).astype(jnp.bfloat16).astype(jnp.float32)
                query_grad = query_grad + jnp.dot(dscore, k_part, precision=high)
                key_add = jnp.dot(dscore.T, q_part, precision=high)
                value_add = jnp.dot(weights.T, c_part, precision=high)
                key_grad = lax.dynamic_update_slice_in_dim(key_grad, lax.dynamic_slice_in_dim(key_grad, key_start_row, block_span, 0) + key_add, key_start_row, 0)
                value_grad = lax.dynamic_update_slice_in_dim(value_grad, lax.dynamic_slice_in_dim(value_grad, key_start_row, block_span, 0) + value_add, key_start_row, 0)
                return (query_grad, key_grad, value_grad)
            seen_any = (key_start_row <= first + block_span - 1) & (key_start_row + block_span - 1 >= least)
            return (lax.cond(seen_any, active, lambda values: values, inner_loop), None)
        start = (jnp.zeros((block_span, HD), jnp.float32), carry[0], carry[1])
        (query_grad, key_grad, value_grad), _ = lax.scan(key_block_step, start, jnp.arange(count, dtype=jnp.int32))
        return ((key_grad, value_grad), query_grad * scale)
    (key_grad, value_grad), query_grad = lax.scan(query_step, (zeros, zeros), jnp.arange(count, dtype=jnp.int32))
    return (query_grad.reshape(SEQ, HD), key_grad * scale, value_grad)

def reference(queries, keys_values, attn_cot, event_rows, adapter, qkv_weight, starts, owners, slots, table, moment_m, moment_v):
    lower = jnp.repeat(starts, QBLK, total_repeat_length=SEQ).astype(jnp.int32)

    def by_head(array):
        return array.astype(jnp.float32).reshape(SEQ, HEADS, HD).transpose(1, 0, 2)
    stacked = (by_head(queries), by_head(keys_values[0]), by_head(keys_values[1]), by_head(attn_cot))
    query_grad, key_grad, value_grad = lax.map(lambda operands: head_backward(operands, lower), stacked)

    def to_rows(array):
        return array.transpose(1, 0, 2).reshape(SEQ, D).astype(jnp.bfloat16)
    layer_grad = jnp.dot(to_rows(query_grad), qkv_weight[0].T, preferred_element_type=jnp.float32)
    layer_grad = layer_grad + jnp.dot(to_rows(key_grad), qkv_weight[1].T, preferred_element_type=jnp.float32)
    layer_grad = layer_grad + jnp.dot(to_rows(value_grad), qkv_weight[2].T, preferred_element_type=jnp.float32)
    layer_grad_b = layer_grad.astype(jnp.bfloat16)
    adapter_grad = jnp.dot(layer_grad_b.T, event_rows, preferred_element_type=jnp.float32)
    row_grads = layer_grad + jnp.dot(layer_grad_b, adapter, preferred_element_type=jnp.float32)
    row_index = (owners[:, 0] * ROWS_DEV + slots).astype(jnp.int32)
    summed = jax.ops.segment_sum(row_grads, row_index, num_segments=ROWS)
    hits = jax.ops.segment_sum(jnp.ones((SEQ,), jnp.int32), row_index, num_segments=ROWS)
    new_table, new_m, new_v = adam_rows(summed, hits > 0, table, moment_m, moment_v)
    return (adapter_grad, new_table, new_m, new_v)
```

```python
import functools
import math

import jax
import jax.numpy as jnp
from jax import lax
from jax.experimental import pallas as pl
from jax.experimental.pallas import tpu as pltpu
from jax.sharding import PartitionSpec as P

HD = 128
QBLK = 128


beta_first = 0.9
beta_second = 0.999
learn_rate = 0.01
epsilon = 1e-08
first_fix = 1.0 - beta_first**10.0
second_fix = 1.0 - beta_second**10.0


def adam_rows(summed, touched, table, moment_m, moment_v):
    fresh_m = beta_first * moment_m + (1.0 - beta_first) * summed
    fresh_v = beta_second * moment_v + (1.0 - beta_second) * summed * summed
    update = learn_rate * (fresh_m / first_fix) / (jnp.sqrt(fresh_v / second_fix) + epsilon)
    keep = touched[:, None]
    return (
        jnp.where(keep, table - update, table),
        jnp.where(keep, fresh_m, moment_m),
        jnp.where(keep, fresh_v, moment_v),
    )


def pair_scores(query_part, key_part, query_places, query_lower, key_places):
    scale = 1.0 / math.sqrt(HD)
    scores = (
        jnp.einsum("ihd,jhd->hij", query_part, key_part, preferred_element_type=jnp.float32) * scale
    )
    seen = (key_places[None, :] <= query_places[:, None]) & (
        key_places[None, :] >= query_lower[:, None]
    )
    squash = jax.nn.sigmoid(scores)
    return (scores, squash, seen[None])


def score_grads(scores, squash, seen, cotangent_piece, value_part, seq_len):
    dprod = jnp.einsum(
        "ihd,jhd->hij", cotangent_piece, value_part, preferred_element_type=jnp.float32
    )
    return jnp.where(seen, dprod * squash * (1.0 + scores * (1.0 - squash)) / seq_len, 0.0).astype(
        jnp.bfloat16
    )


def score_weights(scores, squash, seen, seq_len):
    return jnp.where(seen, scores * squash / seq_len, 0.0).astype(jnp.bfloat16)


def over_blocks(total, fn, carry):
    sub = math.gcd(total, 1024)
    return lax.fori_loop(
        0, total // sub, lambda index, inner_loop: fn(inner_loop, index * sub), carry
    )


def plain_device(
    queries,
    keys_values,
    attn_cot,
    event_rows,
    adapter,
    qkv_weight,
    starts,
    owners,
    slots,
    table,
    moment_m,
    moment_v,
):
    rows_here = queries.shape[0]
    feature_cols = queries.shape[1]
    heads_here = feature_cols // HD
    n_ctx = lax.axis_size("ctx")
    seq_len = rows_here * n_ctx
    scale = 1.0 / math.sqrt(HD)
    myself = lax.axis_index("ctx")
    local_first = myself * rows_here
    local_places = local_first + jnp.arange(rows_here, dtype=jnp.int32)
    lower = jnp.repeat(starts, QBLK, total_repeat_length=rows_here)
    least_lower = jnp.min(lower)
    query_heads = queries.reshape(rows_here, heads_here, HD)
    cot_heads = attn_cot.reshape(rows_here, heads_here, HD)
    key_heads = keys_values[0].reshape(rows_here, heads_here, HD)
    value_heads = keys_values[1].reshape(rows_here, heads_here, HD)
    zeros = jnp.zeros((rows_here, heads_here, HD), jnp.float32)
    piece = lax.all_gather(keys_values, "ctx", axis=1, tiled=True)

    def key_one_block(inner_loop, offset):
        sub = math.gcd(piece.shape[1], 1024)
        key_first = offset
        live = (key_first <= local_first + rows_here - 1) & (key_first + sub - 1 >= least_lower)

        def key_working(values):
            part = lax.dynamic_slice_in_dim(piece, offset, sub, 1)
            key_part = part[0].reshape(sub, heads_here, HD)
            value_part = part[1].reshape(sub, heads_here, HD)
            key_places = key_first + jnp.arange(sub, dtype=jnp.int32)
            scores, squash, seen = pair_scores(
                query_heads, key_part, local_places, lower, key_places
            )
            dscore = score_grads(scores, squash, seen, cot_heads, value_part, seq_len)
            return values + jnp.einsum(
                "hij,jhd->ihd", dscore, key_part, preferred_element_type=jnp.float32
            )

        return lax.cond(live, key_working, lambda values: values, inner_loop)

    query_grad = over_blocks(piece.shape[1], key_one_block, zeros)
    query_piece = (
        lax.all_gather(queries, "ctx", axis=0, tiled=True),
        lax.all_gather(attn_cot, "ctx", axis=0, tiled=True),
        lax.all_gather(lower, "ctx", axis=0, tiled=True),
    )

    def query_one_block(inner_loop, offset):
        sub = math.gcd(query_piece[0].shape[0], 1024)
        query_first = offset
        query_lower = lax.dynamic_slice_in_dim(query_piece[2], offset, sub, 0)
        live = (local_first <= query_first + sub - 1) & (
            local_first + rows_here - 1 >= jnp.min(query_lower)
        )

        def query_working(values):
            query_part = lax.dynamic_slice_in_dim(query_piece[0], offset, sub, 0).reshape(
                sub, heads_here, HD
            )
            cotangent_piece = lax.dynamic_slice_in_dim(query_piece[1], offset, sub, 0).reshape(
                sub, heads_here, HD
            )
            query_places = query_first + jnp.arange(sub, dtype=jnp.int32)
            scores, squash, seen = pair_scores(
                query_part, key_heads, query_places, query_lower, local_places
            )
            weights = score_weights(scores, squash, seen, seq_len)
            dscore = score_grads(scores, squash, seen, cotangent_piece, value_heads, seq_len)
            key_add = jnp.einsum(
                "hij,ihd->jhd", dscore, query_part, preferred_element_type=jnp.float32
            )
            value_add = jnp.einsum(
                "hij,ihd->jhd", weights, cotangent_piece, preferred_element_type=jnp.float32
            )
            return (values[0] + key_add, values[1] + value_add)

        return lax.cond(live, query_working, lambda values: values, inner_loop)

    key_grad, value_grad = over_blocks(query_piece[0].shape[0], query_one_block, (zeros, zeros))
    head_grads = (
        jnp.stack([query_grad * scale, key_grad * scale, value_grad])
        .astype(jnp.bfloat16)
        .reshape(3, rows_here, feature_cols)
    )
    partial_grad = jnp.einsum(
        "mtc,mdc->td", head_grads, qkv_weight, preferred_element_type=jnp.float32
    )
    head_cols = adapter.shape[1]
    first_col = lax.axis_index("head") * head_cols
    layer_grad = lax.psum(partial_grad.astype(jnp.bfloat16), "head").astype(jnp.float32)
    layer_grad_b = layer_grad.astype(jnp.bfloat16)
    own_grad = lax.dynamic_slice_in_dim(layer_grad, first_col, head_cols, 1)
    row_grads = own_grad + jnp.dot(layer_grad_b, adapter, preferred_element_type=jnp.float32)
    own_rows = lax.dynamic_slice_in_dim(event_rows, first_col, head_cols, 1)
    adapter_grad = lax.psum_scatter(
        lax.dot_general(
            layer_grad_b, own_rows, (((0,), (0,)), ((), ())), preferred_element_type=jnp.float32
        ),
        "ctx",
        scatter_dimension=0,
        tiled=True,
    )
    capacity = max(2, 2 * rows_here // n_ctx)
    target = owners[:, 0]
    onehot = (target[:, None] == jnp.arange(n_ctx, dtype=jnp.int32)[None, :]).astype(jnp.int32)
    prior_blocks = jnp.cumsum(onehot, axis=0) - onehot
    ranking = jnp.sum(prior_blocks * onehot, axis=1)
    cell_index = target * capacity + ranking
    placing = cell_index[:, None] == jnp.arange(n_ctx * capacity, dtype=jnp.int32)[None, :]
    send_rows = lax.dot_general(
        placing.astype(jnp.float32),
        row_grads,
        (((0,), (0,)), ((), ())),
        precision=lax.Precision.HIGHEST,
    ).reshape(n_ctx, capacity, head_cols)
    send_slots = (jnp.sum(jnp.where(placing, slots[:, None] + 1, 0), axis=0) - 1).reshape(
        n_ctx, capacity
    )
    got_rows, got_slots = (
        lax.all_to_all(
            send_rows.astype(jnp.bfloat16), "ctx", split_axis=0, concat_axis=0, tiled=True
        ).astype(send_rows.dtype),
        lax.all_to_all(send_slots, "ctx", split_axis=0, concat_axis=0, tiled=True),
    )
    table_rows = table.shape[0]
    landing = got_slots.reshape(-1)[None, :] == jnp.arange(table_rows, dtype=jnp.int32)[:, None]
    summed = jnp.dot(
        landing.astype(jnp.float32),
        got_rows.reshape(n_ctx * capacity, head_cols),
        precision=lax.Precision.HIGHEST,
    )
    touched = jnp.sum(landing.astype(jnp.int32), axis=1) > 0
    new_table, new_m, new_v = adam_rows(summed, touched, table, moment_m, moment_v)
    return (adapter_grad, new_table, new_m, new_v)


BLOCK = 128
PAIR = 2 * BLOCK
META = 16
PART = PAIR + META
SPOTS = (0, 1, 4, 5)
GROUPS = [[zh * 8 + y * 2 + s for s in SPOTS] for zh in range(2) for y in range(2)]
ACROSS_Y = [(i, i ^ 2) for i in range(16)]
FAR_OUT = [(i * 2, (i + 8) * 2) for i in range(8)] + [((i + 8) * 2 + 1, i * 2 + 1) for i in range(8)]
FAR_BACK = [(b, a) for a, b in FAR_OUT]
SWAP = [(0, 1), (1, 0)]
F32 = jnp.float32
BF16 = jnp.bfloat16
VMEM = pl.BlockSpec(memory_space=pltpu.VMEM)
SMEM = pl.BlockSpec(memory_space=pltpu.SMEM)


def dot(a, b, axis_a, axis_b):
    return lax.dot_general(a, b, (((axis_a,), (axis_b,)), ((), ())), preferred_element_type=F32)


def kernel_call(body, out_shape, operands, name, flops=0, in_bytes=0):
    specs = [SMEM if o.dtype == jnp.int32 and o.ndim == 1 else VMEM for o in operands]
    return pl.pallas_call(
        body,
        out_shape=out_shape,
        in_specs=specs,
        out_specs=jax.tree.map(lambda _: VMEM, out_shape),
        compiler_params=pltpu.CompilerParams(vmem_limit_bytes=24 * 1024 * 1024),
        cost_estimate=pl.CostEstimate(flops=flops, bytes_accessed=in_bytes, transcendentals=0),
        name=name,
    )(*operands)


def deal_body(info, starts, queries, keys_values, cot, out):
    core = info[0]
    start = starts[0]
    row = lax.broadcasted_iota(jnp.int32, (META, BLOCK), 0)
    meta = jnp.where(row == 0, start // BLOCK, jnp.where(row == 1, start % BLOCK, 0)).astype(F32).astype(BF16)

    def fill(first, second):
        for head in range(4):
            cols = slice(head * BLOCK, (head + 1) * BLOCK)
            for place, (one, two) in enumerate((first, second)):
                base = place * PART
                out[head, base : base + BLOCK, :] = one(cols)
                out[head, base + BLOCK : base + PAIR, :] = two(cols)
                out[head, base + PAIR : base + PART, :] = meta

    asks = (lambda c: queries[:, c], lambda c: cot[:, c])
    gives = (lambda c: keys_values[0, :, c], lambda c: keys_values[1, :, c])

    @pl.when(core == 0)
    def _():
        fill(asks, gives)

    @pl.when(core == 1)
    def _():
        fill(gives, asks)


def attend_body(scale, seq_len, info, mine, near_in, far_in, keep, near_out, far_out, far_1, far_2, sum_1, sum_2):
    core, zh, y = info[0], info[1], info[2]
    role_q = core == 0
    wide = 4 * BLOCK
    sign = jnp.where(role_q, 1, -1)

    def lower_of(ref, spot, base):
        meta = ref[spot, base + PAIR : base + PART, :].astype(F32)
        return (meta[0:1] * BLOCK + meta[1:2]).astype(jnp.int32)

    def lanes_of(group_zh):
        lane = lax.broadcasted_iota(jnp.int32, (1, BLOCK), 1)
        return jnp.concatenate([lane + (group_zh * 8 + y * 2 + s) * BLOCK for s in SPOTS], axis=1)

    for spot in range(4):
        rows = slice(spot * BLOCK, (spot + 1) * BLOCK)
        far_1[0, rows, :] = mine[spot, PART : PART + BLOCK, :]
        far_2[0, rows, :] = mine[spot, PART + BLOCK : PART + PAIR, :]
        far_1[1, rows, :] = far_in[spot, :BLOCK, :]
        far_2[1, rows, :] = far_in[spot, BLOCK:PAIR, :]
    sum_1[...] = jnp.zeros_like(sum_1)
    sum_2[...] = jnp.zeros_like(sum_2)
    places = (lanes_of(zh), lanes_of(1 - zh))
    lowers = (
        jnp.concatenate([lower_of(mine, s, PART) for s in range(4)], axis=1),
        jnp.concatenate([lower_of(far_in, s, 0) for s in range(4)], axis=1),
    )
    row_in = lax.broadcasted_iota(jnp.int32, (BLOCK, wide), 0)
    grad_scale = scale * 0.5 / seq_len

    def piece(near_1, near_2, near_place, near_lower, side):
        base_1, base_2 = far_1[side], far_2[side]
        half = dot(near_1, base_1, 1, 1) * (0.5 * scale)
        dprod = dot(near_2, base_2, 1, 1)
        seen = []
        for at in range(2):
            low = jnp.where(role_q, jnp.concatenate([near_lower[at]] * 4, axis=1), lowers[side])
            row = row_in + near_place[at]
            causal = sign * row - sign * places[side]
            after = jnp.where(role_q, 0, 1) * row + (jnp.where(role_q, 1, 0) * places[side] - low)
            seen.append(jnp.minimum(causal, after) >= 0)
        seen = jnp.concatenate(seen, axis=0)
        twice = 1.0 + jnp.tanh(half)
        weight = half * twice
        dscore = dprod * (twice * (1.0 + (half + half - weight)))
        weight = jnp.where(seen, weight, 0.0).astype(BF16)
        dscore = jnp.where(seen, dscore, 0.0).astype(BF16)
        sum_1[side] = sum_1[side] + dot(dscore, near_1, 0, 0)
        return dot(dscore, base_1, 1, 0), weight

    def work(near_ref, neighbour, half_at):
        spots = (2 * half_at, 2 * half_at + 1)
        near_1 = jnp.concatenate([near_ref[s, :BLOCK, :] for s in spots], axis=0)
        near_2 = jnp.concatenate([near_ref[s, BLOCK:PAIR, :] for s in spots], axis=0)
        near_y = 1 - y if neighbour else y
        near_place = [(zh * 8 + near_y * 2 + SPOTS[s]) * BLOCK for s in spots]
        near_lower = [lower_of(near_ref, s, 0) for s in spots]

        def put(out, slot, value, start=False):
            for at, s in enumerate(spots):
                part = value[at * BLOCK : (at + 1) * BLOCK]
                if start:
                    out[s, slot] = part.astype(out.dtype)
                else:
                    out[s, slot] = (out[s, slot].astype(F32) + part).astype(out.dtype)

        def side_work(side):
            first, weight = piece(near_1, near_2, near_place, near_lower, side)
            return first * grad_scale, weight

        def second(weight, side):
            return dot(weight, far_2[side], 1, 0) * (1.0 / seq_len)

        def store(first, others):
            if neighbour:
                put(near_out, 0, first, True)
            else:
                put(keep, 0, first, True)

            @pl.when(role_q)
            def _():
                for side, weight in others:
                    sum_2[side] = sum_2[side] + dot(weight, near_2, 0, 0)
                if neighbour:
                    put(near_out, 1, jnp.zeros((PAIR, BLOCK), F32), True)

            @pl.when(jnp.logical_not(role_q))
            def _():
                total = sum([second(weight, side) for side, weight in others])
                put(near_out if neighbour else keep, 1, total, True)

        crosses = jnp.where(role_q, zh, 1 - zh) == 1

        @pl.when(crosses)
        def _():
            here, weight_here = side_work(0)
            there, weight_there = side_work(1)
            store(here + there, ((0, weight_here), (1, weight_there)))

        @pl.when(jnp.logical_not(crosses))
        def _():
            here, weight_here = side_work(0)
            store(here, ((0, weight_here),))

    for half_at in range(2):
        work(mine, False, half_at)
        work(near_in, True, half_at)

    for spot in range(4):
        rows = slice(spot * BLOCK, (spot + 1) * BLOCK)
        keep[spot, 2] = sum_1[0, rows] * grad_scale
        far_out[spot, 0] = (sum_1[1, rows] * grad_scale).astype(BF16)
        far_out[spot, 1] = (sum_2[1, rows] * (1.0 / seq_len)).astype(BF16)

        @pl.when(role_q)
        def _():
            keep[spot, 1] = sum_2[0, rows] * (1.0 / seq_len)


def project_body(info, dealt, weight, partial, sent):
    core = info[0]

    def rows(slot):
        return jnp.concatenate([dealt[h, slot] for h in range(4)], axis=1)

    total = dot(rows(1), weight[2], 1, 1)
    total = total + dot(rows(0), weight[core], 1, 1)
    total = total + dot(rows(2), weight[1 - core], 1, 1)
    partial[...] = total
    sent[...] = total.astype(BF16)


def pack_body(info, own, other, adapter, placing, out, grad, turned):
    core = info[0]
    n_ctx = out.shape[0]
    head_cols = adapter.shape[1]
    capacity = placing.shape[1] // n_ctx
    tiles = head_cols // BLOCK
    share = own.shape[1] // n_ctx // 2
    total = own[...] + other[...].astype(F32)
    grad[...] = total
    rounded = total.astype(BF16)
    turned[...] = jnp.transpose(rounded)
    rows = grad[:, pl.ds(pl.multiple_of(core * head_cols, head_cols), head_cols)]
    rows = rows + dot(rounded, adapter[...], 1, 0)
    cells = dot(placing[...], rows.astype(BF16), 0, 0).astype(BF16)
    for p in range(n_ctx):
        for tile in range(tiles):
            out[p, tile * capacity : (tile + 1) * capacity, :] = cells[
                p * capacity : (p + 1) * capacity, tile * BLOCK : (tile + 1) * BLOCK
            ]
        first = pl.multiple_of(p * 2 * share + core * share, share)
        out[p, tiles * capacity : tiles * capacity + share, :] = turned[pl.ds(first, share), :]


def place_body(info, owners, slots, rows, placing, sent):
    core = info[0]
    count = owners.shape[0]
    head_cols = sent.shape[1]
    capacity = placing.shape[1] // 16
    owner = jnp.broadcast_to(owners[...], (count, BLOCK))
    lane = lax.broadcasted_iota(jnp.int32, (count, BLOCK), 1)
    row = lax.broadcasted_iota(jnp.int32, (count, BLOCK), 0)
    named = owner == lane
    earlier = (lane < row).astype(F32).astype(BF16)
    prior = dot(earlier, named.astype(F32).astype(BF16), 1, 0)
    ranking = jnp.sum(jnp.where(named, prior, 0.0), axis=1, keepdims=True)
    cell = jnp.broadcast_to(owners[...].astype(F32) * capacity + ranking, (count, BLOCK))
    for tile in range(placing.shape[1] // BLOCK):
        hit = cell == (lane + tile * BLOCK).astype(F32)
        placing[:, tile * BLOCK : (tile + 1) * BLOCK] = hit.astype(F32).astype(BF16)
    sent[0:count, :] = rows[:, pl.ds(pl.multiple_of(core * head_cols, head_cols), head_cols)]
    cell_row = jnp.transpose(cell)[0:META]
    at = lax.broadcasted_iota(jnp.int32, (META, BLOCK), 0)
    slot_row = jnp.broadcast_to(slots[...], (META, BLOCK)).astype(F32)
    meta = jnp.where(at == 0, cell_row, jnp.where(at == 1, slot_row, 0.0))
    sent[count : count + META, 0:BLOCK] = meta.astype(BF16)
    sent[count : count + META, BLOCK:] = jnp.zeros((META, head_cols - BLOCK), BF16)


def land_body(info, gathered, landing, touched):
    me = info[3]
    table_rows, cells = landing.shape
    block = BLOCK + META
    n_ctx = gathered.shape[0] // block
    capacity = cells // n_ctx
    total = jnp.zeros((table_rows, cells), F32)
    row = lax.broadcasted_iota(jnp.int32, (table_rows, BLOCK), 0).astype(F32)
    cell_at = lax.broadcasted_iota(jnp.int32, (cells, BLOCK), 0).astype(F32)
    for s in range(n_ctx):
        meta = gathered[s * block + BLOCK : (s + 1) * block, 0:BLOCK].astype(F32)
        local = meta[0:1] - (me * capacity).astype(F32)
        inside = (local >= 0) & (local < capacity)
        local = jnp.where(inside, local + s * capacity, -1.0)
        slot = (row == meta[1:2]).astype(F32).astype(BF16)
        cell = (cell_at == local).astype(F32).astype(BF16)
        total = total + dot(slot, cell, 1, 1)
    landing[...] = total.astype(BF16)
    hits = jnp.sum(total, axis=1, keepdims=True)
    touched[...] = jnp.broadcast_to(hits, touched.shape)


def finish_body(info, got, other, gathered, landing, touched, table, moment_m, moment_v, grad, new_table, new_m, new_v):
    core = info[0]
    n_ctx, capacity = got.shape[0], landing.shape[1] // got.shape[0]
    share = other.shape[1]
    block = BLOCK + META
    tiles = table.shape[1] // BLOCK
    width = tiles * capacity
    for tile in range(tiles):
        cols = slice(tile * BLOCK, (tile + 1) * BLOCK)
        cells = got[:, tile * capacity : (tile + 1) * capacity, :].reshape(n_ctx * capacity, BLOCK)
        summed = dot(landing[...], cells, 1, 0)
        keep = touched[...] > 0.0
        m, v, old = moment_m[:, cols], moment_v[:, cols], table[:, cols]
        fresh_m = beta_first * m + (1.0 - beta_first) * summed
        fresh_v = beta_second * v + (1.0 - beta_second) * summed * summed
        update = learn_rate * (fresh_m / first_fix) / (jnp.sqrt(fresh_v / second_fix) + epsilon)
        new_table[:, cols] = jnp.where(keep, old - update, old)
        new_m[:, cols] = jnp.where(keep, fresh_m, m)
        new_v[:, cols] = jnp.where(keep, fresh_v, v)
    mine_t = jnp.concatenate([got[s, width : width + share, :] for s in range(n_ctx)], axis=1)
    other_t = jnp.concatenate([other[s] for s in range(n_ctx)], axis=1)
    rows = jnp.concatenate([gathered[s * block : s * block + BLOCK, :] for s in range(n_ctx)], axis=0)
    both = dot(jnp.concatenate([mine_t, other_t], axis=0), rows, 1, 0)
    grad[pl.ds(pl.multiple_of(core * share, share), share), :] = both[:share]
    grad[pl.ds(pl.multiple_of((1 - core) * share, share), share), :] = both[share:]


def dealt_device(
    queries,
    keys_values,
    attn_cot,
    event_rows,
    adapter,
    qkv_weight,
    starts,
    owners,
    slots,
    table,
    moment_m,
    moment_v,
):
    shape = jax.ShapeDtypeStruct
    n_ctx = lax.axis_size("ctx")
    rows_here = queries.shape[0]
    seq_len = rows_here * n_ctx
    head_cols = adapter.shape[1]
    width = event_rows.shape[1]
    capacity = max(2, 2 * rows_here // n_ctx)
    me = lax.axis_index("ctx")
    info = jnp.stack([lax.axis_index("head"), me // 8, me // 2 % 2, me]).astype(jnp.int32)
    placing, sent_rows = kernel_call(
        place_body,
        (shape((rows_here, n_ctx * capacity), BF16), shape((rows_here + META, head_cols), BF16)),
        (info, owners, slots.reshape(1, rows_here), event_rows),
        "place",
    )
    dealt = kernel_call(
        deal_body, shape((4, 2 * PART, BLOCK), BF16), (info, starts, queries, keys_values, attn_cot), "deal"
    )
    mine = lax.all_to_all(dealt, "ctx", 0, 0, tiled=True, axis_index_groups=GROUPS)
    gathered = lax.all_gather(sent_rows, "ctx", axis=0, tiled=True)
    far_in = lax.ppermute(mine[:, PART:], ("ctx", "head"), FAR_OUT)
    near_in = lax.ppermute(mine[:, :PART], "ctx", ACROSS_Y)
    keep, near_out, far_out = pl.pallas_call(
        functools.partial(attend_body, 1.0 / math.sqrt(HD), float(seq_len)),
        out_shape=(
            shape((4, 3, BLOCK, BLOCK), F32),
            shape((4, 2, BLOCK, BLOCK), BF16),
            shape((4, 2, BLOCK, BLOCK), BF16),
        ),
        in_specs=[SMEM, VMEM, VMEM, VMEM],
        out_specs=(VMEM, VMEM, VMEM),
        scratch_shapes=[
            pltpu.VMEM((2, 4 * BLOCK, BLOCK), BF16),
            pltpu.VMEM((2, 4 * BLOCK, BLOCK), BF16),
            pltpu.VMEM((2, 4 * BLOCK, BLOCK), F32),
            pltpu.VMEM((2, 4 * BLOCK, BLOCK), F32),
        ],
        compiler_params=pltpu.CompilerParams(vmem_limit_bytes=24 * 1024 * 1024),
        cost_estimate=pl.CostEstimate(flops=2 * 10**9, bytes_accessed=2**21, transcendentals=0),
        name="attend",
    )(info, mine, near_in, far_in)
    far_back = lax.ppermute(far_out, ("ctx", "head"), FAR_BACK).astype(F32)
    near_back = lax.ppermute(near_out, "ctx", ACROSS_Y).astype(F32)
    head_grads = jnp.stack(
        [
            keep[:, 0] + near_back[:, 0],
            keep[:, 1] + near_back[:, 1] + far_back[:, 1],
            keep[:, 2] + far_back[:, 0],
        ],
        axis=1,
    ).astype(BF16)
    head_grads = lax.all_to_all(head_grads, "ctx", 0, 0, tiled=True, axis_index_groups=GROUPS)
    partial, sent = kernel_call(
        project_body,
        (shape((rows_here, width), F32), shape((rows_here, width), BF16)),
        (info, head_grads, qkv_weight),
        "project",
    )
    other = lax.ppermute(sent, "head", SWAP)
    share = width // n_ctx // 2
    packed_rows = capacity * head_cols // BLOCK
    packed = pl.pallas_call(
        pack_body,
        out_shape=shape((n_ctx, packed_rows + share, BLOCK), BF16),
        in_specs=[SMEM] + [VMEM] * 4,
        out_specs=VMEM,
        scratch_shapes=[pltpu.VMEM((rows_here, width), F32), pltpu.VMEM((width, rows_here), BF16)],
        compiler_params=pltpu.CompilerParams(vmem_limit_bytes=24 * 1024 * 1024),
        name="pack",
    )(info, partial, other, adapter, placing)
    got = lax.all_to_all(packed, "ctx", 0, 0, tiled=True)
    other_share = lax.ppermute(got[:, packed_rows:], "head", SWAP)
    landing, touched = kernel_call(
        land_body,
        (shape((table.shape[0], n_ctx * capacity), BF16), shape((table.shape[0], BLOCK), F32)),
        (info, gathered),
        "land",
    )
    held = shape(table.shape, F32)
    return kernel_call(
        finish_body,
        (shape((width // n_ctx, head_cols), F32), held, held, held),
        (info, got, other_share, gathered, landing, touched, table, moment_m, moment_v),
        "finish",
    )


def per_device(*arrays):
    rows_here, cols_here = arrays[0].shape
    fits = lax.axis_size("ctx") == 16 and lax.axis_size("head") == 2
    if fits and rows_here == BLOCK and cols_here == 4 * HD and arrays[9].shape[0] == 2 * BLOCK:
        return dealt_device(*arrays)
    return plain_device(*arrays)


def solution(mesh):
    placed = (
        P("ctx", "head"),
        P(None, "ctx", "head"),
        P("ctx", "head"),
        P("ctx", None),
        P(None, "head"),
        P(None, None, "head"),
        P("ctx"),
        P("ctx", None),
        P("ctx"),
        P("ctx", "head"),
        P("ctx", "head"),
        P("ctx", "head"),
    )
    return jax.shard_map(
        per_device,
        mesh=mesh,
        in_specs=placed,
        out_specs=(P("ctx", "head"), P("ctx", "head"), P("ctx", "head"), P("ctx", "head")),
        check_vma=False,
    )
```

```python
import functools
import math

import jax
import jax.numpy as jnp
from jax import lax
from jax.experimental import pallas as pl
from jax.experimental.pallas import tpu as pltpu
from jax.sharding import PartitionSpec as P

HD = 128
QBLK = 128


beta_first = 0.9
beta_second = 0.999
learn_rate = 0.01
epsilon = 1e-08
first_fix = 1.0 - beta_first**10.0
second_fix = 1.0 - beta_second**10.0


def adam_rows(summed, touched, table, moment_m, moment_v):
    fresh_m = beta_first * moment_m + (1.0 - beta_first) * summed
    fresh_v = beta_second * moment_v + (1.0 - beta_second) * summed * summed
    update = learn_rate * (fresh_m / first_fix) / (jnp.sqrt(fresh_v / second_fix) + epsilon)
    keep = touched[:, None]
    return (
        jnp.where(keep, table - update, table),
        jnp.where(keep, fresh_m, moment_m),
        jnp.where(keep, fresh_v, moment_v),
    )


def pair_scores(query_part, key_part, query_places, query_lower, key_places):
    scale = 1.0 / math.sqrt(HD)
    scores = (
        jnp.einsum("ihd,jhd->hij", query_part, key_part, preferred_element_type=jnp.float32) * scale
    )
    seen = (key_places[None, :] <= query_places[:, None]) & (
        key_places[None, :] >= query_lower[:, None]
    )
    squash = jax.nn.sigmoid(scores)
    return (scores, squash, seen[None])


def score_grads(scores, squash, seen, cotangent_piece, value_part, seq_len):
    dprod = jnp.einsum(
        "ihd,jhd->hij", cotangent_piece, value_part, preferred_element_type=jnp.float32
    )
    return jnp.where(seen, dprod * squash * (1.0 + scores * (1.0 - squash)) / seq_len, 0.0).astype(
        jnp.bfloat16
    )


def score_weights(scores, squash, seen, seq_len):
    return jnp.where(seen, scores * squash / seq_len, 0.0).astype(jnp.bfloat16)


def over_blocks(total, fn, carry):
    sub = math.gcd(total, 1024)
    return lax.fori_loop(
        0, total // sub, lambda index, inner_loop: fn(inner_loop, index * sub), carry
    )


def plain_device(
    queries,
    keys_values,
    attn_cot,
    event_rows,
    adapter,
    qkv_weight,
    starts,
    owners,
    slots,
    table,
    moment_m,
    moment_v,
):
    rows_here = queries.shape[0]
    feature_cols = queries.shape[1]
    heads_here = feature_cols // HD
    n_ctx = lax.axis_size("ctx")
    seq_len = rows_here * n_ctx
    scale = 1.0 / math.sqrt(HD)
    myself = lax.axis_index("ctx")
    local_first = myself * rows_here
    local_places = local_first + jnp.arange(rows_here, dtype=jnp.int32)
    lower = jnp.repeat(starts, QBLK, total_repeat_length=rows_here)
    least_lower = jnp.min(lower)
    query_heads = queries.reshape(rows_here, heads_here, HD)
    cot_heads = attn_cot.reshape(rows_here, heads_here, HD)
    key_heads = keys_values[0].reshape(rows_here, heads_here, HD)
    value_heads = keys_values[1].reshape(rows_here, heads_here, HD)
    zeros = jnp.zeros((rows_here, heads_here, HD), jnp.float32)
    piece = lax.all_gather(keys_values, "ctx", axis=1, tiled=True)

    def key_one_block(inner_loop, offset):
        sub = math.gcd(piece.shape[1], 1024)
        key_first = offset
        live = (key_first <= local_first + rows_here - 1) & (key_first + sub - 1 >= least_lower)

        def key_working(values):
            part = lax.dynamic_slice_in_dim(piece, offset, sub, 1)
            key_part = part[0].reshape(sub, heads_here, HD)
            value_part = part[1].reshape(sub, heads_here, HD)
            key_places = key_first + jnp.arange(sub, dtype=jnp.int32)
            scores, squash, seen = pair_scores(
                query_heads, key_part, local_places, lower, key_places
            )
            dscore = score_grads(scores, squash, seen, cot_heads, value_part, seq_len)
            return values + jnp.einsum(
                "hij,jhd->ihd", dscore, key_part, preferred_element_type=jnp.float32
            )

        return lax.cond(live, key_working, lambda values: values, inner_loop)

    query_grad = over_blocks(piece.shape[1], key_one_block, zeros)
    query_piece = (
        lax.all_gather(queries, "ctx", axis=0, tiled=True),
        lax.all_gather(attn_cot, "ctx", axis=0, tiled=True),
        lax.all_gather(lower, "ctx", axis=0, tiled=True),
    )

    def query_one_block(inner_loop, offset):
        sub = math.gcd(query_piece[0].shape[0], 1024)
        query_first = offset
        query_lower = lax.dynamic_slice_in_dim(query_piece[2], offset, sub, 0)
        live = (local_first <= query_first + sub - 1) & (
            local_first + rows_here - 1 >= jnp.min(query_lower)
        )

        def query_working(values):
            query_part = lax.dynamic_slice_in_dim(query_piece[0], offset, sub, 0).reshape(
                sub, heads_here, HD
            )
            cotangent_piece = lax.dynamic_slice_in_dim(query_piece[1], offset, sub, 0).reshape(
                sub, heads_here, HD
            )
            query_places = query_first + jnp.arange(sub, dtype=jnp.int32)
            scores, squash, seen = pair_scores(
                query_part, key_heads, query_places, query_lower, local_places
            )
            weights = score_weights(scores, squash, seen, seq_len)
            dscore = score_grads(scores, squash, seen, cotangent_piece, value_heads, seq_len)
            key_add = jnp.einsum(
                "hij,ihd->jhd", dscore, query_part, preferred_element_type=jnp.float32
            )
            value_add = jnp.einsum(
                "hij,ihd->jhd", weights, cotangent_piece, preferred_element_type=jnp.float32
            )
            return (values[0] + key_add, values[1] + value_add)

        return lax.cond(live, query_working, lambda values: values, inner_loop)

    key_grad, value_grad = over_blocks(query_piece[0].shape[0], query_one_block, (zeros, zeros))
    head_grads = (
        jnp.stack([query_grad * scale, key_grad * scale, value_grad])
        .astype(jnp.bfloat16)
        .reshape(3, rows_here, feature_cols)
    )
    partial_grad = jnp.einsum(
        "mtc,mdc->td", head_grads, qkv_weight, preferred_element_type=jnp.float32
    )
    head_cols = adapter.shape[1]
    first_col = lax.axis_index("head") * head_cols
    layer_grad = lax.psum(partial_grad.astype(jnp.bfloat16), "head").astype(jnp.float32)
    layer_grad_b = layer_grad.astype(jnp.bfloat16)
    own_grad = lax.dynamic_slice_in_dim(layer_grad, first_col, head_cols, 1)
    row_grads = own_grad + jnp.dot(layer_grad_b, adapter, preferred_element_type=jnp.float32)
    own_rows = lax.dynamic_slice_in_dim(event_rows, first_col, head_cols, 1)
    adapter_grad = lax.psum_scatter(
        lax.dot_general(
            layer_grad_b, own_rows, (((0,), (0,)), ((), ())), preferred_element_type=jnp.float32
        ),
        "ctx",
        scatter_dimension=0,
        tiled=True,
    )
    capacity = max(2, 2 * rows_here // n_ctx)
    target = owners[:, 0]
    onehot = (target[:, None] == jnp.arange(n_ctx, dtype=jnp.int32)[None, :]).astype(jnp.int32)
    prior_blocks = jnp.cumsum(onehot, axis=0) - onehot
    ranking = jnp.sum(prior_blocks * onehot, axis=1)
    cell_index = target * capacity + ranking
    placing = cell_index[:, None] == jnp.arange(n_ctx * capacity, dtype=jnp.int32)[None, :]
    send_rows = lax.dot_general(
        placing.astype(jnp.float32),
        row_grads,
        (((0,), (0,)), ((), ())),
        precision=lax.Precision.HIGHEST,
    ).reshape(n_ctx, capacity, head_cols)
    send_slots = (jnp.sum(jnp.where(placing, slots[:, None] + 1, 0), axis=0) - 1).reshape(
        n_ctx, capacity
    )
    got_rows, got_slots = (
        lax.all_to_all(
            send_rows.astype(jnp.bfloat16), "ctx", split_axis=0, concat_axis=0, tiled=True
        ).astype(send_rows.dtype),
        lax.all_to_all(send_slots, "ctx", split_axis=0, concat_axis=0, tiled=True),
    )
    table_rows = table.shape[0]
    landing = got_slots.reshape(-1)[None, :] == jnp.arange(table_rows, dtype=jnp.int32)[:, None]
    summed = jnp.dot(
        landing.astype(jnp.float32),
        got_rows.reshape(n_ctx * capacity, head_cols),
        precision=lax.Precision.HIGHEST,
    )
    touched = jnp.sum(landing.astype(jnp.int32), axis=1) > 0
    new_table, new_m, new_v = adam_rows(summed, touched, table, moment_m, moment_v)
    return (adapter_grad, new_table, new_m, new_v)


BLOCK = 128
PAIR = 2 * BLOCK
META = 16
PART = PAIR + META
ACROSS_Y = [(i, i ^ 2) for i in range(16)]
FAR_OUT = [(i * 2, (i + 8) * 2) for i in range(8)] + [((i + 8) * 2 + 1, i * 2 + 1) for i in range(8)]
FAR_BACK = [(b, a) for a, b in FAR_OUT]
SWAP = [(0, 1), (1, 0)]
ROUNDS = (8, 4, 1, 2)
F32 = jnp.float32
BF16 = jnp.bfloat16
VMEM = pl.BlockSpec(memory_space=pltpu.VMEM)
SMEM = pl.BlockSpec(memory_space=pltpu.SMEM)


def dot(a, b, axis_a, axis_b):
    return lax.dot_general(a, b, (((axis_a,), (axis_b,)), ((), ())), preferred_element_type=F32)


def spot_of(me):
    return me // 4 % 2 * 2 + me % 2


def kernel_call(body, out_shape, operands, name, flops=0, in_bytes=0):
    specs = [SMEM if o.dtype == jnp.int32 and o.ndim == 1 else VMEM for o in operands]
    return pl.pallas_call(
        body,
        out_shape=out_shape,
        in_specs=specs,
        out_specs=jax.tree.map(lambda _: VMEM, out_shape),
        compiler_params=pltpu.CompilerParams(vmem_limit_bytes=12 * 1024 * 1024),
        cost_estimate=pl.CostEstimate(flops=flops, bytes_accessed=in_bytes, transcendentals=0),
        name=name,
    )(*operands)


def deal_body(starts, queries, keys_values, cot, rows, own, by_x, by_zl, by_both, held_rows, sems):
    core, me = lax.axis_index("head"), lax.axis_index("ctx")
    outs = (own, by_x, by_zl, by_both)
    start = starts[0]
    row = lax.broadcasted_iota(jnp.int32, (META, BLOCK), 0)
    meta = jnp.where(row == 0, start // BLOCK, jnp.where(row == 1, start % BLOCK, 0)).astype(F32).astype(BF16)
    cols = held_rows.shape[1]

    def copies(near, far, half):
        moves = []
        for flip, out in enumerate(outs):
            head = jnp.bitwise_xor(spot_of(me), flip)
            lanes = pl.ds(pl.multiple_of(head * BLOCK, BLOCK), BLOCK)
            for base, pair in ((0, near), (PART, far)):
                for at, source in enumerate(pair):
                    moves.append((source.at[:, lanes], out.at[base + at * BLOCK : base + (at + 1) * BLOCK, :]))
        moves.append((rows.at[:, half * cols : (half + 1) * cols], held_rows))
        moves = [pltpu.make_async_copy(a, b, sems.at[k]) for k, (a, b) in enumerate(moves)]
        for move in moves:
            move.start()
        for out in outs:
            out[PAIR:PART, :] = meta
            out[PART + PAIR :, :] = meta
        for move in moves:
            move.wait()

    asks = (queries, cot)
    gives = (keys_values.at[0], keys_values.at[1])

    @pl.when(core == 0)
    def _():
        copies(asks, gives, 0)

    @pl.when(core == 1)
    def _():
        copies(gives, asks, 1)


def attend_body(
    scale, seq_len, near_own, far_own, near_in, far_in, keep, near_out, far_out, near_1, near_2, far_1, far_2, near_1_sum, near_2_sum, far_1_sum, far_2_sum
):
    core, me = lax.axis_index("head"), lax.axis_index("ctx")
    zh, y = me // 8, me // 2 % 2
    spots = [jnp.bitwise_xor(spot_of(me), flip) for flip in range(4)]
    places = [spot // 2 * 4 + spot % 2 for spot in spots]
    wide = 4 * BLOCK

    def lower_of(meta):
        meta = meta.astype(F32)
        return (meta[0:1] * BLOCK + meta[1:2]).astype(jnp.int32)

    for side, (near, far) in enumerate(((near_own, far_own), (near_in, far_in))):
        for spot in range(4):
            rows = slice(spot * BLOCK, (spot + 1) * BLOCK)
            place = slice((4 * side + spot) * BLOCK, (4 * side + spot + 1) * BLOCK)
            near_1[place, :] = near[spot, :BLOCK, :]
            near_2[place, :] = near[spot, BLOCK:PAIR, :]
            far_1[side, rows, :] = far[spot, :BLOCK, :]
            far_2[side, rows, :] = far[spot, BLOCK:PAIR, :]
    near_1_sum[...] = jnp.zeros_like(near_1_sum)
    near_2_sum[...] = jnp.zeros_like(near_2_sum)
    lane = lax.broadcasted_iota(jnp.int32, (1, BLOCK), 1)
    row_in = lax.broadcasted_iota(jnp.int32, (BLOCK, wide), 0)
    grad_scale = scale * 0.5 / seq_len
    never = 1 << 20

    def work(role_q, side, carry):
        far_zh = jnp.where(side == 0, zh, 1 - zh)
        place = jnp.concatenate([lane + (far_zh * 8 + y * 2 + s) * BLOCK for s in places], axis=1)
        base_1, base_2 = far_1[side], far_2[side]
        if not role_q:
            own = jnp.concatenate([lower_of(far_own[s, PAIR:PART, :]) for s in range(4)], axis=1)
            other = jnp.concatenate([lower_of(far_in[s, PAIR:PART, :]) for s in range(4)], axis=1)
            low = jnp.where(side == 0, own, other)
        dscores, weights = [], []
        for chunk in range(4):
            rows = slice(chunk * PAIR, (chunk + 1) * PAIR)
            half = dot(near_1[rows, :], base_1, 1, 1) * (0.5 * scale)
            dprod = dot(near_2[rows, :], base_2, 1, 1)
            near_ref, near_y = (near_own, y) if chunk < 2 else (near_in, 1 - y)
            seen = []
            for at in range(2):
                start = (zh * 8 + near_y * 2 + places[chunk % 2 * 2 + at]) * BLOCK
                if role_q:
                    low = jnp.concatenate([lower_of(near_ref[chunk % 2 * 2 + at, PAIR:PART, :])] * 4, axis=1)
                    seen.append(row_in >= jnp.where(place >= low, place - start, never))
                else:
                    seen.append((row_in >= low - start) & (row_in <= place - start))
            seen = jnp.concatenate(seen, axis=0)
            tanh = jnp.tanh(half)
            twice = 1.0 + tanh
            weight = half * twice
            dscore = (dprod * twice) * (1.0 + half * (1.0 - tanh))
            weight = jnp.where(seen, weight, 0.0).astype(BF16)
            dscore = jnp.where(seen, dscore, 0.0).astype(BF16)
            near_1_sum[rows, :] += dot(dscore, base_1, 1, 0)
            if not role_q:
                near_2_sum[rows, :] += dot(weight, base_2, 1, 0)
            dscores.append(dscore)
            weights.append(weight)
        far_1_sum[side] = dot(jnp.concatenate(dscores, axis=0), near_1[...], 0, 0)
        if role_q:
            far_2_sum[side] = dot(jnp.concatenate(weights, axis=0), near_2[...], 0, 0)
        return carry

    for spot in range(4):
        far_out[spot] = jnp.zeros((2, BLOCK, BLOCK), BF16)

    @pl.when(core == 0)
    def _():
        lax.fori_loop(0, 1 + zh, functools.partial(work, True), 0)
        for spot in range(4):
            far_rows = slice(spot * BLOCK, (spot + 1) * BLOCK)
            keep[spot, 1] = far_2_sum[0, far_rows] * (1.0 / seq_len)
            far_out[spot, 1] = (far_2_sum[1, far_rows] * (1.0 / seq_len)).astype(BF16)

    @pl.when(core == 1)
    def _():
        lax.fori_loop(0, 2 - zh, functools.partial(work, False), 0)
        for spot in range(4):
            rows = slice(spot * BLOCK, (spot + 1) * BLOCK)
            keep[spot, 1] = near_2_sum[rows, :] * (1.0 / seq_len)

    for spot in range(4):
        rows = slice(spot * BLOCK, (spot + 1) * BLOCK)
        other = slice((4 + spot) * BLOCK, (5 + spot) * BLOCK)
        keep[spot, 0] = near_1_sum[rows, :] * grad_scale
        near_out[spot, 0] = (near_1_sum[other, :] * grad_scale).astype(BF16)
        near_out[spot, 1] = (near_2_sum[other, :] * (1.0 / seq_len)).astype(BF16)
        keep[spot, 2] = far_1_sum[0, rows] * grad_scale
        far_out[spot, 0] = (far_1_sum[1, rows] * grad_scale).astype(BF16)


def project_body(own, by_x, by_zl, by_both, weight, partial, sent, held):
    core, me = lax.axis_index("head"), lax.axis_index("ctx")
    for flip, part in enumerate((own, by_x, by_zl, by_both)):
        head = jnp.bitwise_xor(spot_of(me), flip)
        for slot in range(3):
            held[slot, :, pl.ds(pl.multiple_of(head * BLOCK, BLOCK), BLOCK)] = part[slot]
    total = dot(held[1], weight[2], 1, 1)
    total = total + dot(held[0], weight[core], 1, 1)
    total = total + dot(held[2], weight[1 - core], 1, 1)
    partial[...] = total
    sent[...] = total.astype(BF16)


def pack_body(own, other, adapter, placing, slots, out, grad, turned):
    core = lax.axis_index("head")
    n_ctx = out.shape[0]
    head_cols = adapter.shape[1]
    capacity = placing.shape[1] // n_ctx
    tiles = head_cols // BLOCK
    share = own.shape[1] // n_ctx // 2
    total = own[...] + other[...].astype(F32)
    grad[...] = total
    rounded = total.astype(BF16)
    turned[...] = jnp.transpose(rounded)
    rows = grad[:, pl.ds(pl.multiple_of(core * head_cols, head_cols), head_cols)]
    rows = rows + dot(rounded, adapter[...], 1, 0)
    rows = jnp.concatenate([rows.astype(BF16), slots[...]], axis=1)
    cells = dot(placing[...], rows, 0, 0).astype(BF16)
    for p in range(n_ctx):
        for tile in range(tiles + 1):
            out[p, tile * capacity : (tile + 1) * capacity, :] = cells[
                p * capacity : (p + 1) * capacity, tile * BLOCK : (tile + 1) * BLOCK
            ]
        first = pl.multiple_of(p * 2 * share + core * share, share)
        out[p, (tiles + 1) * capacity :, :] = turned[pl.ds(first, share), :]


def place_body(owners, slots, placing, marks):
    count = owners.shape[1]
    capacity = placing.shape[1] // 16
    lane = lax.broadcasted_iota(jnp.int32, (count, BLOCK), 1)
    row = lax.broadcasted_iota(jnp.int32, (count, BLOCK), 0)
    owner_row = jnp.broadcast_to(owners[...].astype(F32), (count, BLOCK))
    owner = jnp.transpose(owner_row)
    same = jnp.where((owner == owner_row) & (lane < row), 1.0, 0.0)
    ranking = jnp.sum(same, axis=1, keepdims=True)
    cell = owner * capacity + ranking
    for tile in range(placing.shape[1] // BLOCK):
        hit = cell == (lane + tile * BLOCK).astype(F32)
        placing[:, tile * BLOCK : (tile + 1) * BLOCK] = hit.astype(F32).astype(BF16)
    mark = jnp.broadcast_to(slots[...] + 1, (count, BLOCK)).astype(F32)
    marks[...] = jnp.transpose(mark).astype(BF16)


def merge_body(keep, near, far, *outs):
    for at, out in enumerate(outs):
        out[0] = (keep[at, 0] + near[at, 0].astype(F32)).astype(BF16)
        out[1] = (keep[at, 1] + near[at, 1].astype(F32) + far[at, 1].astype(F32)).astype(BF16)
        out[2] = (keep[at, 2] + far[at, 0].astype(F32)).astype(BF16)


def finish_body(got, other, *refs):
    pieces, held, grad, targets = refs[:8], refs[8:11], refs[11], refs[12:15]
    made, rows_held, in_sems, out_sems = refs[15:18], refs[18], refs[19], refs[20]
    chunks = out_sems.shape[1]
    span = held[0].shape[0] // chunks

    def rows_of(c):
        return slice(c * span, (c + 1) * span)

    stores = [
        [pltpu.make_async_copy(a.at[rows_of(c), :], b.at[rows_of(c), :], out_sems.at[k, c]) for k, (a, b) in enumerate(zip(made, targets))]
        for c in range(chunks)
    ]
    part = rows_held.shape[0] // 8
    loads = [pltpu.make_async_copy(p, rows_held.at[k * part : (k + 1) * part, :], in_sems.at[k]) for k, p in enumerate(pieces)]
    for move in loads:
        move.start()
    core, me = lax.axis_index("head"), lax.axis_index("ctx")
    share = other.shape[1]
    tiles = held[0].shape[1] // BLOCK
    table_rows = held[0].shape[0]
    n_ctx = got.shape[0]
    capacity = (got.shape[1] - share) // (tiles + 1)
    marks = got[:, tiles * capacity : (tiles + 1) * capacity, :].reshape(n_ctx * capacity, BLOCK).astype(F32)
    lane = lax.broadcasted_iota(jnp.int32, marks.shape, 1)
    landing = [(marks == (lane + (at * BLOCK + 1)).astype(F32)).astype(F32) for at in range(table_rows // BLOCK)]
    landing = jnp.concatenate(landing, axis=1).astype(BF16)
    cells = [got[:, tile * capacity : (tile + 1) * capacity, :].reshape(n_ctx * capacity, BLOCK) for tile in range(tiles)]
    cells = jnp.concatenate(cells + [jnp.ones(marks.shape, BF16)], axis=1)
    summed_all = dot(landing, cells, 0, 0)
    for c in range(chunks):
        rows = rows_of(c)
        summed = summed_all[rows, : tiles * BLOCK]
        touched = jnp.concatenate([summed_all[rows, tiles * BLOCK :]] * tiles, axis=1) > 0.0
        old, m, v = [ref[rows, :] for ref in held]
        fresh_m = beta_first * m + (1.0 - beta_first) * summed
        fresh_v = beta_second * v + (1.0 - beta_second) * summed * summed
        update = learn_rate * (fresh_m / first_fix) / (jnp.sqrt(fresh_v / second_fix) + epsilon)
        made[0][rows, :] = jnp.where(touched, old - update, old)
        made[1][rows, :] = jnp.where(touched, fresh_m, m)
        made[2][rows, :] = jnp.where(touched, fresh_v, v)
        for move in stores[c]:
            move.start()
    masks = [0]
    for bit in ROUNDS:
        masks = masks + [mask ^ bit for mask in masks]
    senders = [jnp.bitwise_xor(me, mask) for mask in masks]
    width = (tiles + 1) * capacity
    mine_t = jnp.concatenate([got[s, width:, :] for s in senders], axis=1)
    other_t = jnp.concatenate([other[s] for s in senders], axis=1)
    both_t = jnp.concatenate([mine_t, other_t], axis=0)
    for move in loads:
        move.wait()
    both = dot(both_t, rows_held[...], 1, 0)
    grad[pl.ds(pl.multiple_of(core * share, share), share), :] = both[:share]
    grad[pl.ds(pl.multiple_of((1 - core) * share, share), share), :] = both[share:]
    for store in stores:
        for move in store:
            move.wait()


def dealt_device(
    queries,
    keys_values,
    attn_cot,
    event_rows,
    adapter,
    qkv_weight,
    starts,
    owners,
    slots,
    table,
    moment_m,
    moment_v,
):
    shape = jax.ShapeDtypeStruct
    n_ctx = lax.axis_size("ctx")
    rows_here = queries.shape[0]
    seq_len = rows_here * n_ctx
    head_cols = adapter.shape[1]
    width = event_rows.shape[1]
    capacity = max(2, 2 * rows_here // n_ctx)
    dealt = shape((2 * PART, BLOCK), BF16)
    *dealt, own_rows = pl.pallas_call(
        deal_body,
        out_shape=(dealt,) * 4 + (shape((rows_here, head_cols), BF16),),
        in_specs=[SMEM] + [pl.BlockSpec(memory_space=pl.ANY)] * 4,
        out_specs=(VMEM,) * 5,
        scratch_shapes=[pltpu.SemaphoreType.DMA((17,))],
        compiler_params=pltpu.CompilerParams(vmem_limit_bytes=56 * 1024 * 1024),
        name="deal",
    )(starts, queries, keys_values, attn_cot, event_rows)

    def exchange(sent, bit):
        return lax.ppermute(sent, "ctx", [(i, i ^ bit) for i in range(16)])

    zh_rows = exchange(own_rows, ROUNDS[0])
    parts = dealt[:1] + [exchange(part, bit) for part, bit in zip(dealt[1:], (1, 4, 5))]
    *parts, zh_rows = lax.optimization_barrier((*parts, zh_rows))
    two = jnp.concatenate([own_rows, zh_rows], axis=0)
    near_own = jnp.stack([part[:PART] for part in parts])
    far_own = jnp.stack([part[PART:] for part in parts])
    far_in = lax.ppermute(far_own, ("ctx", "head"), FAR_OUT)
    near_in = lax.ppermute(near_own, "ctx", ACROSS_Y)
    zl_rows, x_rows, y_rows = [exchange(two, bit) for bit in ROUNDS[1:]]
    keep, near_out, far_out = pl.pallas_call(
        functools.partial(attend_body, 1.0 / math.sqrt(HD), float(seq_len)),
        out_shape=(
            shape((4, 3, BLOCK, BLOCK), F32),
            shape((4, 2, BLOCK, BLOCK), BF16),
            shape((4, 2, BLOCK, BLOCK), BF16),
        ),
        in_specs=[VMEM] * 4,
        out_specs=(VMEM, VMEM, VMEM),
        scratch_shapes=[
            pltpu.VMEM((8 * BLOCK, BLOCK), BF16),
            pltpu.VMEM((8 * BLOCK, BLOCK), BF16),
            pltpu.VMEM((2, 4 * BLOCK, BLOCK), BF16),
            pltpu.VMEM((2, 4 * BLOCK, BLOCK), BF16),
            pltpu.VMEM((8 * BLOCK, BLOCK), F32),
            pltpu.VMEM((8 * BLOCK, BLOCK), F32),
            pltpu.VMEM((2, 4 * BLOCK, BLOCK), F32),
            pltpu.VMEM((2, 4 * BLOCK, BLOCK), F32),
        ],
        compiler_params=pltpu.CompilerParams(vmem_limit_bytes=12 * 1024 * 1024),
        cost_estimate=pl.CostEstimate(flops=2 * 10**9, bytes_accessed=2**21, transcendentals=0),
        name="attend",
    )(near_own, far_own, near_in, far_in)
    near_out, far_out, zl_rows, x_rows, y_rows = lax.optimization_barrier(
        (near_out, far_out, zl_rows, x_rows, y_rows)
    )
    zl_x_rows = exchange(zl_rows, ROUNDS[2])
    zl_y_rows = exchange(zl_rows, ROUNDS[3])
    far_back = lax.ppermute(far_out, ("ctx", "head"), FAR_BACK)
    near_back = lax.ppermute(near_out, "ctx", ACROSS_Y)
    own, *parts = kernel_call(
        merge_body, (shape((3, BLOCK, BLOCK), BF16),) * 4, (keep, near_back, far_back), "merge"
    )
    own, *parts, zl_x_rows, zl_y_rows = lax.optimization_barrier((own, *parts, zl_x_rows, zl_y_rows))
    x_y_rows, zl_x_y_rows = [exchange(rows, ROUNDS[3]) for rows in (x_rows, zl_x_rows)]
    parts = [exchange(part, bit) for part, bit in zip(parts, (1, 4, 5))]
    *parts, x_y_rows = lax.optimization_barrier((*parts, x_y_rows))
    partial, sent = pl.pallas_call(
        project_body,
        out_shape=(shape((rows_here, width), F32), shape((rows_here, width), BF16)),
        in_specs=[VMEM] * 5,
        out_specs=(VMEM, VMEM),
        scratch_shapes=[pltpu.VMEM((3, rows_here, queries.shape[1]), BF16)],
        compiler_params=pltpu.CompilerParams(vmem_limit_bytes=12 * 1024 * 1024),
        name="project",
    )(own, *parts, qkv_weight)
    sent, owners, slots = lax.optimization_barrier((sent, owners, slots))
    placing, marks = kernel_call(
        place_body,
        (shape((rows_here, n_ctx * capacity), BF16), shape((rows_here, BLOCK), BF16)),
        (owners.reshape(1, rows_here), slots.reshape(1, rows_here)),
        "place",
    )
    other = lax.ppermute(sent, "head", SWAP)
    other, zl_x_y_rows = lax.optimization_barrier((other, zl_x_y_rows))
    share = width // n_ctx // 2
    packed_rows = capacity * (head_cols // BLOCK + 1)
    packed = pl.pallas_call(
        pack_body,
        out_shape=shape((n_ctx, packed_rows + share, BLOCK), BF16),
        in_specs=[VMEM] * 5,
        out_specs=VMEM,
        scratch_shapes=[pltpu.VMEM((rows_here, width), F32), pltpu.VMEM((width, rows_here), BF16)],
        compiler_params=pltpu.CompilerParams(vmem_limit_bytes=12 * 1024 * 1024),
        name="pack",
    )(partial, other, adapter, placing, marks)
    got = lax.all_to_all(packed, "ctx", 0, 0, tiled=True)
    other_share = lax.ppermute(got[:, packed_rows:], "head", SWAP)
    held = shape(table.shape, F32)
    pieces = (two, zl_rows, x_rows, zl_x_rows, y_rows, zl_y_rows, x_y_rows, zl_x_y_rows)
    return pl.pallas_call(
        finish_body,
        out_shape=(shape((width // n_ctx, head_cols), F32), held, held, held),
        in_specs=[VMEM] * 2 + [pl.BlockSpec(memory_space=pl.ANY)] * len(pieces) + [VMEM] * 3,
        out_specs=(VMEM,) + (pl.BlockSpec(memory_space=pl.ANY),) * 3,
        scratch_shapes=[pltpu.VMEM(table.shape, F32)] * 3
        + [
            pltpu.VMEM((n_ctx * rows_here, head_cols), BF16),
            pltpu.SemaphoreType.DMA((len(pieces),)),
            pltpu.SemaphoreType.DMA((3, 4)),
        ],
        compiler_params=pltpu.CompilerParams(vmem_limit_bytes=12 * 1024 * 1024),
        name="finish",
    )(got, other_share, *pieces, table, moment_m, moment_v)


def per_device(*arrays):
    rows_here, cols_here = arrays[0].shape
    fits = lax.axis_size("ctx") == 16 and lax.axis_size("head") == 2
    if fits and rows_here == BLOCK and cols_here == 4 * HD and arrays[9].shape[0] == 2 * BLOCK:
        return dealt_device(*arrays)
    return plain_device(*arrays)


def solution(mesh):
    placed = (
        P("ctx", "head"),
        P(None, "ctx", "head"),
        P("ctx", "head"),
        P("ctx", None),
        P(None, "head"),
        P(None, None, "head"),
        P("ctx"),
        P("ctx", None),
        P("ctx"),
        P("ctx", "head"),
        P("ctx", "head"),
        P("ctx", "head"),
    )
    return jax.shard_map(
        per_device,
        mesh=mesh,
        in_specs=placed,
        out_specs=(P("ctx", "head"), P("ctx", "head"), P("ctx", "head"), P("ctx", "head")),
        check_vma=False,
    )
```

```python
import functools
import math

import jax
import jax.numpy as jnp
from jax import lax
from jax.experimental import pallas as pl
from jax.experimental.pallas import tpu as pltpu
from jax.sharding import PartitionSpec as P

HD = 128
QBLK = 128


beta_first = 0.9
beta_second = 0.999
learn_rate = 0.01
epsilon = 1e-08
first_fix = 1.0 - beta_first**10.0
second_fix = 1.0 - beta_second**10.0


def adam_rows(summed, touched, table, moment_m, moment_v):
    fresh_m = beta_first * moment_m + (1.0 - beta_first) * summed
    fresh_v = beta_second * moment_v + (1.0 - beta_second) * summed * summed
    update = learn_rate * (fresh_m / first_fix) / (jnp.sqrt(fresh_v / second_fix) + epsilon)
    keep = touched[:, None]
    return (
        jnp.where(keep, table - update, table),
        jnp.where(keep, fresh_m, moment_m),
        jnp.where(keep, fresh_v, moment_v),
    )


def pair_scores(query_part, key_part, query_places, query_lower, key_places):
    scale = 1.0 / math.sqrt(HD)
    scores = (
        jnp.einsum("ihd,jhd->hij", query_part, key_part, preferred_element_type=jnp.float32) * scale
    )
    seen = (key_places[None, :] <= query_places[:, None]) & (
        key_places[None, :] >= query_lower[:, None]
    )
    squash = jax.nn.sigmoid(scores)
    return (scores, squash, seen[None])


def score_grads(scores, squash, seen, cotangent_piece, value_part, seq_len):
    dprod = jnp.einsum(
        "ihd,jhd->hij", cotangent_piece, value_part, preferred_element_type=jnp.float32
    )
    return jnp.where(seen, dprod * squash * (1.0 + scores * (1.0 - squash)) / seq_len, 0.0).astype(
        jnp.bfloat16
    )


def score_weights(scores, squash, seen, seq_len):
    return jnp.where(seen, scores * squash / seq_len, 0.0).astype(jnp.bfloat16)


def over_blocks(total, fn, carry):
    sub = math.gcd(total, 1024)
    return lax.fori_loop(
        0, total // sub, lambda index, inner_loop: fn(inner_loop, index * sub), carry
    )


def plain_device(
    queries,
    keys_values,
    attn_cot,
    event_rows,
    adapter,
    qkv_weight,
    starts,
    owners,
    slots,
    table,
    moment_m,
    moment_v,
):
    rows_here = queries.shape[0]
    feature_cols = queries.shape[1]
    heads_here = feature_cols // HD
    n_ctx = lax.axis_size("ctx")
    seq_len = rows_here * n_ctx
    scale = 1.0 / math.sqrt(HD)
    myself = lax.axis_index("ctx")
    local_first = myself * rows_here
    local_places = local_first + jnp.arange(rows_here, dtype=jnp.int32)
    lower = jnp.repeat(starts, QBLK, total_repeat_length=rows_here)
    least_lower = jnp.min(lower)
    query_heads = queries.reshape(rows_here, heads_here, HD)
    cot_heads = attn_cot.reshape(rows_here, heads_here, HD)
    key_heads = keys_values[0].reshape(rows_here, heads_here, HD)
    value_heads = keys_values[1].reshape(rows_here, heads_here, HD)
    zeros = jnp.zeros((rows_here, heads_here, HD), jnp.float32)
    piece = lax.all_gather(keys_values, "ctx", axis=1, tiled=True)

    def key_one_block(inner_loop, offset):
        sub = math.gcd(piece.shape[1], 1024)
        key_first = offset
        live = (key_first <= local_first + rows_here - 1) & (key_first + sub - 1 >= least_lower)

        def key_working(values):
            part = lax.dynamic_slice_in_dim(piece, offset, sub, 1)
            key_part = part[0].reshape(sub, heads_here, HD)
            value_part = part[1].reshape(sub, heads_here, HD)
            key_places = key_first + jnp.arange(sub, dtype=jnp.int32)
            scores, squash, seen = pair_scores(
                query_heads, key_part, local_places, lower, key_places
            )
            dscore = score_grads(scores, squash, seen, cot_heads, value_part, seq_len)
            return values + jnp.einsum(
                "hij,jhd->ihd", dscore, key_part, preferred_element_type=jnp.float32
            )

        return lax.cond(live, key_working, lambda values: values, inner_loop)

    query_grad = over_blocks(piece.shape[1], key_one_block, zeros)
    query_piece = (
        lax.all_gather(queries, "ctx", axis=0, tiled=True),
        lax.all_gather(attn_cot, "ctx", axis=0, tiled=True),
        lax.all_gather(lower, "ctx", axis=0, tiled=True),
    )

    def query_one_block(inner_loop, offset):
        sub = math.gcd(query_piece[0].shape[0], 1024)
        query_first = offset
        query_lower = lax.dynamic_slice_in_dim(query_piece[2], offset, sub, 0)
        live = (local_first <= query_first + sub - 1) & (
            local_first + rows_here - 1 >= jnp.min(query_lower)
        )

        def query_working(values):
            query_part = lax.dynamic_slice_in_dim(query_piece[0], offset, sub, 0).reshape(
                sub, heads_here, HD
            )
            cotangent_piece = lax.dynamic_slice_in_dim(query_piece[1], offset, sub, 0).reshape(
                sub, heads_here, HD
            )
            query_places = query_first + jnp.arange(sub, dtype=jnp.int32)
            scores, squash, seen = pair_scores(
                query_part, key_heads, query_places, query_lower, local_places
            )
            weights = score_weights(scores, squash, seen, seq_len)
            dscore = score_grads(scores, squash, seen, cotangent_piece, value_heads, seq_len)
            key_add = jnp.einsum(
                "hij,ihd->jhd", dscore, query_part, preferred_element_type=jnp.float32
            )
            value_add = jnp.einsum(
                "hij,ihd->jhd", weights, cotangent_piece, preferred_element_type=jnp.float32
            )
            return (values[0] + key_add, values[1] + value_add)

        return lax.cond(live, query_working, lambda values: values, inner_loop)

    key_grad, value_grad = over_blocks(query_piece[0].shape[0], query_one_block, (zeros, zeros))
    head_grads = (
        jnp.stack([query_grad * scale, key_grad * scale, value_grad])
        .astype(jnp.bfloat16)
        .reshape(3, rows_here, feature_cols)
    )
    partial_grad = jnp.einsum(
        "mtc,mdc->td", head_grads, qkv_weight, preferred_element_type=jnp.float32
    )
    head_cols = adapter.shape[1]
    first_col = lax.axis_index("head") * head_cols
    layer_grad = lax.psum(partial_grad.astype(jnp.bfloat16), "head").astype(jnp.float32)
    layer_grad_b = layer_grad.astype(jnp.bfloat16)
    own_grad = lax.dynamic_slice_in_dim(layer_grad, first_col, head_cols, 1)
    row_grads = own_grad + jnp.dot(layer_grad_b, adapter, preferred_element_type=jnp.float32)
    own_rows = lax.dynamic_slice_in_dim(event_rows, first_col, head_cols, 1)
    adapter_grad = lax.psum_scatter(
        lax.dot_general(
            layer_grad_b, own_rows, (((0,), (0,)), ((), ())), preferred_element_type=jnp.float32
        ),
        "ctx",
        scatter_dimension=0,
        tiled=True,
    )
    capacity = max(2, 2 * rows_here // n_ctx)
    target = owners[:, 0]
    onehot = (target[:, None] == jnp.arange(n_ctx, dtype=jnp.int32)[None, :]).astype(jnp.int32)
    prior_blocks = jnp.cumsum(onehot, axis=0) - onehot
    ranking = jnp.sum(prior_blocks * onehot, axis=1)
    cell_index = target * capacity + ranking
    placing = cell_index[:, None] == jnp.arange(n_ctx * capacity, dtype=jnp.int32)[None, :]
    send_rows = lax.dot_general(
        placing.astype(jnp.float32),
        row_grads,
        (((0,), (0,)), ((), ())),
        precision=lax.Precision.HIGHEST,
    ).reshape(n_ctx, capacity, head_cols)
    send_slots = (jnp.sum(jnp.where(placing, slots[:, None] + 1, 0), axis=0) - 1).reshape(
        n_ctx, capacity
    )
    got_rows, got_slots = (
        lax.all_to_all(
            send_rows.astype(jnp.bfloat16), "ctx", split_axis=0, concat_axis=0, tiled=True
        ).astype(send_rows.dtype),
        lax.all_to_all(send_slots, "ctx", split_axis=0, concat_axis=0, tiled=True),
    )
    table_rows = table.shape[0]
    landing = got_slots.reshape(-1)[None, :] == jnp.arange(table_rows, dtype=jnp.int32)[:, None]
    summed = jnp.dot(
        landing.astype(jnp.float32),
        got_rows.reshape(n_ctx * capacity, head_cols),
        precision=lax.Precision.HIGHEST,
    )
    touched = jnp.sum(landing.astype(jnp.int32), axis=1) > 0
    new_table, new_m, new_v = adam_rows(summed, touched, table, moment_m, moment_v)
    return (adapter_grad, new_table, new_m, new_v)


BLOCK = 128
PAIR = 2 * BLOCK
META = 16
PART = PAIR + META
ACROSS_Y = [(i, i ^ 2) for i in range(16)]
FAR_OUT = [(i * 2, (i + 8) * 2) for i in range(8)] + [((i + 8) * 2 + 1, i * 2 + 1) for i in range(8)]
FAR_BACK = [(b, a) for a, b in FAR_OUT]
SWAP = [(0, 1), (1, 0)]
ROUNDS = (8, 4, 1, 2)
F32 = jnp.float32
BF16 = jnp.bfloat16
VMEM = pl.BlockSpec(memory_space=pltpu.VMEM)
SMEM = pl.BlockSpec(memory_space=pltpu.SMEM)


def dot(a, b, axis_a, axis_b):
    return lax.dot_general(a, b, (((axis_a,), (axis_b,)), ((), ())), preferred_element_type=F32)


def spot_of(me):
    return me // 4 % 2 * 2 + me % 2


def kernel_call(body, out_shape, operands, name, flops=0, in_bytes=0):
    specs = [SMEM if o.dtype == jnp.int32 and o.ndim == 1 else VMEM for o in operands]
    return pl.pallas_call(
        body,
        out_shape=out_shape,
        in_specs=specs,
        out_specs=jax.tree.map(lambda _: VMEM, out_shape),
        compiler_params=pltpu.CompilerParams(vmem_limit_bytes=12 * 1024 * 1024),
        cost_estimate=pl.CostEstimate(flops=flops, bytes_accessed=in_bytes, transcendentals=0),
        name=name,
    )(*operands)


def deal_body(starts, queries, keys_values, cot, rows, own, by_x, by_zl, by_both, held_rows, sems):
    core, me = lax.axis_index("head"), lax.axis_index("ctx")
    outs = (own, by_x, by_zl, by_both)
    start = starts[0]
    row = lax.broadcasted_iota(jnp.int32, (META, BLOCK), 0)
    meta = jnp.where(row == 0, start // BLOCK, jnp.where(row == 1, start % BLOCK, 0)).astype(F32).astype(BF16)
    cols = held_rows.shape[1]

    def copies(near, far, half):
        moves = []
        for flip, out in enumerate(outs):
            head = jnp.bitwise_xor(spot_of(me), flip)
            lanes = pl.ds(pl.multiple_of(head * BLOCK, BLOCK), BLOCK)
            for base, pair in ((0, near), (PART, far)):
                for at, source in enumerate(pair):
                    moves.append((source.at[:, lanes], out.at[base + at * BLOCK : base + (at + 1) * BLOCK, :]))
        moves.append((rows.at[:, half * cols : (half + 1) * cols], held_rows))
        moves = [pltpu.make_async_copy(a, b, sems.at[k]) for k, (a, b) in enumerate(moves)]
        for move in moves:
            move.start()
        for out in outs:
            out[PAIR:PART, :] = meta
            out[PART + PAIR :, :] = meta
        for move in moves:
            move.wait()

    asks = (queries, cot)
    gives = (keys_values.at[0], keys_values.at[1])

    @pl.when(core == 0)
    def _():
        copies(asks, gives, 0)

    @pl.when(core == 1)
    def _():
        copies(gives, asks, 1)


def gather_body(own, rows_1, by_x, by_zl, by_both, rows_2, far, near, two):
    for flip, part in enumerate((own, by_x, by_zl, by_both)):
        near[flip] = part[:PART, :]
        far[flip] = part[PART:, :]
    count = rows_1.shape[0]
    two[:count, :] = rows_1[...]
    two[count:, :] = rows_2[...]


def lower_of(meta):
    meta = meta.astype(F32)
    return (meta[0:1] * BLOCK + meta[1:2]).astype(jnp.int32)


def attend(scale, role_q, crossing, nears, far, far_1, far_2, near_1_sum, near_2_sum, put_far_1, put_far_2):
    me = lax.axis_index("ctx")
    zh, y = me // 8, me // 2 % 2
    spots = [jnp.bitwise_xor(spot_of(me), flip) for flip in range(4)]
    places = [spot // 2 * 4 + spot % 2 for spot in spots]
    lane = lax.broadcasted_iota(jnp.int32, (1, BLOCK), 1)
    row_in = lax.broadcasted_iota(jnp.int32, (BLOCK, 4 * BLOCK), 0)
    never = 1 << 20
    far_zh = 1 - zh if crossing else zh
    place = jnp.concatenate([lane + (far_zh * 8 + y * 2 + s) * BLOCK for s in places], axis=1)
    base_1, base_2 = far_1[...], far_2[...]
    if not role_q:
        low = jnp.concatenate([lower_of(far[s, PAIR:PART, :]) for s in range(4)], axis=1)
    dscores, weights, firsts, seconds = [], [], [], []
    for chunk in range(4):
        rows = slice(chunk * PAIR, (chunk + 1) * PAIR)
        near_ref, near_y = nears[chunk // 2], (y, 1 - y)[chunk // 2]
        pair = (chunk % 2 * 2, chunk % 2 * 2 + 1)
        first = jnp.concatenate([near_ref[s, :BLOCK, :] for s in pair], axis=0)
        second = jnp.concatenate([near_ref[s, BLOCK:PAIR, :] for s in pair], axis=0)
        half = dot(first, base_1, 1, 1) * (0.5 * scale)
        dprod = dot(second, base_2, 1, 1)
        seen = []
        for s in pair:
            start = (zh * 8 + near_y * 2 + places[s]) * BLOCK
            if role_q:
                low = jnp.concatenate([lower_of(near_ref[s, PAIR:PART, :])] * 4, axis=1)
                seen.append(row_in >= jnp.where(place >= low, place - start, never))
            else:
                seen.append((row_in >= low - start) & (row_in <= place - start))
        seen = jnp.concatenate(seen, axis=0)
        tanh = jnp.tanh(half)
        twice = 1.0 + tanh
        weight = half * twice
        dscore = (dprod * twice) * (1.0 + half * (1.0 - tanh))
        weight = jnp.where(seen, weight, 0.0).astype(BF16)
        dscore = jnp.where(seen, dscore, 0.0).astype(BF16)
        grad_1 = dot(dscore, base_1, 1, 0)
        near_1_sum[rows, :] = near_1_sum[rows, :] + grad_1 if crossing else grad_1
        if not role_q:
            grad_2 = dot(weight, base_2, 1, 0)
            near_2_sum[rows, :] = near_2_sum[rows, :] + grad_2 if crossing else grad_2
        dscores.append(dscore)
        weights.append(weight)
        firsts.append(first)
        seconds.append(second)
    put_far_1(dot(jnp.concatenate(dscores, axis=0), jnp.concatenate(firsts, axis=0), 0, 0))
    if role_q:
        put_far_2(dot(jnp.concatenate(weights, axis=0), jnp.concatenate(seconds, axis=0), 0, 0))


def gather_far(far, far_1, far_2):
    for spot in range(4):
        rows = slice(spot * BLOCK, (spot + 1) * BLOCK)
        far_1[rows, :] = far[spot, :BLOCK, :]
        far_2[rows, :] = far[spot, BLOCK:PAIR, :]


def attend_own_body(scale, near_own, far_own, near_in, near_1_sum, near_2_sum, far_sum, far_1, far_2):
    gather_far(far_own, far_1, far_2)
    core = lax.axis_index("head")

    def put(at):
        def store(value):
            far_sum[at] = value

        return store

    rest = ((near_own, near_in), far_own, far_1, far_2, near_1_sum, near_2_sum, put(0), put(1))

    @pl.when(core == 0)
    def _():
        near_2_sum[...] = jnp.zeros_like(near_2_sum)
        attend(scale, True, False, *rest)

    @pl.when(core == 1)
    def _():
        far_sum[1] = jnp.zeros((4 * BLOCK, BLOCK), F32)
        attend(scale, False, False, *rest)


def attend_far_body(scale, seq_len, near_own, near_in, far_in, _1, _2, near_1_sum, near_2_sum, far_out, far_1, far_2):
    core, zh = lax.axis_index("head"), lax.axis_index("ctx") // 8
    far_out[...] = jnp.zeros_like(far_out)

    def put(at, factor):
        def store(value):
            for spot in range(4):
                far_out[spot, at] = (value[spot * BLOCK : (spot + 1) * BLOCK] * factor).astype(BF16)

        return store

    puts = (put(0, scale * 0.5 / seq_len), put(1, 1.0 / seq_len))
    rest = ((near_own, near_in), far_in, far_1, far_2, near_1_sum, near_2_sum, *puts)

    @pl.when((core == 0) & (zh == 1))
    def _():
        gather_far(far_in, far_1, far_2)
        attend(scale, True, True, *rest)

    @pl.when((core == 1) & (zh == 0))
    def _():
        gather_far(far_in, far_1, far_2)
        attend(scale, False, True, *rest)


def near_body(scale, seq_len, near_1_sum, near_2_sum, out):
    for spot in range(4):
        rows = slice((4 + spot) * BLOCK, (5 + spot) * BLOCK)
        out[spot, 0] = (near_1_sum[rows, :] * (scale * 0.5 / seq_len)).astype(BF16)
        out[spot, 1] = (near_2_sum[rows, :] * (1.0 / seq_len)).astype(BF16)


def project_body(by_both, by_zl, by_x, own, weight, partial, sent, held):
    core, me = lax.axis_index("head"), lax.axis_index("ctx")
    for flip, part in enumerate((own, by_x, by_zl, by_both)):
        head = jnp.bitwise_xor(spot_of(me), flip)
        for slot in range(3):
            held[slot, :, pl.ds(pl.multiple_of(head * BLOCK, BLOCK), BLOCK)] = part[slot]
    total = dot(held[1], weight[2], 1, 1)
    total = total + dot(held[0], weight[core], 1, 1)
    total = total + dot(held[2], weight[1 - core], 1, 1)
    partial[...] = total
    sent[...] = total.astype(BF16)


def pack_body(own, other, adapter, placing, slots, out, grad, turned):
    core = lax.axis_index("head")
    n_ctx = out.shape[0]
    head_cols = adapter.shape[1]
    capacity = placing.shape[1] // n_ctx
    tiles = head_cols // BLOCK
    share = own.shape[1] // n_ctx // 2
    total = own[...] + other[...].astype(F32)
    grad[...] = total
    rounded = total.astype(BF16)
    turned[...] = jnp.transpose(rounded)
    rows = grad[:, pl.ds(pl.multiple_of(core * head_cols, head_cols), head_cols)]
    rows = rows + dot(rounded, adapter[...], 1, 0)
    rows = jnp.concatenate([rows.astype(BF16), slots[...]], axis=1)
    cells = dot(placing[...], rows, 0, 0).astype(BF16)
    for p in range(n_ctx):
        for tile in range(tiles + 1):
            out[p, tile * capacity : (tile + 1) * capacity, :] = cells[
                p * capacity : (p + 1) * capacity, tile * BLOCK : (tile + 1) * BLOCK
            ]
        first = pl.multiple_of(p * 2 * share + core * share, share)
        out[p, (tiles + 1) * capacity :, :] = turned[pl.ds(first, share), :]


def place_body(owners, slots, placing, marks):
    count = owners.shape[1]
    capacity = placing.shape[1] // 16
    lane = lax.broadcasted_iota(jnp.int32, (count, BLOCK), 1)
    row = lax.broadcasted_iota(jnp.int32, (count, BLOCK), 0)
    owner_row = jnp.broadcast_to(owners[...].astype(F32), (count, BLOCK))
    owner = jnp.transpose(owner_row)
    same = jnp.where((owner == owner_row) & (lane < row), 1.0, 0.0)
    ranking = jnp.sum(same, axis=1, keepdims=True)
    cell = owner * capacity + ranking
    for tile in range(placing.shape[1] // BLOCK):
        hit = cell == (lane + tile * BLOCK).astype(F32)
        placing[:, tile * BLOCK : (tile + 1) * BLOCK] = hit.astype(F32).astype(BF16)
    mark = jnp.broadcast_to(slots[...] + 1, (count, BLOCK)).astype(F32)
    marks[...] = jnp.transpose(mark).astype(BF16)


def merge_body(flips, scale, seq_len, far, near, near_1_sum, near_2_sum, far_sum, *outs):
    grad_scale, weight_scale = scale * 0.5 / seq_len, 1.0 / seq_len
    for flip, out in zip(flips, outs):
        rows = slice(flip * BLOCK, (flip + 1) * BLOCK)
        out[0] = (near_1_sum[rows, :] * grad_scale + near[flip, 0].astype(F32)).astype(BF16)
        both = (near_2_sum[rows, :] + far_sum[1, rows, :]) * weight_scale
        out[1] = (both + near[flip, 1].astype(F32) + far[flip, 1].astype(F32)).astype(BF16)
        out[2] = (far_sum[0, rows, :] * grad_scale + far[flip, 0].astype(F32)).astype(BF16)


def finish_body(got, other, *refs):
    pieces, held, grad, targets = refs[:8], refs[8:11], refs[11], refs[12:15]
    made, rows_held, in_sems, out_sems = refs[15:18], refs[18], refs[19], refs[20]
    chunks = out_sems.shape[1]
    span = held[0].shape[0] // chunks

    def rows_of(c):
        return slice(c * span, (c + 1) * span)

    stores = [
        [pltpu.make_async_copy(a.at[rows_of(c), :], b.at[rows_of(c), :], out_sems.at[k, c]) for k, (a, b) in enumerate(zip(made, targets))]
        for c in range(chunks)
    ]
    part = rows_held.shape[0] // 8
    loads = [pltpu.make_async_copy(p, rows_held.at[k * part : (k + 1) * part, :], in_sems.at[k]) for k, p in enumerate(pieces)]
    for move in loads:
        move.start()
    core, me = lax.axis_index("head"), lax.axis_index("ctx")
    share = other.shape[1]
    tiles = held[0].shape[1] // BLOCK
    table_rows = held[0].shape[0]
    n_ctx = got.shape[0]
    capacity = (got.shape[1] - share) // (tiles + 1)
    marks = got[:, tiles * capacity : (tiles + 1) * capacity, :].reshape(n_ctx * capacity, BLOCK).astype(F32)
    lane = lax.broadcasted_iota(jnp.int32, marks.shape, 1)
    landing = [(marks == (lane + (at * BLOCK + 1)).astype(F32)).astype(F32) for at in range(table_rows // BLOCK)]
    landing = jnp.concatenate(landing, axis=1).astype(BF16)
    cells = [got[:, tile * capacity : (tile + 1) * capacity, :].reshape(n_ctx * capacity, BLOCK) for tile in range(tiles)]
    cells = jnp.concatenate(cells + [jnp.ones(marks.shape, BF16)], axis=1)
    summed_all = dot(landing, cells, 0, 0)
    for c in range(chunks):
        rows = rows_of(c)
        summed = summed_all[rows, : tiles * BLOCK]
        touched = jnp.concatenate([summed_all[rows, tiles * BLOCK :]] * tiles, axis=1) > 0.0
        old, m, v = [ref[rows, :] for ref in held]
        fresh_m = beta_first * m + (1.0 - beta_first) * summed
        fresh_v = beta_second * v + (1.0 - beta_second) * summed * summed
        update = learn_rate * (fresh_m / first_fix) / (jnp.sqrt(fresh_v / second_fix) + epsilon)
        made[0][rows, :] = jnp.where(touched, old - update, old)
        made[1][rows, :] = jnp.where(touched, fresh_m, m)
        made[2][rows, :] = jnp.where(touched, fresh_v, v)
        for move in stores[c]:
            move.start()
    masks = [0]
    for bit in ROUNDS:
        masks = masks + [mask ^ bit for mask in masks]
    senders = [jnp.bitwise_xor(me, mask) for mask in masks]
    width = (tiles + 1) * capacity
    mine_t = jnp.concatenate([got[s, width:, :] for s in senders], axis=1)
    other_t = jnp.concatenate([other[s] for s in senders], axis=1)
    both_t = jnp.concatenate([mine_t, other_t], axis=0)
    for move in loads:
        move.wait()
    both = dot(both_t, rows_held[...], 1, 0)
    grad[pl.ds(pl.multiple_of(core * share, share), share), :] = both[:share]
    grad[pl.ds(pl.multiple_of((1 - core) * share, share), share), :] = both[share:]
    for store in stores:
        for move in store:
            move.wait()


def dealt_device(
    queries,
    keys_values,
    attn_cot,
    event_rows,
    adapter,
    qkv_weight,
    starts,
    owners,
    slots,
    table,
    moment_m,
    moment_v,
):
    shape = jax.ShapeDtypeStruct
    n_ctx = lax.axis_size("ctx")
    rows_here = queries.shape[0]
    seq_len = rows_here * n_ctx
    head_cols = adapter.shape[1]
    width = event_rows.shape[1]
    capacity = max(2, 2 * rows_here // n_ctx)
    dealt = shape((2 * PART, BLOCK), BF16)
    *dealt, own_rows = pl.pallas_call(
        deal_body,
        out_shape=(dealt,) * 4 + (shape((rows_here, head_cols), BF16),),
        in_specs=[SMEM] + [pl.BlockSpec(memory_space=pltpu.HBM)] * 4,
        out_specs=(VMEM,) * 5,
        scratch_shapes=[pltpu.SemaphoreType.DMA((17,))],
        compiler_params=pltpu.CompilerParams(vmem_limit_bytes=12 * 1024 * 1024),
        name="deal",
    )(starts, queries, keys_values, attn_cot, event_rows)

    def exchange(sent, bit):
        return lax.ppermute(sent, "ctx", [(i, i ^ bit) for i in range(16)])

    zh_rows = exchange(own_rows, ROUNDS[0])
    both, by_zl, by_x = [exchange(part, bit) for part, bit in zip(dealt[:0:-1], (5, 4, 1))]
    zh_rows, both, by_zl, by_x = lax.optimization_barrier((zh_rows, both, by_zl, by_x))
    far_own, near_own, two = kernel_call(
        gather_body,
        (shape((4, PART, BLOCK), BF16),) * 2 + (shape((2 * rows_here, head_cols), BF16),),
        (dealt[0], own_rows, by_x, by_zl, both, zh_rows),
        "gather",
    )
    far_in = lax.ppermute(far_own, ("ctx", "head"), FAR_OUT)
    near_in = lax.ppermute(near_own, "ctx", ACROSS_Y)
    zl_rows, x_rows, y_rows = [exchange(two, bit) for bit in ROUNDS[1:]]
    scales = (1.0 / math.sqrt(HD), float(seq_len))
    side_scratch = [pltpu.VMEM((4 * BLOCK, BLOCK), BF16)] * 2
    near_sum = shape((8 * BLOCK, BLOCK), F32)
    cost = pl.CostEstimate(flops=10**9, bytes_accessed=2**20, transcendentals=0)
    near_1, near_2, far_sum = pl.pallas_call(
        functools.partial(attend_own_body, scales[0]),
        out_shape=(near_sum, near_sum, shape((2, 4 * BLOCK, BLOCK), F32)),
        in_specs=[VMEM] * 3,
        out_specs=(VMEM,) * 3,
        scratch_shapes=side_scratch,
        compiler_params=pltpu.CompilerParams(vmem_limit_bytes=12 * 1024 * 1024),
        cost_estimate=cost,
        name="attend_own",
    )(near_own, far_own, near_in)
    near_1, near_2, far_out = pl.pallas_call(
        functools.partial(attend_far_body, *scales),
        out_shape=(near_sum, near_sum, shape((4, 2, BLOCK, BLOCK), BF16)),
        in_specs=[VMEM] * 5,
        out_specs=(VMEM,) * 3,
        scratch_shapes=side_scratch,
        input_output_aliases={3: 0, 4: 1},
        compiler_params=pltpu.CompilerParams(vmem_limit_bytes=12 * 1024 * 1024),
        cost_estimate=cost,
        name="attend_far",
    )(near_own, near_in, far_in, near_1, near_2)
    near_1, near_2, far_out, zl_rows, x_rows, y_rows = lax.optimization_barrier(
        (near_1, near_2, far_out, zl_rows, x_rows, y_rows)
    )
    near_out = kernel_call(
        functools.partial(near_body, *scales), shape((4, 2, BLOCK, BLOCK), BF16), (near_1, near_2), "near"
    )
    zl_x_rows = exchange(zl_rows, ROUNDS[2])
    zl_y_rows = exchange(zl_rows, ROUNDS[3])
    far_back = lax.ppermute(far_out, ("ctx", "head"), FAR_BACK)
    near_back = lax.ppermute(near_out, "ctx", ACROSS_Y)
    sums = (far_back, near_back, near_1, near_2, far_sum)
    part = shape((3, BLOCK, BLOCK), BF16)
    (both,) = kernel_call(functools.partial(merge_body, (3,), *scales), (part,), sums, "merge_both")
    both, *sums = lax.optimization_barrier((both, *sums))
    own, *parts = kernel_call(functools.partial(merge_body, (0, 1, 2), *scales), (part,) * 3, sums, "merge")
    both, *parts, zl_x_rows, zl_y_rows = lax.optimization_barrier((both, *parts, zl_x_rows, zl_y_rows))
    x_y_rows, zl_x_y_rows = [exchange(rows, ROUNDS[3]) for rows in (x_rows, zl_x_rows)]
    both, by_zl, by_x = [exchange(part, bit) for part, bit in zip((both, parts[1], parts[0]), (5, 4, 1))]
    both, by_zl, by_x, x_y_rows = lax.optimization_barrier((both, by_zl, by_x, x_y_rows))
    partial, sent = pl.pallas_call(
        project_body,
        out_shape=(shape((rows_here, width), F32), shape((rows_here, width), BF16)),
        in_specs=[VMEM] * 5,
        out_specs=(VMEM, VMEM),
        scratch_shapes=[pltpu.VMEM((3, rows_here, queries.shape[1]), BF16)],
        compiler_params=pltpu.CompilerParams(vmem_limit_bytes=12 * 1024 * 1024),
        name="project",
    )(both, by_zl, by_x, own, qkv_weight)
    sent, owners, slots = lax.optimization_barrier((sent, owners, slots))
    placing, marks = kernel_call(
        place_body,
        (shape((rows_here, n_ctx * capacity), BF16), shape((rows_here, BLOCK), BF16)),
        (owners.reshape(1, rows_here), slots.reshape(1, rows_here)),
        "place",
    )
    other = lax.ppermute(sent, "head", SWAP)
    other, zl_x_y_rows = lax.optimization_barrier((other, zl_x_y_rows))
    share = width // n_ctx // 2
    packed_rows = capacity * (head_cols // BLOCK + 1)
    packed = pl.pallas_call(
        pack_body,
        out_shape=shape((n_ctx, packed_rows + share, BLOCK), BF16),
        in_specs=[VMEM] * 5,
        out_specs=VMEM,
        scratch_shapes=[pltpu.VMEM((rows_here, width), F32), pltpu.VMEM((width, rows_here), BF16)],
        compiler_params=pltpu.CompilerParams(vmem_limit_bytes=12 * 1024 * 1024),
        name="pack",
    )(partial, other, adapter, placing, marks)
    got = lax.all_to_all(packed, "ctx", 0, 0, tiled=True)
    other_share = lax.ppermute(got[:, packed_rows:], "head", SWAP)
    held = shape(table.shape, F32)
    pieces = (two, zl_rows, x_rows, zl_x_rows, y_rows, zl_y_rows, x_y_rows, zl_x_y_rows)
    return pl.pallas_call(
        finish_body,
        out_shape=(shape((width // n_ctx, head_cols), F32), held, held, held),
        in_specs=[VMEM] * 2 + [pl.BlockSpec(memory_space=pl.ANY)] * len(pieces) + [VMEM] * 3,
        out_specs=(VMEM,) + (pl.BlockSpec(memory_space=pl.ANY),) * 3,
        scratch_shapes=[pltpu.VMEM(table.shape, F32)] * 3
        + [
            pltpu.VMEM((n_ctx * rows_here, head_cols), BF16),
            pltpu.SemaphoreType.DMA((len(pieces),)),
            pltpu.SemaphoreType.DMA((3, 4)),
        ],
        compiler_params=pltpu.CompilerParams(vmem_limit_bytes=12 * 1024 * 1024),
        name="finish",
    )(got, other_share, *pieces, table, moment_m, moment_v)


def per_device(*arrays):
    rows_here, cols_here = arrays[0].shape
    fits = lax.axis_size("ctx") == 16 and lax.axis_size("head") == 2
    if fits and rows_here == BLOCK and cols_here == 4 * HD and arrays[9].shape[0] == 2 * BLOCK:
        return dealt_device(*arrays)
    return plain_device(*arrays)


def solution(mesh):
    placed = (
        P("ctx", "head"),
        P(None, "ctx", "head"),
        P("ctx", "head"),
        P("ctx", None),
        P(None, "head"),
        P(None, None, "head"),
        P("ctx"),
        P("ctx", None),
        P("ctx"),
        P("ctx", "head"),
        P("ctx", "head"),
        P("ctx", "head"),
    )
    return jax.shard_map(
        per_device,
        mesh=mesh,
        in_specs=placed,
        out_specs=(P("ctx", "head"), P("ctx", "head"), P("ctx", "head"), P("ctx", "head")),
        check_vma=False,
    )
```

```python
import functools
import math

import jax
import jax.numpy as jnp
from jax import lax
from jax.experimental import pallas as pl
from jax.experimental.pallas import tpu as pltpu
from jax.sharding import PartitionSpec as P

HD = 128
QBLK = 128


beta_first = 0.9
beta_second = 0.999
learn_rate = 0.01
epsilon = 1e-08
first_fix = 1.0 - beta_first**10.0
second_fix = 1.0 - beta_second**10.0


def adam_rows(summed, touched, table, moment_m, moment_v):
    fresh_m = beta_first * moment_m + (1.0 - beta_first) * summed
    fresh_v = beta_second * moment_v + (1.0 - beta_second) * summed * summed
    update = learn_rate * (fresh_m / first_fix) / (jnp.sqrt(fresh_v / second_fix) + epsilon)
    keep = touched[:, None]
    return (
        jnp.where(keep, table - update, table),
        jnp.where(keep, fresh_m, moment_m),
        jnp.where(keep, fresh_v, moment_v),
    )


def pair_scores(query_part, key_part, query_places, query_lower, key_places):
    scale = 1.0 / math.sqrt(HD)
    scores = (
        jnp.einsum("ihd,jhd->hij", query_part, key_part, preferred_element_type=jnp.float32) * scale
    )
    seen = (key_places[None, :] <= query_places[:, None]) & (
        key_places[None, :] >= query_lower[:, None]
    )
    squash = jax.nn.sigmoid(scores)
    return (scores, squash, seen[None])


def score_grads(scores, squash, seen, cotangent_piece, value_part, seq_len):
    dprod = jnp.einsum(
        "ihd,jhd->hij", cotangent_piece, value_part, preferred_element_type=jnp.float32
    )
    return jnp.where(seen, dprod * squash * (1.0 + scores * (1.0 - squash)) / seq_len, 0.0).astype(
        jnp.bfloat16
    )


def score_weights(scores, squash, seen, seq_len):
    return jnp.where(seen, scores * squash / seq_len, 0.0).astype(jnp.bfloat16)


def over_blocks(total, fn, carry):
    sub = math.gcd(total, 1024)
    return lax.fori_loop(
        0, total // sub, lambda index, inner_loop: fn(inner_loop, index * sub), carry
    )


def plain_device(
    queries,
    keys_values,
    attn_cot,
    event_rows,
    adapter,
    qkv_weight,
    starts,
    owners,
    slots,
    table,
    moment_m,
    moment_v,
):
    rows_here = queries.shape[0]
    feature_cols = queries.shape[1]
    heads_here = feature_cols // HD
    n_ctx = lax.axis_size("ctx")
    seq_len = rows_here * n_ctx
    scale = 1.0 / math.sqrt(HD)
    myself = lax.axis_index("ctx")
    local_first = myself * rows_here
    local_places = local_first + jnp.arange(rows_here, dtype=jnp.int32)
    lower = jnp.repeat(starts, QBLK, total_repeat_length=rows_here)
    least_lower = jnp.min(lower)
    query_heads = queries.reshape(rows_here, heads_here, HD)
    cot_heads = attn_cot.reshape(rows_here, heads_here, HD)
    key_heads = keys_values[0].reshape(rows_here, heads_here, HD)
    value_heads = keys_values[1].reshape(rows_here, heads_here, HD)
    zeros = jnp.zeros((rows_here, heads_here, HD), jnp.float32)
    piece = lax.all_gather(keys_values, "ctx", axis=1, tiled=True)

    def key_one_block(inner_loop, offset):
        sub = math.gcd(piece.shape[1], 1024)
        key_first = offset
        live = (key_first <= local_first + rows_here - 1) & (key_first + sub - 1 >= least_lower)

        def key_working(values):
            part = lax.dynamic_slice_in_dim(piece, offset, sub, 1)
            key_part = part[0].reshape(sub, heads_here, HD)
            value_part = part[1].reshape(sub, heads_here, HD)
            key_places = key_first + jnp.arange(sub, dtype=jnp.int32)
            scores, squash, seen = pair_scores(
                query_heads, key_part, local_places, lower, key_places
            )
            dscore = score_grads(scores, squash, seen, cot_heads, value_part, seq_len)
            return values + jnp.einsum(
                "hij,jhd->ihd", dscore, key_part, preferred_element_type=jnp.float32
            )

        return lax.cond(live, key_working, lambda values: values, inner_loop)

    query_grad = over_blocks(piece.shape[1], key_one_block, zeros)
    query_piece = (
        lax.all_gather(queries, "ctx", axis=0, tiled=True),
        lax.all_gather(attn_cot, "ctx", axis=0, tiled=True),
        lax.all_gather(lower, "ctx", axis=0, tiled=True),
    )

    def query_one_block(inner_loop, offset):
        sub = math.gcd(query_piece[0].shape[0], 1024)
        query_first = offset
        query_lower = lax.dynamic_slice_in_dim(query_piece[2], offset, sub, 0)
        live = (local_first <= query_first + sub - 1) & (
            local_first + rows_here - 1 >= jnp.min(query_lower)
        )

        def query_working(values):
            query_part = lax.dynamic_slice_in_dim(query_piece[0], offset, sub, 0).reshape(
                sub, heads_here, HD
            )
            cotangent_piece = lax.dynamic_slice_in_dim(query_piece[1], offset, sub, 0).reshape(
                sub, heads_here, HD
            )
            query_places = query_first + jnp.arange(sub, dtype=jnp.int32)
            scores, squash, seen = pair_scores(
                query_part, key_heads, query_places, query_lower, local_places
            )
            weights = score_weights(scores, squash, seen, seq_len)
            dscore = score_grads(scores, squash, seen, cotangent_piece, value_heads, seq_len)
            key_add = jnp.einsum(
                "hij,ihd->jhd", dscore, query_part, preferred_element_type=jnp.float32
            )
            value_add = jnp.einsum(
                "hij,ihd->jhd", weights, cotangent_piece, preferred_element_type=jnp.float32
            )
            return (values[0] + key_add, values[1] + value_add)

        return lax.cond(live, query_working, lambda values: values, inner_loop)

    key_grad, value_grad = over_blocks(query_piece[0].shape[0], query_one_block, (zeros, zeros))
    head_grads = (
        jnp.stack([query_grad * scale, key_grad * scale, value_grad])
        .astype(jnp.bfloat16)
        .reshape(3, rows_here, feature_cols)
    )
    partial_grad = jnp.einsum(
        "mtc,mdc->td", head_grads, qkv_weight, preferred_element_type=jnp.float32
    )
    head_cols = adapter.shape[1]
    first_col = lax.axis_index("head") * head_cols
    layer_grad = lax.psum(partial_grad.astype(jnp.bfloat16), "head").astype(jnp.float32)
    layer_grad_b = layer_grad.astype(jnp.bfloat16)
    own_grad = lax.dynamic_slice_in_dim(layer_grad, first_col, head_cols, 1)
    row_grads = own_grad + jnp.dot(layer_grad_b, adapter, preferred_element_type=jnp.float32)
    own_rows = lax.dynamic_slice_in_dim(event_rows, first_col, head_cols, 1)
    adapter_grad = lax.psum_scatter(
        lax.dot_general(
            layer_grad_b, own_rows, (((0,), (0,)), ((), ())), preferred_element_type=jnp.float32
        ),
        "ctx",
        scatter_dimension=0,
        tiled=True,
    )
    capacity = max(2, 2 * rows_here // n_ctx)
    target = owners[:, 0]
    onehot = (target[:, None] == jnp.arange(n_ctx, dtype=jnp.int32)[None, :]).astype(jnp.int32)
    prior_blocks = jnp.cumsum(onehot, axis=0) - onehot
    ranking = jnp.sum(prior_blocks * onehot, axis=1)
    cell_index = target * capacity + ranking
    placing = cell_index[:, None] == jnp.arange(n_ctx * capacity, dtype=jnp.int32)[None, :]
    send_rows = lax.dot_general(
        placing.astype(jnp.float32),
        row_grads,
        (((0,), (0,)), ((), ())),
        precision=lax.Precision.HIGHEST,
    ).reshape(n_ctx, capacity, head_cols)
    send_slots = (jnp.sum(jnp.where(placing, slots[:, None] + 1, 0), axis=0) - 1).reshape(
        n_ctx, capacity
    )
    got_rows, got_slots = (
        lax.all_to_all(
            send_rows.astype(jnp.bfloat16), "ctx", split_axis=0, concat_axis=0, tiled=True
        ).astype(send_rows.dtype),
        lax.all_to_all(send_slots, "ctx", split_axis=0, concat_axis=0, tiled=True),
    )
    table_rows = table.shape[0]
    landing = got_slots.reshape(-1)[None, :] == jnp.arange(table_rows, dtype=jnp.int32)[:, None]
    summed = jnp.dot(
        landing.astype(jnp.float32),
        got_rows.reshape(n_ctx * capacity, head_cols),
        precision=lax.Precision.HIGHEST,
    )
    touched = jnp.sum(landing.astype(jnp.int32), axis=1) > 0
    new_table, new_m, new_v = adam_rows(summed, touched, table, moment_m, moment_v)
    return (adapter_grad, new_table, new_m, new_v)


BLOCK = 128
PAIR = 2 * BLOCK
META = 16
PART = PAIR + META
FAR_PART = PART + META
ACROSS_Y = [(i, i ^ 2) for i in range(16)]
FAR_OUT = [(i * 2, (i + 8) * 2) for i in range(8)] + [((i + 8) * 2 + 1, i * 2 + 1) for i in range(8)]
FAR_BACK = [(b, a) for a, b in FAR_OUT]
SWAP = [(0, 1), (1, 0)]
ROUNDS = (8, 4, 1, 2)
F32 = jnp.float32
BF16 = jnp.bfloat16
VMEM = pl.BlockSpec(memory_space=pltpu.VMEM)
SMEM = pl.BlockSpec(memory_space=pltpu.SMEM)


def dot(a, b, axis_a, axis_b):
    return lax.dot_general(a, b, (((axis_a,), (axis_b,)), ((), ())), preferred_element_type=F32)


def spot_of(me):
    return me // 4 % 2 * 2 + me % 2


def kernel_call(body, out_shape, operands, name, flops=0, in_bytes=0):
    specs = [SMEM if o.dtype == jnp.int32 and o.ndim == 1 else VMEM for o in operands]
    return pl.pallas_call(
        body,
        out_shape=out_shape,
        in_specs=specs,
        out_specs=jax.tree.map(lambda _: VMEM, out_shape),
        compiler_params=pltpu.CompilerParams(vmem_limit_bytes=12 * 1024 * 1024),
        cost_estimate=pl.CostEstimate(flops=flops, bytes_accessed=in_bytes, transcendentals=0),
        name=name,
    )(*operands)


def deal_body(starts, queries, keys_values, cot, rows, own, by_x, by_zl, by_both, held_rows, sems):
    core, me = lax.axis_index("head"), lax.axis_index("ctx")
    outs = (own, by_x, by_zl, by_both)
    start = starts[0]
    row = lax.broadcasted_iota(jnp.int32, (META, BLOCK), 0)
    meta = jnp.where(row == 0, start // BLOCK, jnp.where(row == 1, start % BLOCK, 0)).astype(F32).astype(BF16)
    cols = held_rows.shape[1]

    def copies(near, far, half):
        moves = []
        for flip, out in enumerate(outs):
            head = jnp.bitwise_xor(spot_of(me), flip)
            lanes = pl.ds(pl.multiple_of(head * BLOCK, BLOCK), BLOCK)
            for base, pair in ((0, near), (PART, far)):
                for at, source in enumerate(pair):
                    moves.append((source.at[:, lanes], out.at[base + at * BLOCK : base + (at + 1) * BLOCK, :]))
        moves.append((rows.at[:, half * cols : (half + 1) * cols], held_rows.at[:BLOCK, :]))
        moves = [pltpu.make_async_copy(a, b, sems.at[k]) for k, (a, b) in enumerate(moves)]
        for move in moves:
            move.start()
        held_rows[BLOCK:, :] = jnp.zeros((META, cols), BF16)
        for out in outs:
            out[PAIR:PART, :] = meta
            out[PART + PAIR : PART + PART, :] = meta
            out[PART + PART :, :] = jnp.zeros((META, BLOCK), BF16)
        for move in moves:
            move.wait()

    asks = (queries, cot)
    gives = (keys_values.at[0], keys_values.at[1])

    @pl.when(core == 0)
    def _():
        copies(asks, gives, 0)

    @pl.when(core == 1)
    def _():
        copies(gives, asks, 1)


def gather_body(own, rows_1, by_x, by_zl, by_both, rows_2, far, near, two):
    for flip, part in enumerate((own, by_x, by_zl, by_both)):
        near[flip] = part[:PART, :]
        far[flip] = part[PART:, :]
    count = two.shape[0] // 2
    two[:count, :] = rows_1[:count, :]
    two[count:, :] = rows_2[:count, :]


def lower_of(meta):
    meta = meta.astype(F32)
    return (meta[0:1] * BLOCK + meta[1:2]).astype(jnp.int32)


def attend(scale, role_q, crossing, nears, far, far_1, far_2, near_1_sum, near_2_sum, put_far_1, put_far_2):
    me = lax.axis_index("ctx")
    zh, y = me // 8, me // 2 % 2
    spots = [jnp.bitwise_xor(spot_of(me), flip) for flip in range(4)]
    places = [spot // 2 * 4 + spot % 2 for spot in spots]
    lane = lax.broadcasted_iota(jnp.int32, (1, BLOCK), 1)
    row_in = lax.broadcasted_iota(jnp.int32, (BLOCK, 4 * BLOCK), 0)
    never = 1 << 20
    far_zh = 1 - zh if crossing else zh
    place = jnp.concatenate([lane + (far_zh * 8 + y * 2 + s) * BLOCK for s in places], axis=1)
    base_1, base_2 = far_1[...], far_2[...]
    if not role_q:
        low = jnp.concatenate([lower_of(far[s, PAIR:PART, :]) for s in range(4)], axis=1)
    dscores, weights, firsts, seconds = [], [], [], []
    for chunk in range(4):
        rows = slice(chunk * PAIR, (chunk + 1) * PAIR)
        near_ref, near_y = nears[chunk // 2], (y, 1 - y)[chunk // 2]
        pair = (chunk % 2 * 2, chunk % 2 * 2 + 1)
        first = jnp.concatenate([near_ref[s, :BLOCK, :] for s in pair], axis=0)
        second = jnp.concatenate([near_ref[s, BLOCK:PAIR, :] for s in pair], axis=0)
        half = dot(first, base_1, 1, 1) * (0.5 * scale)
        dprod = dot(second, base_2, 1, 1)
        seen = []
        for s in pair:
            start = (zh * 8 + near_y * 2 + places[s]) * BLOCK
            if role_q:
                low = jnp.concatenate([lower_of(near_ref[s, PAIR:PART, :])] * 4, axis=1)
                seen.append(row_in >= jnp.where(place >= low, place - start, never))
            else:
                seen.append((row_in >= low - start) & (row_in <= place - start))
        seen = jnp.concatenate(seen, axis=0)
        tanh = jnp.tanh(half)
        twice = 1.0 + tanh
        weight = half * twice
        dscore = (dprod * twice) * (1.0 + half * (1.0 - tanh))
        weight = jnp.where(seen, weight, 0.0).astype(BF16)
        dscore = jnp.where(seen, dscore, 0.0).astype(BF16)
        grad_1 = dot(dscore, base_1, 1, 0)
        near_1_sum[rows, :] = near_1_sum[rows, :] + grad_1 if crossing else grad_1
        if not role_q:
            grad_2 = dot(weight, base_2, 1, 0)
            near_2_sum[rows, :] = near_2_sum[rows, :] + grad_2 if crossing else grad_2
        dscores.append(dscore)
        weights.append(weight)
        firsts.append(first)
        seconds.append(second)
    put_far_1(dot(jnp.concatenate(dscores, axis=0), jnp.concatenate(firsts, axis=0), 0, 0))
    if role_q:
        put_far_2(dot(jnp.concatenate(weights, axis=0), jnp.concatenate(seconds, axis=0), 0, 0))


def gather_far(far, far_1, far_2):
    for spot in range(4):
        rows = slice(spot * BLOCK, (spot + 1) * BLOCK)
        far_1[rows, :] = far[spot, :BLOCK, :]
        far_2[rows, :] = far[spot, BLOCK:PAIR, :]


def attend_own_body(scale, near_own, far_own, near_in, near_1_sum, near_2_sum, far_sum, far_1, far_2):
    gather_far(far_own, far_1, far_2)
    core = lax.axis_index("head")

    def put(at):
        def store(value):
            far_sum[at] = value

        return store

    rest = ((near_own, near_in), far_own, far_1, far_2, near_1_sum, near_2_sum, put(0), put(1))

    @pl.when(core == 0)
    def _():
        near_2_sum[...] = jnp.zeros_like(near_2_sum)
        attend(scale, True, False, *rest)

    @pl.when(core == 1)
    def _():
        far_sum[1] = jnp.zeros((4 * BLOCK, BLOCK), F32)
        attend(scale, False, False, *rest)


def attend_far_body(scale, seq_len, near_own, near_in, far_in, _1, _2, near_1_sum, near_2_sum, far_out, far_1, far_2):
    core, zh = lax.axis_index("head"), lax.axis_index("ctx") // 8
    far_out[...] = jnp.zeros_like(far_out)

    def put(at, factor):
        def store(value):
            for spot in range(4):
                far_out[spot, at * BLOCK : (at + 1) * BLOCK, :] = (value[spot * BLOCK : (spot + 1) * BLOCK] * factor).astype(BF16)

        return store

    puts = (put(0, scale * 0.5 / seq_len), put(1, 1.0 / seq_len))
    rest = ((near_own, near_in), far_in, far_1, far_2, near_1_sum, near_2_sum, *puts)

    @pl.when((core == 0) & (zh == 1))
    def _():
        gather_far(far_in, far_1, far_2)
        attend(scale, True, True, *rest)

    @pl.when((core == 1) & (zh == 0))
    def _():
        gather_far(far_in, far_1, far_2)
        attend(scale, False, True, *rest)


def near_body(scale, seq_len, near_1_sum, near_2_sum, out):
    for spot in range(4):
        rows = slice((4 + spot) * BLOCK, (5 + spot) * BLOCK)
        out[spot, 0] = (near_1_sum[rows, :] * (scale * 0.5 / seq_len)).astype(BF16)
        out[spot, 1] = (near_2_sum[rows, :] * (1.0 / seq_len)).astype(BF16)


def project_body(by_both, by_zl, by_x, own, weight, partial, sent, held):
    core, me = lax.axis_index("head"), lax.axis_index("ctx")
    for flip, part in enumerate((own, by_x, by_zl, by_both)):
        head = jnp.bitwise_xor(spot_of(me), flip)
        for slot in range(3):
            held[slot, :, pl.ds(pl.multiple_of(head * BLOCK, BLOCK), BLOCK)] = part[slot]
    total = dot(held[1], weight[2], 1, 1)
    total = total + dot(held[0], weight[core], 1, 1)
    total = total + dot(held[2], weight[1 - core], 1, 1)
    partial[...] = total
    sent[...] = total.astype(BF16)


def pack_body(own, other, adapter, placing, slots, out, grad, turned):
    core = lax.axis_index("head")
    n_ctx = out.shape[0]
    head_cols = adapter.shape[1]
    capacity = placing.shape[1] // n_ctx
    tiles = head_cols // BLOCK
    share = own.shape[1] // n_ctx // 2
    total = own[...] + other[...].astype(F32)
    grad[...] = total
    rounded = total.astype(BF16)
    turned[...] = jnp.transpose(rounded)
    rows = grad[:, pl.ds(pl.multiple_of(core * head_cols, head_cols), head_cols)]
    rows = rows + dot(rounded, adapter[...], 1, 0)
    rows = jnp.concatenate([rows.astype(BF16), slots[...]], axis=1)
    cells = dot(placing[...], rows, 0, 0).astype(BF16)
    for p in range(n_ctx):
        for tile in range(tiles + 1):
            out[p, tile * capacity : (tile + 1) * capacity, :] = cells[
                p * capacity : (p + 1) * capacity, tile * BLOCK : (tile + 1) * BLOCK
            ]
        first = pl.multiple_of(p * 2 * share + core * share, share)
        out[p, (tiles + 1) * capacity :, :] = turned[pl.ds(first, share), :]


def place_body(owners, slots, placing, marks):
    count = owners.shape[1]
    capacity = placing.shape[1] // 16
    lane = lax.broadcasted_iota(jnp.int32, (count, BLOCK), 1)
    row = lax.broadcasted_iota(jnp.int32, (count, BLOCK), 0)
    owner_row = jnp.broadcast_to(owners[...].astype(F32), (count, BLOCK))
    owner = jnp.transpose(owner_row)
    same = jnp.where((owner == owner_row) & (lane < row), 1.0, 0.0)
    ranking = jnp.sum(same, axis=1, keepdims=True)
    cell = owner * capacity + ranking
    for tile in range(placing.shape[1] // BLOCK):
        hit = cell == (lane + tile * BLOCK).astype(F32)
        placing[:, tile * BLOCK : (tile + 1) * BLOCK] = hit.astype(F32).astype(BF16)
    mark = jnp.broadcast_to(slots[...] + 1, (count, BLOCK)).astype(F32)
    marks[...] = jnp.transpose(mark).astype(BF16)


def merge_body(flips, scale, seq_len, far, near, near_1_sum, near_2_sum, far_sum, *outs):
    grad_scale, weight_scale = scale * 0.5 / seq_len, 1.0 / seq_len
    for flip, out in zip(flips, outs):
        rows = slice(flip * BLOCK, (flip + 1) * BLOCK)
        out[0] = (near_1_sum[rows, :] * grad_scale + near[flip, 0].astype(F32)).astype(BF16)
        both = (near_2_sum[rows, :] + far_sum[1, rows, :]) * weight_scale
        out[1] = (both + near[flip, 1].astype(F32) + far[flip, BLOCK:PAIR, :].astype(F32)).astype(BF16)
        out[2] = (far_sum[0, rows, :] * grad_scale + far[flip, :BLOCK, :].astype(F32)).astype(BF16)


def finish_body(got, other, *refs):
    pieces, held, grad, targets = refs[:8], refs[8:11], refs[11], refs[12:15]
    made, rows_held, in_sems, out_sems = refs[15:18], refs[18], refs[19], refs[20]
    chunks = out_sems.shape[1]
    span = held[0].shape[0] // chunks

    def rows_of(c):
        return slice(c * span, (c + 1) * span)

    stores = [
        [pltpu.make_async_copy(a.at[rows_of(c), :], b.at[rows_of(c), :], out_sems.at[k, c]) for k, (a, b) in enumerate(zip(made, targets))]
        for c in range(chunks)
    ]
    part = rows_held.shape[0] // 8
    loads = [pltpu.make_async_copy(p, rows_held.at[k * part : (k + 1) * part, :], in_sems.at[k]) for k, p in enumerate(pieces)]
    for move in loads:
        move.start()
    core, me = lax.axis_index("head"), lax.axis_index("ctx")
    share = other.shape[1]
    tiles = held[0].shape[1] // BLOCK
    table_rows = held[0].shape[0]
    n_ctx = got.shape[0]
    capacity = (got.shape[1] - share) // (tiles + 1)
    marks = got[:, tiles * capacity : (tiles + 1) * capacity, :].reshape(n_ctx * capacity, BLOCK).astype(F32)
    lane = lax.broadcasted_iota(jnp.int32, marks.shape, 1)
    landing = [(marks == (lane + (at * BLOCK + 1)).astype(F32)).astype(F32) for at in range(table_rows // BLOCK)]
    landing = jnp.concatenate(landing, axis=1).astype(BF16)
    cells = [got[:, tile * capacity : (tile + 1) * capacity, :].reshape(n_ctx * capacity, BLOCK) for tile in range(tiles)]
    cells = jnp.concatenate(cells + [jnp.ones(marks.shape, BF16)], axis=1)
    summed_all = dot(landing, cells, 0, 0)
    for c in range(chunks):
        rows = rows_of(c)
        summed = summed_all[rows, : tiles * BLOCK]
        touched = jnp.concatenate([summed_all[rows, tiles * BLOCK :]] * tiles, axis=1) > 0.0
        old, m, v = [ref[rows, :] for ref in held]
        fresh_m = beta_first * m + (1.0 - beta_first) * summed
        fresh_v = beta_second * v + (1.0 - beta_second) * summed * summed
        update = learn_rate * (fresh_m / first_fix) / (jnp.sqrt(fresh_v / second_fix) + epsilon)
        made[0][rows, :] = jnp.where(touched, old - update, old)
        made[1][rows, :] = jnp.where(touched, fresh_m, m)
        made[2][rows, :] = jnp.where(touched, fresh_v, v)
        for move in stores[c]:
            move.start()
    masks = [0]
    for bit in ROUNDS:
        masks = masks + [mask ^ bit for mask in masks]
    senders = [jnp.bitwise_xor(me, mask) for mask in masks]
    width = (tiles + 1) * capacity
    mine_t = jnp.concatenate([got[s, width:, :] for s in senders], axis=1)
    other_t = jnp.concatenate([other[s] for s in senders], axis=1)
    both_t = jnp.concatenate([mine_t, other_t], axis=0)
    for move in loads:
        move.wait()
    both = dot(both_t, rows_held[...], 1, 0)
    grad[pl.ds(pl.multiple_of(core * share, share), share), :] = both[:share]
    grad[pl.ds(pl.multiple_of((1 - core) * share, share), share), :] = both[share:]
    for store in stores:
        for move in store:
            move.wait()


def dealt_device(
    queries,
    keys_values,
    attn_cot,
    event_rows,
    adapter,
    qkv_weight,
    starts,
    owners,
    slots,
    table,
    moment_m,
    moment_v,
):
    shape = jax.ShapeDtypeStruct
    n_ctx = lax.axis_size("ctx")
    rows_here = queries.shape[0]
    seq_len = rows_here * n_ctx
    head_cols = adapter.shape[1]
    width = event_rows.shape[1]
    capacity = max(2, 2 * rows_here // n_ctx)
    dealt = shape((PART + FAR_PART, BLOCK), BF16)
    *dealt, own_rows = pl.pallas_call(
        deal_body,
        out_shape=(dealt,) * 4 + (shape((rows_here + META, head_cols), BF16),),
        in_specs=[SMEM] + [pl.BlockSpec(memory_space=pltpu.HBM)] * 4,
        out_specs=(VMEM,) * 5,
        scratch_shapes=[pltpu.SemaphoreType.DMA((17,))],
        compiler_params=pltpu.CompilerParams(vmem_limit_bytes=12 * 1024 * 1024),
        name="deal",
    )(starts, queries, keys_values, attn_cot, event_rows)

    def exchange(sent, bit):
        return lax.ppermute(sent, "ctx", [(i, i ^ bit) for i in range(16)])

    zh_rows = exchange(own_rows, ROUNDS[0])
    both, by_zl, by_x = [exchange(part, bit) for part, bit in zip(dealt[:0:-1], (5, 4, 1))]
    zh_rows, both, by_zl, by_x = lax.optimization_barrier((zh_rows, both, by_zl, by_x))
    far_own, near_own, two = kernel_call(
        gather_body,
        (shape((4, FAR_PART, BLOCK), BF16), shape((4, PART, BLOCK), BF16), shape((2 * rows_here, head_cols), BF16)),
        (dealt[0], own_rows, by_x, by_zl, both, zh_rows),
        "gather",
    )
    far_in = lax.ppermute(far_own, ("ctx", "head"), FAR_OUT)
    near_in = lax.ppermute(near_own, "ctx", ACROSS_Y)
    zl_rows, x_rows, y_rows = [exchange(two, bit) for bit in ROUNDS[1:]]
    scales = (1.0 / math.sqrt(HD), float(seq_len))
    side_scratch = [pltpu.VMEM((4 * BLOCK, BLOCK), BF16)] * 2
    near_sum = shape((8 * BLOCK, BLOCK), F32)
    cost = pl.CostEstimate(flops=10**9, bytes_accessed=2**20, transcendentals=0)
    near_1, near_2, far_sum = pl.pallas_call(
        functools.partial(attend_own_body, scales[0]),
        out_shape=(near_sum, near_sum, shape((2, 4 * BLOCK, BLOCK), F32)),
        in_specs=[VMEM] * 3,
        out_specs=(VMEM,) * 3,
        scratch_shapes=side_scratch,
        compiler_params=pltpu.CompilerParams(vmem_limit_bytes=12 * 1024 * 1024),
        cost_estimate=cost,
        name="attend_own",
    )(near_own, far_own, near_in)
    near_1, near_2, far_out = pl.pallas_call(
        functools.partial(attend_far_body, *scales),
        out_shape=(near_sum, near_sum, shape((4, PART, BLOCK), BF16)),
        in_specs=[VMEM] * 5,
        out_specs=(VMEM,) * 3,
        scratch_shapes=side_scratch,
        input_output_aliases={3: 0, 4: 1},
        compiler_params=pltpu.CompilerParams(vmem_limit_bytes=12 * 1024 * 1024),
        cost_estimate=cost,
        name="attend_far",
    )(near_own, near_in, far_in, near_1, near_2)
    near_1, near_2, far_out, zl_rows, x_rows, y_rows = lax.optimization_barrier(
        (near_1, near_2, far_out, zl_rows, x_rows, y_rows)
    )
    near_out = kernel_call(
        functools.partial(near_body, *scales), shape((4, 2, BLOCK, BLOCK), BF16), (near_1, near_2), "near"
    )
    zl_x_rows = exchange(zl_rows, ROUNDS[2])
    zl_y_rows = exchange(zl_rows, ROUNDS[3])
    far_back = lax.ppermute(far_out, ("ctx", "head"), FAR_BACK)
    near_back = lax.ppermute(near_out, "ctx", ACROSS_Y)
    sums = (far_back, near_back, near_1, near_2, far_sum)
    part = shape((3, BLOCK, BLOCK), BF16)
    (both,) = kernel_call(functools.partial(merge_body, (3,), *scales), (part,), sums, "merge_both")
    both, *sums = lax.optimization_barrier((both, *sums))
    own, *parts = kernel_call(functools.partial(merge_body, (0, 1, 2), *scales), (part,) * 3, sums, "merge")
    both, *parts, zl_x_rows = lax.optimization_barrier((both, *parts, zl_x_rows))
    x_y_rows, zl_x_y_rows = exchange(y_rows, ROUNDS[2]), exchange(zl_x_rows, ROUNDS[3])
    both, by_zl, by_x = [exchange(part, bit) for part, bit in zip((both, parts[1], parts[0]), (5, 4, 1))]
    both, by_zl, by_x, zl_y_rows, zl_x_y_rows = lax.optimization_barrier((both, by_zl, by_x, zl_y_rows, zl_x_y_rows))
    partial, sent = pl.pallas_call(
        project_body,
        out_shape=(shape((rows_here, width), F32), shape((rows_here, width), BF16)),
        in_specs=[VMEM] * 5,
        out_specs=(VMEM, VMEM),
        scratch_shapes=[pltpu.VMEM((3, rows_here, queries.shape[1]), BF16)],
        compiler_params=pltpu.CompilerParams(vmem_limit_bytes=12 * 1024 * 1024),
        name="project",
    )(both, by_zl, by_x, own, qkv_weight)
    sent, owners, slots = lax.optimization_barrier((sent, owners, slots))
    placing, marks = kernel_call(
        place_body,
        (shape((rows_here, n_ctx * capacity), BF16), shape((rows_here, BLOCK), BF16)),
        (owners.reshape(1, rows_here), slots.reshape(1, rows_here)),
        "place",
    )
    other = lax.ppermute(sent, "head", SWAP)
    other, x_y_rows = lax.optimization_barrier((other, x_y_rows))
    share = width // n_ctx // 2
    packed_rows = capacity * (head_cols // BLOCK + 1)
    packed = pl.pallas_call(
        pack_body,
        out_shape=shape((n_ctx, packed_rows + share, BLOCK), BF16),
        in_specs=[VMEM] * 5,
        out_specs=VMEM,
        scratch_shapes=[pltpu.VMEM((rows_here, width), F32), pltpu.VMEM((width, rows_here), BF16)],
        compiler_params=pltpu.CompilerParams(vmem_limit_bytes=12 * 1024 * 1024),
        name="pack",
    )(partial, other, adapter, placing, marks)
    got = lax.all_to_all(packed, "ctx", 0, 0, tiled=True)
    other_share = lax.ppermute(got[:, packed_rows:], "head", SWAP)
    held = shape(table.shape, F32)
    pieces = (two, zl_rows, x_rows, zl_x_rows, y_rows, zl_y_rows, x_y_rows, zl_x_y_rows)
    return pl.pallas_call(
        finish_body,
        out_shape=(shape((width // n_ctx, head_cols), F32), held, held, held),
        in_specs=[VMEM] * 2 + [pl.BlockSpec(memory_space=pl.ANY)] * len(pieces) + [VMEM] * 3,
        out_specs=(VMEM,) + (pl.BlockSpec(memory_space=pl.ANY),) * 3,
        scratch_shapes=[pltpu.VMEM(table.shape, F32)] * 3
        + [
            pltpu.VMEM((n_ctx * rows_here, head_cols), BF16),
            pltpu.SemaphoreType.DMA((len(pieces),)),
            pltpu.SemaphoreType.DMA((3, 4)),
        ],
        compiler_params=pltpu.CompilerParams(vmem_limit_bytes=12 * 1024 * 1024),
        name="finish",
    )(got, other_share, *pieces, table, moment_m, moment_v)


def per_device(*arrays):
    rows_here, cols_here = arrays[0].shape
    fits = lax.axis_size("ctx") == 16 and lax.axis_size("head") == 2
    if fits and rows_here == BLOCK and cols_here == 4 * HD and arrays[9].shape[0] == 2 * BLOCK:
        return dealt_device(*arrays)
    return plain_device(*arrays)


def solution(mesh):
    placed = (
        P("ctx", "head"),
        P(None, "ctx", "head"),
        P("ctx", "head"),
        P("ctx", None),
        P(None, "head"),
        P(None, None, "head"),
        P("ctx"),
        P("ctx", None),
        P("ctx"),
        P("ctx", "head"),
        P("ctx", "head"),
        P("ctx", "head"),
    )
    return jax.shard_map(
        per_device,
        mesh=mesh,
        in_specs=placed,
        out_specs=(P("ctx", "head"), P("ctx", "head"), P("ctx", "head"), P("ctx", "head")),
        check_vma=False,
    )
```

```python
import functools
import math

import jax
import jax.numpy as jnp
from jax import lax
from jax.experimental import pallas as pl
from jax.experimental.pallas import tpu as pltpu
from jax.sharding import PartitionSpec as P

HD = 128
QBLK = 128


beta_first = 0.9
beta_second = 0.999
learn_rate = 0.01
epsilon = 1e-08
first_fix = 1.0 - beta_first**10.0
second_fix = 1.0 - beta_second**10.0


def adam_rows(summed, touched, table, moment_m, moment_v):
    fresh_m = beta_first * moment_m + (1.0 - beta_first) * summed
    fresh_v = beta_second * moment_v + (1.0 - beta_second) * summed * summed
    update = learn_rate * (fresh_m / first_fix) / (jnp.sqrt(fresh_v / second_fix) + epsilon)
    keep = touched[:, None]
    return (
        jnp.where(keep, table - update, table),
        jnp.where(keep, fresh_m, moment_m),
        jnp.where(keep, fresh_v, moment_v),
    )


def pair_scores(query_part, key_part, query_places, query_lower, key_places):
    scale = 1.0 / math.sqrt(HD)
    scores = (
        jnp.einsum("ihd,jhd->hij", query_part, key_part, preferred_element_type=jnp.float32) * scale
    )
    seen = (key_places[None, :] <= query_places[:, None]) & (
        key_places[None, :] >= query_lower[:, None]
    )
    squash = jax.nn.sigmoid(scores)
    return (scores, squash, seen[None])


def score_grads(scores, squash, seen, cotangent_piece, value_part, seq_len):
    dprod = jnp.einsum(
        "ihd,jhd->hij", cotangent_piece, value_part, preferred_element_type=jnp.float32
    )
    return jnp.where(seen, dprod * squash * (1.0 + scores * (1.0 - squash)) / seq_len, 0.0).astype(
        jnp.bfloat16
    )


def score_weights(scores, squash, seen, seq_len):
    return jnp.where(seen, scores * squash / seq_len, 0.0).astype(jnp.bfloat16)


def over_blocks(total, fn, carry):
    sub = math.gcd(total, 1024)
    return lax.fori_loop(
        0, total // sub, lambda index, inner_loop: fn(inner_loop, index * sub), carry
    )


def plain_device(
    queries,
    keys_values,
    attn_cot,
    event_rows,
    adapter,
    qkv_weight,
    starts,
    owners,
    slots,
    table,
    moment_m,
    moment_v,
):
    rows_here = queries.shape[0]
    feature_cols = queries.shape[1]
    heads_here = feature_cols // HD
    n_ctx = lax.axis_size("ctx")
    seq_len = rows_here * n_ctx
    scale = 1.0 / math.sqrt(HD)
    myself = lax.axis_index("ctx")
    local_first = myself * rows_here
    local_places = local_first + jnp.arange(rows_here, dtype=jnp.int32)
    lower = jnp.repeat(starts, QBLK, total_repeat_length=rows_here)
    least_lower = jnp.min(lower)
    query_heads = queries.reshape(rows_here, heads_here, HD)
    cot_heads = attn_cot.reshape(rows_here, heads_here, HD)
    key_heads = keys_values[0].reshape(rows_here, heads_here, HD)
    value_heads = keys_values[1].reshape(rows_here, heads_here, HD)
    zeros = jnp.zeros((rows_here, heads_here, HD), jnp.float32)
    piece = lax.all_gather(keys_values, "ctx", axis=1, tiled=True)

    def key_one_block(inner_loop, offset):
        sub = math.gcd(piece.shape[1], 1024)
        key_first = offset
        live = (key_first <= local_first + rows_here - 1) & (key_first + sub - 1 >= least_lower)

        def key_working(values):
            part = lax.dynamic_slice_in_dim(piece, offset, sub, 1)
            key_part = part[0].reshape(sub, heads_here, HD)
            value_part = part[1].reshape(sub, heads_here, HD)
            key_places = key_first + jnp.arange(sub, dtype=jnp.int32)
            scores, squash, seen = pair_scores(
                query_heads, key_part, local_places, lower, key_places
            )
            dscore = score_grads(scores, squash, seen, cot_heads, value_part, seq_len)
            return values + jnp.einsum(
                "hij,jhd->ihd", dscore, key_part, preferred_element_type=jnp.float32
            )

        return lax.cond(live, key_working, lambda values: values, inner_loop)

    query_grad = over_blocks(piece.shape[1], key_one_block, zeros)
    query_piece = (
        lax.all_gather(queries, "ctx", axis=0, tiled=True),
        lax.all_gather(attn_cot, "ctx", axis=0, tiled=True),
        lax.all_gather(lower, "ctx", axis=0, tiled=True),
    )

    def query_one_block(inner_loop, offset):
        sub = math.gcd(query_piece[0].shape[0], 1024)
        query_first = offset
        query_lower = lax.dynamic_slice_in_dim(query_piece[2], offset, sub, 0)
        live = (local_first <= query_first + sub - 1) & (
            local_first + rows_here - 1 >= jnp.min(query_lower)
        )

        def query_working(values):
            query_part = lax.dynamic_slice_in_dim(query_piece[0], offset, sub, 0).reshape(
                sub, heads_here, HD
            )
            cotangent_piece = lax.dynamic_slice_in_dim(query_piece[1], offset, sub, 0).reshape(
                sub, heads_here, HD
            )
            query_places = query_first + jnp.arange(sub, dtype=jnp.int32)
            scores, squash, seen = pair_scores(
                query_part, key_heads, query_places, query_lower, local_places
            )
            weights = score_weights(scores, squash, seen, seq_len)
            dscore = score_grads(scores, squash, seen, cotangent_piece, value_heads, seq_len)
            key_add = jnp.einsum(
                "hij,ihd->jhd", dscore, query_part, preferred_element_type=jnp.float32
            )
            value_add = jnp.einsum(
                "hij,ihd->jhd", weights, cotangent_piece, preferred_element_type=jnp.float32
            )
            return (values[0] + key_add, values[1] + value_add)

        return lax.cond(live, query_working, lambda values: values, inner_loop)

    key_grad, value_grad = over_blocks(query_piece[0].shape[0], query_one_block, (zeros, zeros))
    head_grads = (
        jnp.stack([query_grad * scale, key_grad * scale, value_grad])
        .astype(jnp.bfloat16)
        .reshape(3, rows_here, feature_cols)
    )
    partial_grad = jnp.einsum(
        "mtc,mdc->td", head_grads, qkv_weight, preferred_element_type=jnp.float32
    )
    head_cols = adapter.shape[1]
    first_col = lax.axis_index("head") * head_cols
    layer_grad = lax.psum(partial_grad.astype(jnp.bfloat16), "head").astype(jnp.float32)
    layer_grad_b = layer_grad.astype(jnp.bfloat16)
    own_grad = lax.dynamic_slice_in_dim(layer_grad, first_col, head_cols, 1)
    row_grads = own_grad + jnp.dot(layer_grad_b, adapter, preferred_element_type=jnp.float32)
    own_rows = lax.dynamic_slice_in_dim(event_rows, first_col, head_cols, 1)
    adapter_grad = lax.psum_scatter(
        lax.dot_general(
            layer_grad_b, own_rows, (((0,), (0,)), ((), ())), preferred_element_type=jnp.float32
        ),
        "ctx",
        scatter_dimension=0,
        tiled=True,
    )
    capacity = max(2, 2 * rows_here // n_ctx)
    target = owners[:, 0]
    onehot = (target[:, None] == jnp.arange(n_ctx, dtype=jnp.int32)[None, :]).astype(jnp.int32)
    prior_blocks = jnp.cumsum(onehot, axis=0) - onehot
    ranking = jnp.sum(prior_blocks * onehot, axis=1)
    cell_index = target * capacity + ranking
    placing = cell_index[:, None] == jnp.arange(n_ctx * capacity, dtype=jnp.int32)[None, :]
    send_rows = lax.dot_general(
        placing.astype(jnp.float32),
        row_grads,
        (((0,), (0,)), ((), ())),
        precision=lax.Precision.HIGHEST,
    ).reshape(n_ctx, capacity, head_cols)
    send_slots = (jnp.sum(jnp.where(placing, slots[:, None] + 1, 0), axis=0) - 1).reshape(
        n_ctx, capacity
    )
    got_rows, got_slots = (
        lax.all_to_all(
            send_rows.astype(jnp.bfloat16), "ctx", split_axis=0, concat_axis=0, tiled=True
        ).astype(send_rows.dtype),
        lax.all_to_all(send_slots, "ctx", split_axis=0, concat_axis=0, tiled=True),
    )
    table_rows = table.shape[0]
    landing = got_slots.reshape(-1)[None, :] == jnp.arange(table_rows, dtype=jnp.int32)[:, None]
    summed = jnp.dot(
        landing.astype(jnp.float32),
        got_rows.reshape(n_ctx * capacity, head_cols),
        precision=lax.Precision.HIGHEST,
    )
    touched = jnp.sum(landing.astype(jnp.int32), axis=1) > 0
    new_table, new_m, new_v = adam_rows(summed, touched, table, moment_m, moment_v)
    return (adapter_grad, new_table, new_m, new_v)


BLOCK = 128
PAIR = 2 * BLOCK
META = 16
PART = PAIR + META
FAR_PART = PART + META
ACROSS_Y = [(i, i ^ 2) for i in range(16)]
FAR_OUT = [(i * 2, (i + 8) * 2) for i in range(8)] + [((i + 8) * 2 + 1, i * 2 + 1) for i in range(8)]
FAR_BACK = [(b, a) for a, b in FAR_OUT]
SWAP = [(0, 1), (1, 0)]
ROUNDS = (8, 4, 1, 2)
F32 = jnp.float32
BF16 = jnp.bfloat16
VMEM = pl.BlockSpec(memory_space=pltpu.VMEM)
SMEM = pl.BlockSpec(memory_space=pltpu.SMEM)


def dot(a, b, axis_a, axis_b):
    return lax.dot_general(a, b, (((axis_a,), (axis_b,)), ((), ())), preferred_element_type=F32)


def spot_of(me):
    return me // 4 % 2 * 2 + me % 2


def kernel_call(body, out_shape, operands, name, flops=0, in_bytes=0):
    specs = [SMEM if o.dtype == jnp.int32 and o.ndim == 1 else VMEM for o in operands]
    return pl.pallas_call(
        body,
        out_shape=out_shape,
        in_specs=specs,
        out_specs=jax.tree.map(lambda _: VMEM, out_shape),
        compiler_params=pltpu.CompilerParams(vmem_limit_bytes=12 * 1024 * 1024),
        cost_estimate=pl.CostEstimate(flops=flops, bytes_accessed=in_bytes, transcendentals=0),
        name=name,
    )(*operands)


def deal_body(starts, queries, keys_values, cot, rows, own, by_x, by_zl, by_both, held_rows, sems):
    core, me = lax.axis_index("head"), lax.axis_index("ctx")
    outs = (own, by_x, by_zl, by_both)
    start = starts[0]
    row = lax.broadcasted_iota(jnp.int32, (META, BLOCK), 0)
    meta = jnp.where(row == 0, start // BLOCK, jnp.where(row == 1, start % BLOCK, 0)).astype(F32).astype(BF16)
    cols = held_rows.shape[1]

    def copies(near, far, half):
        moves = []
        for flip, out in enumerate(outs):
            head = jnp.bitwise_xor(spot_of(me), flip)
            lanes = pl.ds(pl.multiple_of(head * BLOCK, BLOCK), BLOCK)
            for base, pair in ((0, near), (PART, far)):
                for at, source in enumerate(pair):
                    moves.append((source.at[:, lanes], out.at[base + at * BLOCK : base + (at + 1) * BLOCK, :]))
        moves.append((rows.at[:, half * cols : (half + 1) * cols], held_rows.at[:BLOCK, :]))
        moves = [pltpu.make_async_copy(a, b, sems.at[k]) for k, (a, b) in enumerate(moves)]
        for move in moves:
            move.start()
        held_rows[BLOCK:, :] = jnp.zeros((META, cols), BF16)
        for out in outs:
            out[PAIR:PART, :] = meta
            out[PART + PAIR : PART + PART, :] = meta
            out[PART + PART :, :] = jnp.zeros((META, BLOCK), BF16)
        for move in moves:
            move.wait()

    asks = (queries, cot)
    gives = (keys_values.at[0], keys_values.at[1])

    @pl.when(core == 0)
    def _():
        copies(asks, gives, 0)

    @pl.when(core == 1)
    def _():
        copies(gives, asks, 1)


def gather_body(own, rows_1, by_x, by_zl, by_both, rows_2, far, near, two):
    for flip, part in enumerate((own, by_x, by_zl, by_both)):
        near[flip] = part[:PART, :]
        far[flip] = part[PART:, :]
    count = two.shape[0] // 2
    two[:count, :] = rows_1[:count, :]
    two[count:, :] = rows_2[:count, :]


def lower_of(meta):
    meta = meta.astype(F32)
    return (meta[0:1] * BLOCK + meta[1:2]).astype(jnp.int32)


def attend(scale, role_q, crossing, nears, far, far_1, far_2, near_1_sum, near_2_sum, put_far_1, put_far_2):
    me = lax.axis_index("ctx")
    zh, y = me // 8, me // 2 % 2
    spots = [jnp.bitwise_xor(spot_of(me), flip) for flip in range(4)]
    places = [spot // 2 * 4 + spot % 2 for spot in spots]
    lane = lax.broadcasted_iota(jnp.int32, (1, BLOCK), 1)
    row_in = lax.broadcasted_iota(jnp.int32, (BLOCK, 4 * BLOCK), 0)
    never = 1 << 20
    far_zh = 1 - zh if crossing else zh
    place = jnp.concatenate([lane + (far_zh * 8 + y * 2 + s) * BLOCK for s in places], axis=1)
    base_1, base_2 = far_1[...], far_2[...]
    if not role_q:
        low = jnp.concatenate([lower_of(far[s, PAIR:PART, :]) for s in range(4)], axis=1)
    dscores, weights, firsts, seconds = [], [], [], []
    for chunk in range(4):
        rows = slice(chunk * PAIR, (chunk + 1) * PAIR)
        near_ref, near_y = nears[chunk // 2], (y, 1 - y)[chunk // 2]
        pair = (chunk % 2 * 2, chunk % 2 * 2 + 1)
        first = jnp.concatenate([near_ref[s, :BLOCK, :] for s in pair], axis=0)
        second = jnp.concatenate([near_ref[s, BLOCK:PAIR, :] for s in pair], axis=0)
        half = dot(first, base_1, 1, 1) * (0.5 * scale)
        dprod = dot(second, base_2, 1, 1)
        seen = []
        for s in pair:
            start = (zh * 8 + near_y * 2 + places[s]) * BLOCK
            if role_q:
                low = jnp.concatenate([lower_of(near_ref[s, PAIR:PART, :])] * 4, axis=1)
                seen.append(row_in >= jnp.where(place >= low, place - start, never))
            else:
                seen.append((row_in >= low - start) & (row_in <= place - start))
        seen = jnp.concatenate(seen, axis=0)
        tanh = jnp.tanh(half)
        twice = 1.0 + tanh
        weight = half * twice
        dscore = (dprod * twice) * (1.0 + half * (1.0 - tanh))
        weight = jnp.where(seen, weight, 0.0).astype(BF16)
        dscore = jnp.where(seen, dscore, 0.0).astype(BF16)
        grad_1 = dot(dscore, base_1, 1, 0)
        near_1_sum[rows, :] = near_1_sum[rows, :] + grad_1 if crossing else grad_1
        if not role_q:
            grad_2 = dot(weight, base_2, 1, 0)
            near_2_sum[rows, :] = near_2_sum[rows, :] + grad_2 if crossing else grad_2
        dscores.append(dscore)
        weights.append(weight)
        firsts.append(first)
        seconds.append(second)
    put_far_1(dot(jnp.concatenate(dscores, axis=0), jnp.concatenate(firsts, axis=0), 0, 0))
    if role_q:
        put_far_2(dot(jnp.concatenate(weights, axis=0), jnp.concatenate(seconds, axis=0), 0, 0))


def gather_far(far, far_1, far_2):
    for spot in range(4):
        rows = slice(spot * BLOCK, (spot + 1) * BLOCK)
        far_1[rows, :] = far[spot, :BLOCK, :]
        far_2[rows, :] = far[spot, BLOCK:PAIR, :]


def attend_own_body(scale, near_own, far_own, near_in, near_1_sum, near_2_sum, far_sum, far_1, far_2):
    gather_far(far_own, far_1, far_2)
    core = lax.axis_index("head")

    def put(at):
        def store(value):
            far_sum[at] = value

        return store

    rest = ((near_own, near_in), far_own, far_1, far_2, near_1_sum, near_2_sum, put(0), put(1))

    @pl.when(core == 0)
    def _():
        near_2_sum[...] = jnp.zeros_like(near_2_sum)
        attend(scale, True, False, *rest)

    @pl.when(core == 1)
    def _():
        far_sum[1] = jnp.zeros((4 * BLOCK, BLOCK), F32)
        attend(scale, False, False, *rest)


def attend_far_body(scale, seq_len, near_own, near_in, far_in, _1, _2, near_1_sum, near_2_sum, far_out, far_1, far_2):
    core, zh = lax.axis_index("head"), lax.axis_index("ctx") // 8
    far_out[...] = jnp.zeros_like(far_out)

    def put(at, factor):
        def store(value):
            for spot in range(4):
                far_out[spot, at * BLOCK : (at + 1) * BLOCK, :] = (value[spot * BLOCK : (spot + 1) * BLOCK] * factor).astype(BF16)

        return store

    puts = (put(0, scale * 0.5 / seq_len), put(1, 1.0 / seq_len))
    rest = ((near_own, near_in), far_in, far_1, far_2, near_1_sum, near_2_sum, *puts)

    @pl.when((core == 0) & (zh == 1))
    def _():
        gather_far(far_in, far_1, far_2)
        attend(scale, True, True, *rest)

    @pl.when((core == 1) & (zh == 0))
    def _():
        gather_far(far_in, far_1, far_2)
        attend(scale, False, True, *rest)


def near_body(scale, seq_len, near_1_sum, near_2_sum, out):
    for spot in range(4):
        rows = slice((4 + spot) * BLOCK, (5 + spot) * BLOCK)
        out[spot, 0] = (near_1_sum[rows, :] * (scale * 0.5 / seq_len)).astype(BF16)
        out[spot, 1] = (near_2_sum[rows, :] * (1.0 / seq_len)).astype(BF16)


def project_body(by_both, by_zl, by_x, own, weight, partial, sent, held):
    core, me = lax.axis_index("head"), lax.axis_index("ctx")
    for flip, part in enumerate((own, by_x, by_zl, by_both)):
        head = jnp.bitwise_xor(spot_of(me), flip)
        for slot in range(3):
            held[slot, :, pl.ds(pl.multiple_of(head * BLOCK, BLOCK), BLOCK)] = part[slot]
    total = dot(held[1], weight[2], 1, 1)
    total = total + dot(held[0], weight[core], 1, 1)
    total = total + dot(held[2], weight[1 - core], 1, 1)
    partial[...] = total
    sent[...] = total.astype(BF16)


def pack_body(own, other, adapter, placing, slots, out, grad, turned):
    core = lax.axis_index("head")
    n_ctx = out.shape[0]
    head_cols = adapter.shape[1]
    capacity = placing.shape[1] // n_ctx
    tiles = head_cols // BLOCK
    share = own.shape[1] // n_ctx // 2
    total = own[...] + other[...].astype(F32)
    grad[...] = total
    rounded = total.astype(BF16)
    turned[...] = jnp.transpose(rounded)
    rows = grad[:, pl.ds(pl.multiple_of(core * head_cols, head_cols), head_cols)]
    rows = rows + dot(rounded, adapter[...], 1, 0)
    rows = jnp.concatenate([rows.astype(BF16), slots[...]], axis=1)
    cells = dot(placing[...], rows, 0, 0).astype(BF16)
    for p in range(n_ctx):
        for tile in range(tiles + 1):
            out[p, tile * capacity : (tile + 1) * capacity, :] = cells[
                p * capacity : (p + 1) * capacity, tile * BLOCK : (tile + 1) * BLOCK
            ]
        first = pl.multiple_of(p * 2 * share + core * share, share)
        out[p, (tiles + 1) * capacity :, :] = turned[pl.ds(first, share), :]


def place_body(owners, slots, placing, marks):
    count = owners.shape[1]
    capacity = placing.shape[1] // 16
    lane = lax.broadcasted_iota(jnp.int32, (count, BLOCK), 1)
    row = lax.broadcasted_iota(jnp.int32, (count, BLOCK), 0)
    owner_row = jnp.broadcast_to(owners[...].astype(F32), (count, BLOCK))
    owner = jnp.transpose(owner_row)
    same = jnp.where((owner == owner_row) & (lane < row), 1.0, 0.0)
    ranking = jnp.sum(same, axis=1, keepdims=True)
    cell = owner * capacity + ranking
    for tile in range(placing.shape[1] // BLOCK):
        hit = cell == (lane + tile * BLOCK).astype(F32)
        placing[:, tile * BLOCK : (tile + 1) * BLOCK] = hit.astype(F32).astype(BF16)
    mark = jnp.broadcast_to(slots[...] + 1, (count, BLOCK)).astype(F32)
    marks[...] = jnp.transpose(mark).astype(BF16)


def merge_body(flips, scale, seq_len, far, near, near_1_sum, near_2_sum, far_sum, *outs):
    grad_scale, weight_scale = scale * 0.5 / seq_len, 1.0 / seq_len
    for flip, out in zip(flips, outs):
        rows = slice(flip * BLOCK, (flip + 1) * BLOCK)
        out[0] = (near_1_sum[rows, :] * grad_scale + near[flip, 0].astype(F32)).astype(BF16)
        both = (near_2_sum[rows, :] + far_sum[1, rows, :]) * weight_scale
        out[1] = (both + near[flip, 1].astype(F32) + far[flip, BLOCK:PAIR, :].astype(F32)).astype(BF16)
        out[2] = (far_sum[0, rows, :] * grad_scale + far[flip, :BLOCK, :].astype(F32)).astype(BF16)


def finish_body(got, other, *refs):
    pieces, held, grad, targets = refs[:8], refs[8:11], refs[11], refs[12:15]
    made, rows_held, in_sems, out_sems = refs[15:18], refs[18], refs[19], refs[20]
    chunks = out_sems.shape[1]
    span = held[0].shape[0] // chunks

    def rows_of(c):
        return slice(c * span, (c + 1) * span)

    stores = [
        [pltpu.make_async_copy(a.at[rows_of(c), :], b.at[rows_of(c), :], out_sems.at[k, c]) for k, (a, b) in enumerate(zip(made, targets))]
        for c in range(chunks)
    ]
    part = rows_held.shape[0] // 8
    loads = [pltpu.make_async_copy(p, rows_held.at[k * part : (k + 1) * part, :], in_sems.at[k]) for k, p in enumerate(pieces)]
    for move in loads:
        move.start()
    core, me = lax.axis_index("head"), lax.axis_index("ctx")
    share = other.shape[1]
    tiles = held[0].shape[1] // BLOCK
    table_rows = held[0].shape[0]
    n_ctx = got.shape[0]
    capacity = (got.shape[1] - share) // (tiles + 1)
    marks = got[:, tiles * capacity : (tiles + 1) * capacity, :].reshape(n_ctx * capacity, BLOCK).astype(F32)
    lane = lax.broadcasted_iota(jnp.int32, marks.shape, 1)
    landing = [(marks == (lane + (at * BLOCK + 1)).astype(F32)).astype(F32) for at in range(table_rows // BLOCK)]
    landing = jnp.concatenate(landing, axis=1).astype(BF16)
    cells = [got[:, tile * capacity : (tile + 1) * capacity, :].reshape(n_ctx * capacity, BLOCK) for tile in range(tiles)]
    cells = jnp.concatenate(cells + [jnp.ones(marks.shape, BF16)], axis=1)
    summed_all = dot(landing, cells, 0, 0)
    for c in range(chunks):
        rows = rows_of(c)
        summed = summed_all[rows, : tiles * BLOCK]
        touched = jnp.concatenate([summed_all[rows, tiles * BLOCK :]] * tiles, axis=1) > 0.0
        old, m, v = [ref[rows, :] for ref in held]
        fresh_m = beta_first * m + (1.0 - beta_first) * summed
        fresh_v = beta_second * v + (1.0 - beta_second) * summed * summed
        update = learn_rate * (fresh_m / first_fix) / (jnp.sqrt(fresh_v / second_fix) + epsilon)
        made[0][rows, :] = jnp.where(touched, old - update, old)
        made[1][rows, :] = jnp.where(touched, fresh_m, m)
        made[2][rows, :] = jnp.where(touched, fresh_v, v)
        for move in stores[c]:
            move.start()
    masks = [0]
    for bit in ROUNDS:
        masks = masks + [mask ^ bit for mask in masks]
    senders = [jnp.bitwise_xor(me, mask) for mask in masks]
    width = (tiles + 1) * capacity
    mine_t = jnp.concatenate([got[s, width:, :] for s in senders], axis=1)
    other_t = jnp.concatenate([other[s] for s in senders], axis=1)
    both_t = jnp.concatenate([mine_t, other_t], axis=0)
    for move in loads:
        move.wait()
    both = dot(both_t, rows_held[...], 1, 0)
    grad[pl.ds(pl.multiple_of(core * share, share), share), :] = both[:share]
    grad[pl.ds(pl.multiple_of((1 - core) * share, share), share), :] = both[share:]
    for store in stores:
        for move in store:
            move.wait()


def dealt_device(
    queries,
    keys_values,
    attn_cot,
    event_rows,
    adapter,
    qkv_weight,
    starts,
    owners,
    slots,
    table,
    moment_m,
    moment_v,
):
    shape = jax.ShapeDtypeStruct
    n_ctx = lax.axis_size("ctx")
    rows_here = queries.shape[0]
    seq_len = rows_here * n_ctx
    head_cols = adapter.shape[1]
    width = event_rows.shape[1]
    capacity = max(2, 2 * rows_here // n_ctx)
    dealt = shape((PART + FAR_PART, BLOCK), BF16)
    *dealt, own_rows = pl.pallas_call(
        deal_body,
        out_shape=(dealt,) * 4 + (shape((rows_here + META, head_cols), BF16),),
        in_specs=[SMEM] + [pl.BlockSpec(memory_space=pltpu.HBM)] * 4,
        out_specs=(VMEM,) * 5,
        scratch_shapes=[pltpu.SemaphoreType.DMA((17,))],
        compiler_params=pltpu.CompilerParams(vmem_limit_bytes=12 * 1024 * 1024),
        name="deal",
    )(starts, queries, keys_values, attn_cot, event_rows)

    def exchange(sent, bit):
        return lax.ppermute(sent, "ctx", [(i, i ^ bit) for i in range(16)])

    zh_rows = exchange(own_rows, ROUNDS[0])
    both, by_zl, by_x = [exchange(part, bit) for part, bit in zip(dealt[:0:-1], (5, 4, 1))]
    zh_rows, both, by_zl, by_x = lax.optimization_barrier((zh_rows, both, by_zl, by_x))
    far_own, near_own, two = kernel_call(
        gather_body,
        (shape((4, FAR_PART, BLOCK), BF16), shape((4, PART, BLOCK), BF16), shape((2 * rows_here, head_cols), BF16)),
        (dealt[0], own_rows, by_x, by_zl, both, zh_rows),
        "gather",
    )
    far_in = lax.ppermute(far_own, ("ctx", "head"), FAR_OUT)
    near_in = lax.ppermute(near_own, "ctx", ACROSS_Y)
    zl_rows, x_rows, y_rows = [exchange(two, bit) for bit in ROUNDS[1:]]
    scales = (1.0 / math.sqrt(HD), float(seq_len))
    side_scratch = [pltpu.VMEM((4 * BLOCK, BLOCK), BF16)] * 2
    near_sum = shape((8 * BLOCK, BLOCK), F32)
    cost = pl.CostEstimate(flops=10**9, bytes_accessed=2**20, transcendentals=0)
    near_1, near_2, far_sum = pl.pallas_call(
        functools.partial(attend_own_body, scales[0]),
        out_shape=(near_sum, near_sum, shape((2, 4 * BLOCK, BLOCK), F32)),
        in_specs=[VMEM] * 3,
        out_specs=(VMEM,) * 3,
        scratch_shapes=side_scratch,
        compiler_params=pltpu.CompilerParams(vmem_limit_bytes=12 * 1024 * 1024),
        cost_estimate=cost,
        name="attend_own",
    )(near_own, far_own, near_in)
    near_1, near_2, far_out = pl.pallas_call(
        functools.partial(attend_far_body, *scales),
        out_shape=(near_sum, near_sum, shape((4, PART, BLOCK), BF16)),
        in_specs=[VMEM] * 5,
        out_specs=(VMEM,) * 3,
        scratch_shapes=side_scratch,
        input_output_aliases={3: 0, 4: 1},
        compiler_params=pltpu.CompilerParams(vmem_limit_bytes=12 * 1024 * 1024),
        cost_estimate=cost,
        name="attend_far",
    )(near_own, near_in, far_in, near_1, near_2)
    near_1, near_2, far_out, zl_rows, x_rows, y_rows = lax.optimization_barrier(
        (near_1, near_2, far_out, zl_rows, x_rows, y_rows)
    )
    near_out = kernel_call(
        functools.partial(near_body, *scales), shape((4, 2, BLOCK, BLOCK), BF16), (near_1, near_2), "near"
    )
    zl_x_rows = exchange(zl_rows, ROUNDS[2])
    zl_y_rows = exchange(zl_rows, ROUNDS[3])
    far_back = lax.ppermute(far_out, ("ctx", "head"), FAR_BACK)
    near_back = lax.ppermute(near_out, "ctx", ACROSS_Y)
    sums = (far_back, near_back, near_1, near_2, far_sum)
    part = shape((3, BLOCK, BLOCK), BF16)
    (both,) = kernel_call(functools.partial(merge_body, (3,), *scales), (part,), sums, "merge_both")
    both, *sums = lax.optimization_barrier((both, *sums))
    own, *parts = kernel_call(functools.partial(merge_body, (0, 1, 2), *scales), (part,) * 3, sums, "merge")
    both, *parts, zl_x_rows = lax.optimization_barrier((both, *parts, zl_x_rows))
    x_y_rows, zl_x_y_rows = exchange(y_rows, ROUNDS[2]), exchange(zl_x_rows, ROUNDS[3])
    both, by_zl, by_x = [exchange(part, bit) for part, bit in zip((both, parts[1], parts[0]), (5, 4, 1))]
    both, by_zl, by_x, zl_y_rows, zl_x_y_rows = lax.optimization_barrier((both, by_zl, by_x, zl_y_rows, zl_x_y_rows))
    partial, sent = pl.pallas_call(
        project_body,
        out_shape=(shape((rows_here, width), F32), shape((rows_here, width), BF16)),
        in_specs=[VMEM] * 5,
        out_specs=(VMEM, VMEM),
        scratch_shapes=[pltpu.VMEM((3, rows_here, queries.shape[1]), BF16)],
        compiler_params=pltpu.CompilerParams(vmem_limit_bytes=12 * 1024 * 1024),
        name="project",
    )(both, by_zl, by_x, own, qkv_weight)
    sent, owners, slots = lax.optimization_barrier((sent, owners, slots))
    placing, marks = kernel_call(
        place_body,
        (shape((rows_here, n_ctx * capacity), BF16), shape((rows_here, BLOCK), BF16)),
        (owners.reshape(1, rows_here), slots.reshape(1, rows_here)),
        "place",
    )
    other = lax.ppermute(sent, "head", SWAP)
    share = width // n_ctx // 2
    packed_rows = capacity * (head_cols // BLOCK + 1)
    packed = pl.pallas_call(
        pack_body,
        out_shape=shape((n_ctx, packed_rows + share, BLOCK), BF16),
        in_specs=[VMEM] * 5,
        out_specs=VMEM,
        scratch_shapes=[pltpu.VMEM((rows_here, width), F32), pltpu.VMEM((width, rows_here), BF16)],
        compiler_params=pltpu.CompilerParams(vmem_limit_bytes=12 * 1024 * 1024),
        name="pack",
    )(partial, other, adapter, placing, marks)
    got = lax.all_to_all(packed, "ctx", 0, 0, tiled=True)
    other_share = lax.ppermute(got[:, packed_rows:], "head", SWAP)
    held = shape(table.shape, F32)
    pieces = (two, zl_rows, x_rows, zl_x_rows, y_rows, zl_y_rows, x_y_rows, zl_x_y_rows)
    return pl.pallas_call(
        finish_body,
        out_shape=(shape((width // n_ctx, head_cols), F32), held, held, held),
        in_specs=[VMEM] * 2 + [pl.BlockSpec(memory_space=pl.ANY)] * len(pieces) + [VMEM] * 3,
        out_specs=(VMEM,) + (pl.BlockSpec(memory_space=pl.ANY),) * 3,
        scratch_shapes=[pltpu.VMEM(table.shape, F32)] * 3
        + [
            pltpu.VMEM((n_ctx * rows_here, head_cols), BF16),
            pltpu.SemaphoreType.DMA((len(pieces),)),
            pltpu.SemaphoreType.DMA((3, 4)),
        ],
        compiler_params=pltpu.CompilerParams(vmem_limit_bytes=12 * 1024 * 1024),
        name="finish",
    )(got, other_share, *pieces, table, moment_m, moment_v)


def per_device(*arrays):
    rows_here, cols_here = arrays[0].shape
    fits = lax.axis_size("ctx") == 16 and lax.axis_size("head") == 2
    if fits and rows_here == BLOCK and cols_here == 4 * HD and arrays[9].shape[0] == 2 * BLOCK:
        return dealt_device(*arrays)
    return plain_device(*arrays)


def solution(mesh):
    placed = (
        P("ctx", "head"),
        P(None, "ctx", "head"),
        P("ctx", "head"),
        P("ctx", None),
        P(None, "head"),
        P(None, None, "head"),
        P("ctx"),
        P("ctx", None),
        P("ctx"),
        P("ctx", "head"),
        P("ctx", "head"),
        P("ctx", "head"),
    )
    return jax.shard_map(
        per_device,
        mesh=mesh,
        in_specs=placed,
        out_specs=(P("ctx", "head"), P("ctx", "head"), P("ctx", "head"), P("ctx", "head")),
        check_vma=False,
    )
```

```python
import functools
import math

import jax
import jax.numpy as jnp
from jax import lax
from jax.experimental import pallas as pl
from jax.experimental.pallas import tpu as pltpu
from jax.sharding import PartitionSpec as P

HD = 128
QBLK = 128


beta_first = 0.9
beta_second = 0.999
learn_rate = 0.01
epsilon = 1e-08
first_fix = 1.0 - beta_first**10.0
second_fix = 1.0 - beta_second**10.0


def adam_rows(summed, touched, table, moment_m, moment_v):
    fresh_m = beta_first * moment_m + (1.0 - beta_first) * summed
    fresh_v = beta_second * moment_v + (1.0 - beta_second) * summed * summed
    update = learn_rate * (fresh_m / first_fix) / (jnp.sqrt(fresh_v / second_fix) + epsilon)
    keep = touched[:, None]
    return (
        jnp.where(keep, table - update, table),
        jnp.where(keep, fresh_m, moment_m),
        jnp.where(keep, fresh_v, moment_v),
    )


def pair_scores(query_part, key_part, query_places, query_lower, key_places):
    scale = 1.0 / math.sqrt(HD)
    scores = (
        jnp.einsum("ihd,jhd->hij", query_part, key_part, preferred_element_type=jnp.float32) * scale
    )
    seen = (key_places[None, :] <= query_places[:, None]) & (
        key_places[None, :] >= query_lower[:, None]
    )
    squash = jax.nn.sigmoid(scores)
    return (scores, squash, seen[None])


def score_grads(scores, squash, seen, cotangent_piece, value_part, seq_len):
    dprod = jnp.einsum(
        "ihd,jhd->hij", cotangent_piece, value_part, preferred_element_type=jnp.float32
    )
    return jnp.where(seen, dprod * squash * (1.0 + scores * (1.0 - squash)) / seq_len, 0.0).astype(
        jnp.bfloat16
    )


def score_weights(scores, squash, seen, seq_len):
    return jnp.where(seen, scores * squash / seq_len, 0.0).astype(jnp.bfloat16)


def over_blocks(total, fn, carry):
    sub = math.gcd(total, 1024)
    return lax.fori_loop(
        0, total // sub, lambda index, inner_loop: fn(inner_loop, index * sub), carry
    )


def plain_device(
    queries,
    keys_values,
    attn_cot,
    event_rows,
    adapter,
    qkv_weight,
    starts,
    owners,
    slots,
    table,
    moment_m,
    moment_v,
):
    rows_here = queries.shape[0]
    feature_cols = queries.shape[1]
    heads_here = feature_cols // HD
    n_ctx = lax.axis_size("ctx")
    seq_len = rows_here * n_ctx
    scale = 1.0 / math.sqrt(HD)
    myself = lax.axis_index("ctx")
    local_first = myself * rows_here
    local_places = local_first + jnp.arange(rows_here, dtype=jnp.int32)
    lower = jnp.repeat(starts, QBLK, total_repeat_length=rows_here)
    least_lower = jnp.min(lower)
    query_heads = queries.reshape(rows_here, heads_here, HD)
    cot_heads = attn_cot.reshape(rows_here, heads_here, HD)
    key_heads = keys_values[0].reshape(rows_here, heads_here, HD)
    value_heads = keys_values[1].reshape(rows_here, heads_here, HD)
    zeros = jnp.zeros((rows_here, heads_here, HD), jnp.float32)
    piece = lax.all_gather(keys_values, "ctx", axis=1, tiled=True)

    def key_one_block(inner_loop, offset):
        sub = math.gcd(piece.shape[1], 1024)
        key_first = offset
        live = (key_first <= local_first + rows_here - 1) & (key_first + sub - 1 >= least_lower)

        def key_working(values):
            part = lax.dynamic_slice_in_dim(piece, offset, sub, 1)
            key_part = part[0].reshape(sub, heads_here, HD)
            value_part = part[1].reshape(sub, heads_here, HD)
            key_places = key_first + jnp.arange(sub, dtype=jnp.int32)
            scores, squash, seen = pair_scores(
                query_heads, key_part, local_places, lower, key_places
            )
            dscore = score_grads(scores, squash, seen, cot_heads, value_part, seq_len)
            return values + jnp.einsum(
                "hij,jhd->ihd", dscore, key_part, preferred_element_type=jnp.float32
            )

        return lax.cond(live, key_working, lambda values: values, inner_loop)

    query_grad = over_blocks(piece.shape[1], key_one_block, zeros)
    query_piece = (
        lax.all_gather(queries, "ctx", axis=0, tiled=True),
        lax.all_gather(attn_cot, "ctx", axis=0, tiled=True),
        lax.all_gather(lower, "ctx", axis=0, tiled=True),
    )

    def query_one_block(inner_loop, offset):
        sub = math.gcd(query_piece[0].shape[0], 1024)
        query_first = offset
        query_lower = lax.dynamic_slice_in_dim(query_piece[2], offset, sub, 0)
        live = (local_first <= query_first + sub - 1) & (
            local_first + rows_here - 1 >= jnp.min(query_lower)
        )

        def query_working(values):
            query_part = lax.dynamic_slice_in_dim(query_piece[0], offset, sub, 0).reshape(
                sub, heads_here, HD
            )
            cotangent_piece = lax.dynamic_slice_in_dim(query_piece[1], offset, sub, 0).reshape(
                sub, heads_here, HD
            )
            query_places = query_first + jnp.arange(sub, dtype=jnp.int32)
            scores, squash, seen = pair_scores(
                query_part, key_heads, query_places, query_lower, local_places
            )
            weights = score_weights(scores, squash, seen, seq_len)
            dscore = score_grads(scores, squash, seen, cotangent_piece, value_heads, seq_len)
            key_add = jnp.einsum(
                "hij,ihd->jhd", dscore, query_part, preferred_element_type=jnp.float32
            )
            value_add = jnp.einsum(
                "hij,ihd->jhd", weights, cotangent_piece, preferred_element_type=jnp.float32
            )
            return (values[0] + key_add, values[1] + value_add)

        return lax.cond(live, query_working, lambda values: values, inner_loop)

    key_grad, value_grad = over_blocks(query_piece[0].shape[0], query_one_block, (zeros, zeros))
    head_grads = (
        jnp.stack([query_grad * scale, key_grad * scale, value_grad])
        .astype(jnp.bfloat16)
        .reshape(3, rows_here, feature_cols)
    )
    partial_grad = jnp.einsum(
        "mtc,mdc->td", head_grads, qkv_weight, preferred_element_type=jnp.float32
    )
    head_cols = adapter.shape[1]
    first_col = lax.axis_index("head") * head_cols
    layer_grad = lax.psum(partial_grad.astype(jnp.bfloat16), "head").astype(jnp.float32)
    layer_grad_b = layer_grad.astype(jnp.bfloat16)
    own_grad = lax.dynamic_slice_in_dim(layer_grad, first_col, head_cols, 1)
    row_grads = own_grad + jnp.dot(layer_grad_b, adapter, preferred_element_type=jnp.float32)
    own_rows = lax.dynamic_slice_in_dim(event_rows, first_col, head_cols, 1)
    adapter_grad = lax.psum_scatter(
        lax.dot_general(
            layer_grad_b, own_rows, (((0,), (0,)), ((), ())), preferred_element_type=jnp.float32
        ),
        "ctx",
        scatter_dimension=0,
        tiled=True,
    )
    capacity = max(2, 2 * rows_here // n_ctx)
    target = owners[:, 0]
    onehot = (target[:, None] == jnp.arange(n_ctx, dtype=jnp.int32)[None, :]).astype(jnp.int32)
    prior_blocks = jnp.cumsum(onehot, axis=0) - onehot
    ranking = jnp.sum(prior_blocks * onehot, axis=1)
    cell_index = target * capacity + ranking
    placing = cell_index[:, None] == jnp.arange(n_ctx * capacity, dtype=jnp.int32)[None, :]
    send_rows = lax.dot_general(
        placing.astype(jnp.float32),
        row_grads,
        (((0,), (0,)), ((), ())),
        precision=lax.Precision.HIGHEST,
    ).reshape(n_ctx, capacity, head_cols)
    send_slots = (jnp.sum(jnp.where(placing, slots[:, None] + 1, 0), axis=0) - 1).reshape(
        n_ctx, capacity
    )
    got_rows, got_slots = (
        lax.all_to_all(
            send_rows.astype(jnp.bfloat16), "ctx", split_axis=0, concat_axis=0, tiled=True
        ).astype(send_rows.dtype),
        lax.all_to_all(send_slots, "ctx", split_axis=0, concat_axis=0, tiled=True),
    )
    table_rows = table.shape[0]
    landing = got_slots.reshape(-1)[None, :] == jnp.arange(table_rows, dtype=jnp.int32)[:, None]
    summed = jnp.dot(
        landing.astype(jnp.float32),
        got_rows.reshape(n_ctx * capacity, head_cols),
        precision=lax.Precision.HIGHEST,
    )
    touched = jnp.sum(landing.astype(jnp.int32), axis=1) > 0
    new_table, new_m, new_v = adam_rows(summed, touched, table, moment_m, moment_v)
    return (adapter_grad, new_table, new_m, new_v)


BLOCK = 128
PAIR = 2 * BLOCK
META = 16
PART = PAIR + META
FAR_PART = PART + META
ACROSS_Y = [(i, i ^ 2) for i in range(16)]
FAR_OUT = [(i * 2, (i + 8) * 2) for i in range(8)] + [((i + 8) * 2 + 1, i * 2 + 1) for i in range(8)]
FAR_BACK = [(b, a) for a, b in FAR_OUT]
SWAP = [(0, 1), (1, 0)]
ROUNDS = (8, 4, 1, 2)
F32 = jnp.float32
BF16 = jnp.bfloat16
VMEM = pl.BlockSpec(memory_space=pltpu.VMEM)
SMEM = pl.BlockSpec(memory_space=pltpu.SMEM)


def dot(a, b, axis_a, axis_b):
    return lax.dot_general(a, b, (((axis_a,), (axis_b,)), ((), ())), preferred_element_type=F32)


def spot_of(me):
    return me // 4 % 2 * 2 + me % 2


def kernel_call(body, out_shape, operands, name, flops=0, in_bytes=0):
    specs = [SMEM if o.dtype == jnp.int32 and o.ndim == 1 else VMEM for o in operands]
    return pl.pallas_call(
        body,
        out_shape=out_shape,
        in_specs=specs,
        out_specs=jax.tree.map(lambda _: VMEM, out_shape),
        compiler_params=pltpu.CompilerParams(vmem_limit_bytes=12 * 1024 * 1024),
        cost_estimate=pl.CostEstimate(flops=flops, bytes_accessed=in_bytes, transcendentals=0),
        name=name,
    )(*operands)


def deal_body(starts, queries, keys_values, cot, rows, own, by_x, by_zl, by_both, held_rows, sems):
    core, me = lax.axis_index("head"), lax.axis_index("ctx")
    outs = (own, by_x, by_zl, by_both)
    start = starts[0]
    row = lax.broadcasted_iota(jnp.int32, (META, BLOCK), 0)
    meta = jnp.where(row == 0, start // BLOCK, jnp.where(row == 1, start % BLOCK, 0)).astype(F32).astype(BF16)
    cols = held_rows.shape[1]

    def copies(near, far, half):
        moves = []
        for flip, out in enumerate(outs):
            head = jnp.bitwise_xor(spot_of(me), flip)
            lanes = pl.ds(pl.multiple_of(head * BLOCK, BLOCK), BLOCK)
            for base, pair in ((0, near), (PART, far)):
                for at, source in enumerate(pair):
                    moves.append((source.at[:, lanes], out.at[base + at * BLOCK : base + (at + 1) * BLOCK, :]))
        moves.append((rows.at[:, half * cols : (half + 1) * cols], held_rows.at[:BLOCK, :]))
        moves = [pltpu.make_async_copy(a, b, sems.at[k]) for k, (a, b) in enumerate(moves)]
        for move in moves:
            move.start()
        held_rows[BLOCK:, :] = jnp.zeros((META, cols), BF16)
        for out in outs:
            out[PAIR:PART, :] = meta
            out[PART + PAIR : PART + PART, :] = meta
            out[PART + PART :, :] = jnp.zeros((META, BLOCK), BF16)
        for move in moves:
            move.wait()

    asks = (queries, cot)
    gives = (keys_values.at[0], keys_values.at[1])

    @pl.when(core == 0)
    def _():
        copies(asks, gives, 0)

    @pl.when(core == 1)
    def _():
        copies(gives, asks, 1)


def gather_body(own, rows_1, by_x, by_zl, by_both, rows_2, far, near, two):
    for flip, part in enumerate((own, by_x, by_zl, by_both)):
        near[flip] = part[:PART, :]
        far[flip] = part[PART:, :]
    count = two.shape[0] // 2
    two[:count, :] = rows_1[:count, :]
    two[count:, :] = rows_2[:count, :]


def lower_of(meta):
    meta = meta.astype(F32)
    return (meta[0:1] * BLOCK + meta[1:2]).astype(jnp.int32)


def attend(scale, role_q, crossing, nears, far, far_1, far_2, near_1_sum, near_2_sum, put_far_1, put_far_2):
    me = lax.axis_index("ctx")
    zh, y = me // 8, me // 2 % 2
    spots = [jnp.bitwise_xor(spot_of(me), flip) for flip in range(4)]
    places = [spot // 2 * 4 + spot % 2 for spot in spots]
    lane = lax.broadcasted_iota(jnp.int32, (1, BLOCK), 1)
    row_in = lax.broadcasted_iota(jnp.int32, (BLOCK, 4 * BLOCK), 0)
    never = 1 << 20
    far_zh = 1 - zh if crossing else zh
    place = jnp.concatenate([lane + (far_zh * 8 + y * 2 + s) * BLOCK for s in places], axis=1)
    base_1, base_2 = far_1[...], far_2[...]
    if not role_q:
        low = jnp.concatenate([lower_of(far[s, PAIR:PART, :]) for s in range(4)], axis=1)
    dscores, weights, firsts, seconds = [], [], [], []
    for chunk in range(4):
        rows = slice(chunk * PAIR, (chunk + 1) * PAIR)
        near_ref, near_y = nears[chunk // 2], (y, 1 - y)[chunk // 2]
        pair = (chunk % 2 * 2, chunk % 2 * 2 + 1)
        first = jnp.concatenate([near_ref[s, :BLOCK, :] for s in pair], axis=0)
        second = jnp.concatenate([near_ref[s, BLOCK:PAIR, :] for s in pair], axis=0)
        half = dot(first, base_1, 1, 1) * (0.5 * scale)
        dprod = dot(second, base_2, 1, 1)
        seen = []
        for s in pair:
            start = (zh * 8 + near_y * 2 + places[s]) * BLOCK
            if role_q:
                low = jnp.concatenate([lower_of(near_ref[s, PAIR:PART, :])] * 4, axis=1)
                seen.append(row_in >= jnp.where(place >= low, place - start, never))
            else:
                seen.append((row_in >= low - start) & (row_in <= place - start))
        seen = jnp.concatenate(seen, axis=0)
        tanh = jnp.tanh(half)
        twice = 1.0 + tanh
        weight = half * twice
        dscore = (dprod * twice) * (1.0 + half * (1.0 - tanh))
        weight = jnp.where(seen, weight, 0.0).astype(BF16)
        dscore = jnp.where(seen, dscore, 0.0).astype(BF16)
        grad_1 = dot(dscore, base_1, 1, 0)
        near_1_sum[rows, :] = near_1_sum[rows, :] + grad_1 if crossing else grad_1
        if not role_q:
            grad_2 = dot(weight, base_2, 1, 0)
            near_2_sum[rows, :] = near_2_sum[rows, :] + grad_2 if crossing else grad_2
        dscores.append(dscore)
        weights.append(weight)
        firsts.append(first)
        seconds.append(second)
    put_far_1(dot(jnp.concatenate(dscores, axis=0), jnp.concatenate(firsts, axis=0), 0, 0))
    if role_q:
        put_far_2(dot(jnp.concatenate(weights, axis=0), jnp.concatenate(seconds, axis=0), 0, 0))


def gather_far(far, far_1, far_2):
    for spot in range(4):
        rows = slice(spot * BLOCK, (spot + 1) * BLOCK)
        far_1[rows, :] = far[spot, :BLOCK, :]
        far_2[rows, :] = far[spot, BLOCK:PAIR, :]


def attend_own_body(scale, near_own, far_own, near_in, near_1_sum, near_2_sum, far_sum, far_1, far_2):
    gather_far(far_own, far_1, far_2)
    core = lax.axis_index("head")

    def put(at):
        def store(value):
            far_sum[at] = value

        return store

    rest = ((near_own, near_in), far_own, far_1, far_2, near_1_sum, near_2_sum, put(0), put(1))

    @pl.when(core == 0)
    def _():
        near_2_sum[...] = jnp.zeros_like(near_2_sum)
        attend(scale, True, False, *rest)

    @pl.when(core == 1)
    def _():
        far_sum[1] = jnp.zeros((4 * BLOCK, BLOCK), F32)
        attend(scale, False, False, *rest)


def attend_far_body(scale, seq_len, near_own, near_in, far_in, _1, _2, near_1_sum, near_2_sum, far_out, far_1, far_2):
    core, zh = lax.axis_index("head"), lax.axis_index("ctx") // 8
    far_out[...] = jnp.zeros_like(far_out)

    def put(at, factor):
        def store(value):
            for spot in range(4):
                far_out[spot, at * BLOCK : (at + 1) * BLOCK, :] = (value[spot * BLOCK : (spot + 1) * BLOCK] * factor).astype(BF16)

        return store

    puts = (put(0, scale * 0.5 / seq_len), put(1, 1.0 / seq_len))
    rest = ((near_own, near_in), far_in, far_1, far_2, near_1_sum, near_2_sum, *puts)

    @pl.when((core == 0) & (zh == 1))
    def _():
        gather_far(far_in, far_1, far_2)
        attend(scale, True, True, *rest)

    @pl.when((core == 1) & (zh == 0))
    def _():
        gather_far(far_in, far_1, far_2)
        attend(scale, False, True, *rest)


def near_body(scale, seq_len, near_1_sum, near_2_sum, out):
    for spot in range(4):
        rows = slice((4 + spot) * BLOCK, (5 + spot) * BLOCK)
        out[spot, 0] = (near_1_sum[rows, :] * (scale * 0.5 / seq_len)).astype(BF16)
        out[spot, 1] = (near_2_sum[rows, :] * (1.0 / seq_len)).astype(BF16)


def project_body(by_both, by_zl, by_x, own, weight, partial, sent, held):
    core, me = lax.axis_index("head"), lax.axis_index("ctx")
    for flip, part in enumerate((own, by_x, by_zl, by_both)):
        head = jnp.bitwise_xor(spot_of(me), flip)
        for slot in range(3):
            held[slot, :, pl.ds(pl.multiple_of(head * BLOCK, BLOCK), BLOCK)] = part[slot]
    total = dot(held[1], weight[2], 1, 1)
    total = total + dot(held[0], weight[core], 1, 1)
    total = total + dot(held[2], weight[1 - core], 1, 1)
    partial[...] = total
    sent[...] = total.astype(BF16)


def pack_body(own, other, adapter, placing, slots, out, grad, turned):
    core = lax.axis_index("head")
    n_ctx = out.shape[0]
    head_cols = adapter.shape[1]
    capacity = placing.shape[1] // n_ctx
    tiles = head_cols // BLOCK
    share = own.shape[1] // n_ctx // 2
    total = own[...] + other[...].astype(F32)
    grad[...] = total
    rounded = total.astype(BF16)
    turned[...] = jnp.transpose(rounded)
    rows = grad[:, pl.ds(pl.multiple_of(core * head_cols, head_cols), head_cols)]
    rows = rows + dot(rounded, adapter[...], 1, 0)
    rows = jnp.concatenate([rows.astype(BF16), slots[...]], axis=1)
    cells = dot(placing[...], rows, 0, 0).astype(BF16)
    for p in range(n_ctx):
        for tile in range(tiles + 1):
            out[p, tile * capacity : (tile + 1) * capacity, :] = cells[
                p * capacity : (p + 1) * capacity, tile * BLOCK : (tile + 1) * BLOCK
            ]
        first = pl.multiple_of(p * 2 * share + core * share, share)
        out[p, (tiles + 1) * capacity :, :] = turned[pl.ds(first, share), :]


def place_body(owners, slots, placing, marks):
    count = owners.shape[1]
    capacity = placing.shape[1] // 16
    lane = lax.broadcasted_iota(jnp.int32, (count, BLOCK), 1)
    row = lax.broadcasted_iota(jnp.int32, (count, BLOCK), 0)
    owner_row = jnp.broadcast_to(owners[...].astype(F32), (count, BLOCK))
    owner = jnp.transpose(owner_row)
    same = jnp.where((owner == owner_row) & (lane < row), 1.0, 0.0)
    ranking = jnp.sum(same, axis=1, keepdims=True)
    cell = owner * capacity + ranking
    for tile in range(placing.shape[1] // BLOCK):
        hit = cell == (lane + tile * BLOCK).astype(F32)
        placing[:, tile * BLOCK : (tile + 1) * BLOCK] = hit.astype(F32).astype(BF16)
    mark = jnp.broadcast_to(slots[...] + 1, (count, BLOCK)).astype(F32)
    marks[...] = jnp.transpose(mark).astype(BF16)


def merge_body(flips, scale, seq_len, far, near, near_1_sum, near_2_sum, far_sum, *outs):
    grad_scale, weight_scale = scale * 0.5 / seq_len, 1.0 / seq_len
    for flip, out in zip(flips, outs):
        rows = slice(flip * BLOCK, (flip + 1) * BLOCK)
        out[0] = (near_1_sum[rows, :] * grad_scale + near[flip, 0].astype(F32)).astype(BF16)
        both = (near_2_sum[rows, :] + far_sum[1, rows, :]) * weight_scale
        out[1] = (both + near[flip, 1].astype(F32) + far[flip, BLOCK:PAIR, :].astype(F32)).astype(BF16)
        out[2] = (far_sum[0, rows, :] * grad_scale + far[flip, :BLOCK, :].astype(F32)).astype(BF16)


def finish_body(got, other, *refs):
    pieces, held, grad, targets = refs[:8], refs[8:11], refs[11], refs[12:15]
    made, rows_held, in_sems, out_sems = refs[15:18], refs[18], refs[19], refs[20]
    chunks = out_sems.shape[1]
    span = held[0].shape[0] // chunks

    def rows_of(c):
        return slice(c * span, (c + 1) * span)

    stores = [
        [pltpu.make_async_copy(a.at[rows_of(c), :], b.at[rows_of(c), :], out_sems.at[k, c]) for k, (a, b) in enumerate(zip(made, targets))]
        for c in range(chunks)
    ]
    part = rows_held.shape[0] // 8
    loads = [pltpu.make_async_copy(p, rows_held.at[k * part : (k + 1) * part, :], in_sems.at[k]) for k, p in enumerate(pieces)]
    for move in loads:
        move.start()
    core, me = lax.axis_index("head"), lax.axis_index("ctx")
    share = other.shape[1]
    tiles = held[0].shape[1] // BLOCK
    table_rows = held[0].shape[0]
    n_ctx = got.shape[0]
    capacity = (got.shape[1] - share) // (tiles + 1)
    marks = got[:, tiles * capacity : (tiles + 1) * capacity, :].reshape(n_ctx * capacity, BLOCK).astype(F32)
    lane = lax.broadcasted_iota(jnp.int32, marks.shape, 1)
    landing = [(marks == (lane + (at * BLOCK + 1)).astype(F32)).astype(F32) for at in range(table_rows // BLOCK)]
    landing = jnp.concatenate(landing, axis=1).astype(BF16)
    cells = [got[:, tile * capacity : (tile + 1) * capacity, :].reshape(n_ctx * capacity, BLOCK) for tile in range(tiles)]
    cells = jnp.concatenate(cells + [jnp.ones(marks.shape, BF16)], axis=1)
    summed_all = dot(landing, cells, 0, 0)
    for c in range(chunks):
        rows = rows_of(c)
        summed = summed_all[rows, : tiles * BLOCK]
        touched = jnp.concatenate([summed_all[rows, tiles * BLOCK :]] * tiles, axis=1) > 0.0
        old, m, v = [ref[rows, :] for ref in held]
        fresh_m = beta_first * m + (1.0 - beta_first) * summed
        fresh_v = beta_second * v + (1.0 - beta_second) * summed * summed
        update = learn_rate * (fresh_m / first_fix) / (jnp.sqrt(fresh_v / second_fix) + epsilon)
        made[0][rows, :] = jnp.where(touched, old - update, old)
        made[1][rows, :] = jnp.where(touched, fresh_m, m)
        made[2][rows, :] = jnp.where(touched, fresh_v, v)
        for move in stores[c]:
            move.start()
    masks = [0]
    for bit in ROUNDS:
        masks = masks + [mask ^ bit for mask in masks]
    senders = [jnp.bitwise_xor(me, mask) for mask in masks]
    width = (tiles + 1) * capacity
    mine_t = jnp.concatenate([got[s, width:, :] for s in senders], axis=1)
    other_t = jnp.concatenate([other[s] for s in senders], axis=1)
    both_t = jnp.concatenate([mine_t, other_t], axis=0)
    for move in loads:
        move.wait()
    both = dot(both_t, rows_held[...], 1, 0)
    grad[pl.ds(pl.multiple_of(core * share, share), share), :] = both[:share]
    grad[pl.ds(pl.multiple_of((1 - core) * share, share), share), :] = both[share:]
    for store in stores:
        for move in store:
            move.wait()


def dealt_device(
    queries,
    keys_values,
    attn_cot,
    event_rows,
    adapter,
    qkv_weight,
    starts,
    owners,
    slots,
    table,
    moment_m,
    moment_v,
):
    shape = jax.ShapeDtypeStruct
    n_ctx = lax.axis_size("ctx")
    rows_here = queries.shape[0]
    seq_len = rows_here * n_ctx
    head_cols = adapter.shape[1]
    width = event_rows.shape[1]
    capacity = max(2, 2 * rows_here // n_ctx)
    dealt = shape((PART + FAR_PART, BLOCK), BF16)
    *dealt, own_rows = pl.pallas_call(
        deal_body,
        out_shape=(dealt,) * 4 + (shape((rows_here + META, head_cols), BF16),),
        in_specs=[SMEM] + [pl.BlockSpec(memory_space=pltpu.HBM)] * 4,
        out_specs=(VMEM,) * 5,
        scratch_shapes=[pltpu.SemaphoreType.DMA((17,))],
        compiler_params=pltpu.CompilerParams(vmem_limit_bytes=12 * 1024 * 1024),
        name="deal",
    )(starts, queries, keys_values, attn_cot, event_rows)

    def exchange(sent, bit):
        return lax.ppermute(sent, "ctx", [(i, i ^ bit) for i in range(16)])

    zh_rows = exchange(own_rows, ROUNDS[0])
    both, by_zl, by_x = [exchange(part, bit) for part, bit in zip(dealt[:0:-1], (5, 4, 1))]
    zh_rows, both, by_zl, by_x = lax.optimization_barrier((zh_rows, both, by_zl, by_x))
    far_own, near_own, two = kernel_call(
        gather_body,
        (shape((4, FAR_PART, BLOCK), BF16), shape((4, PART, BLOCK), BF16), shape((2 * rows_here, head_cols), BF16)),
        (dealt[0], own_rows, by_x, by_zl, both, zh_rows),
        "gather",
    )
    far_in = lax.ppermute(far_own, ("ctx", "head"), FAR_OUT)
    near_in = lax.ppermute(near_own, "ctx", ACROSS_Y)
    zl_rows, x_rows, y_rows = [exchange(two, bit) for bit in ROUNDS[1:]]
    scales = (1.0 / math.sqrt(HD), float(seq_len))
    side_scratch = [pltpu.VMEM((4 * BLOCK, BLOCK), BF16)] * 2
    near_sum = shape((8 * BLOCK, BLOCK), F32)
    cost = pl.CostEstimate(flops=10**8, bytes_accessed=2**16, transcendentals=0)
    near_1, near_2, far_sum = pl.pallas_call(
        functools.partial(attend_own_body, scales[0]),
        out_shape=(near_sum, near_sum, shape((2, 4 * BLOCK, BLOCK), F32)),
        in_specs=[VMEM] * 3,
        out_specs=(VMEM,) * 3,
        scratch_shapes=side_scratch,
        compiler_params=pltpu.CompilerParams(vmem_limit_bytes=12 * 1024 * 1024),
        cost_estimate=cost,
        name="attend_own",
    )(near_own, far_own, near_in)
    near_1, near_2, far_out = pl.pallas_call(
        functools.partial(attend_far_body, *scales),
        out_shape=(near_sum, near_sum, shape((4, PART, BLOCK), BF16)),
        in_specs=[VMEM] * 5,
        out_specs=(VMEM,) * 3,
        scratch_shapes=side_scratch,
        input_output_aliases={3: 0, 4: 1},
        compiler_params=pltpu.CompilerParams(vmem_limit_bytes=12 * 1024 * 1024),
        cost_estimate=cost,
        name="attend_far",
    )(near_own, near_in, far_in, near_1, near_2)
    near_1, near_2, far_out, zl_rows, x_rows, y_rows = lax.optimization_barrier(
        (near_1, near_2, far_out, zl_rows, x_rows, y_rows)
    )
    near_out = kernel_call(
        functools.partial(near_body, *scales), shape((4, 2, BLOCK, BLOCK), BF16), (near_1, near_2), "near"
    )
    zl_x_rows = exchange(zl_rows, ROUNDS[2])
    zl_y_rows = exchange(zl_rows, ROUNDS[3])
    far_back = lax.ppermute(far_out, ("ctx", "head"), FAR_BACK)
    near_back = lax.ppermute(near_out, "ctx", ACROSS_Y)
    sums = (far_back, near_back, near_1, near_2, far_sum)
    part = shape((3, BLOCK, BLOCK), BF16)
    (both,) = kernel_call(functools.partial(merge_body, (3,), *scales), (part,), sums, "merge_both")
    both, *sums = lax.optimization_barrier((both, *sums))
    own, *parts = kernel_call(functools.partial(merge_body, (0, 1, 2), *scales), (part,) * 3, sums, "merge")
    both, *parts, zl_x_rows = lax.optimization_barrier((both, *parts, zl_x_rows))
    x_y_rows, zl_x_y_rows = exchange(y_rows, ROUNDS[2]), exchange(zl_x_rows, ROUNDS[3])
    both, by_zl, by_x = [exchange(part, bit) for part, bit in zip((both, parts[1], parts[0]), (5, 4, 1))]
    both, by_zl, by_x, zl_y_rows, zl_x_y_rows = lax.optimization_barrier((both, by_zl, by_x, zl_y_rows, zl_x_y_rows))
    partial, sent = pl.pallas_call(
        project_body,
        out_shape=(shape((rows_here, width), F32), shape((rows_here, width), BF16)),
        in_specs=[VMEM] * 5,
        out_specs=(VMEM, VMEM),
        scratch_shapes=[pltpu.VMEM((3, rows_here, queries.shape[1]), BF16)],
        compiler_params=pltpu.CompilerParams(vmem_limit_bytes=12 * 1024 * 1024),
        name="project",
    )(both, by_zl, by_x, own, qkv_weight)
    sent, owners, slots = lax.optimization_barrier((sent, owners, slots))
    placing, marks = kernel_call(
        place_body,
        (shape((rows_here, n_ctx * capacity), BF16), shape((rows_here, BLOCK), BF16)),
        (owners.reshape(1, rows_here), slots.reshape(1, rows_here)),
        "place",
    )
    other = lax.ppermute(sent, "head", SWAP)
    other, x_y_rows = lax.optimization_barrier((other, x_y_rows))
    share = width // n_ctx // 2
    packed_rows = capacity * (head_cols // BLOCK + 1)
    packed = pl.pallas_call(
        pack_body,
        out_shape=shape((n_ctx, packed_rows + share, BLOCK), BF16),
        in_specs=[VMEM] * 5,
        out_specs=VMEM,
        scratch_shapes=[pltpu.VMEM((rows_here, width), F32), pltpu.VMEM((width, rows_here), BF16)],
        compiler_params=pltpu.CompilerParams(vmem_limit_bytes=12 * 1024 * 1024),
        name="pack",
    )(partial, other, adapter, placing, marks)
    got = lax.all_to_all(packed, "ctx", 0, 0, tiled=True)
    other_share = lax.ppermute(got[:, packed_rows:], "head", SWAP)
    held = shape(table.shape, F32)
    pieces = (two, zl_rows, x_rows, zl_x_rows, y_rows, zl_y_rows, x_y_rows, zl_x_y_rows)
    return pl.pallas_call(
        finish_body,
        out_shape=(shape((width // n_ctx, head_cols), F32), held, held, held),
        in_specs=[VMEM] * 2 + [pl.BlockSpec(memory_space=pl.ANY)] * len(pieces) + [VMEM] * 3,
        out_specs=(VMEM,) + (pl.BlockSpec(memory_space=pl.ANY),) * 3,
        scratch_shapes=[pltpu.VMEM(table.shape, F32)] * 3
        + [
            pltpu.VMEM((n_ctx * rows_here, head_cols), BF16),
            pltpu.SemaphoreType.DMA((len(pieces),)),
            pltpu.SemaphoreType.DMA((3, 4)),
        ],
        compiler_params=pltpu.CompilerParams(vmem_limit_bytes=12 * 1024 * 1024),
        name="finish",
    )(got, other_share, *pieces, table, moment_m, moment_v)


def per_device(*arrays):
    rows_here, cols_here = arrays[0].shape
    fits = lax.axis_size("ctx") == 16 and lax.axis_size("head") == 2
    if fits and rows_here == BLOCK and cols_here == 4 * HD and arrays[9].shape[0] == 2 * BLOCK:
        return dealt_device(*arrays)
    return plain_device(*arrays)


def solution(mesh):
    placed = (
        P("ctx", "head"),
        P(None, "ctx", "head"),
        P("ctx", "head"),
        P("ctx", None),
        P(None, "head"),
        P(None, None, "head"),
        P("ctx"),
        P("ctx", None),
        P("ctx"),
        P("ctx", "head"),
        P("ctx", "head"),
        P("ctx", "head"),
    )
    return jax.shard_map(
        per_device,
        mesh=mesh,
        in_specs=placed,
        out_specs=(P("ctx", "head"), P("ctx", "head"), P("ctx", "head"), P("ctx", "head")),
        check_vma=False,
    )
```

```python
import functools
import math

import jax
import jax.numpy as jnp
from jax import lax
from jax.experimental import pallas as pl
from jax.experimental.pallas import tpu as pltpu
from jax.sharding import PartitionSpec as P

HD = 128
QBLK = 128


beta_first = 0.9
beta_second = 0.999
learn_rate = 0.01
epsilon = 1e-08
first_fix = 1.0 - beta_first**10.0
second_fix = 1.0 - beta_second**10.0


def adam_rows(summed, touched, table, moment_m, moment_v):
    fresh_m = beta_first * moment_m + (1.0 - beta_first) * summed
    fresh_v = beta_second * moment_v + (1.0 - beta_second) * summed * summed
    update = learn_rate * (fresh_m / first_fix) / (jnp.sqrt(fresh_v / second_fix) + epsilon)
    keep = touched[:, None]
    return (
        jnp.where(keep, table - update, table),
        jnp.where(keep, fresh_m, moment_m),
        jnp.where(keep, fresh_v, moment_v),
    )


def pair_scores(query_part, key_part, query_places, query_lower, key_places):
    scale = 1.0 / math.sqrt(HD)
    scores = (
        jnp.einsum("ihd,jhd->hij", query_part, key_part, preferred_element_type=jnp.float32) * scale
    )
    seen = (key_places[None, :] <= query_places[:, None]) & (
        key_places[None, :] >= query_lower[:, None]
    )
    squash = jax.nn.sigmoid(scores)
    return (scores, squash, seen[None])


def score_grads(scores, squash, seen, cotangent_piece, value_part, seq_len):
    dprod = jnp.einsum(
        "ihd,jhd->hij", cotangent_piece, value_part, preferred_element_type=jnp.float32
    )
    return jnp.where(seen, dprod * squash * (1.0 + scores * (1.0 - squash)) / seq_len, 0.0).astype(
        jnp.bfloat16
    )


def score_weights(scores, squash, seen, seq_len):
    return jnp.where(seen, scores * squash / seq_len, 0.0).astype(jnp.bfloat16)


def over_blocks(total, fn, carry):
    sub = math.gcd(total, 1024)
    return lax.fori_loop(
        0, total // sub, lambda index, inner_loop: fn(inner_loop, index * sub), carry
    )


def plain_device(
    queries,
    keys_values,
    attn_cot,
    event_rows,
    adapter,
    qkv_weight,
    starts,
    owners,
    slots,
    table,
    moment_m,
    moment_v,
):
    rows_here = queries.shape[0]
    feature_cols = queries.shape[1]
    heads_here = feature_cols // HD
    n_ctx = lax.axis_size("ctx")
    seq_len = rows_here * n_ctx
    scale = 1.0 / math.sqrt(HD)
    myself = lax.axis_index("ctx")
    local_first = myself * rows_here
    local_places = local_first + jnp.arange(rows_here, dtype=jnp.int32)
    lower = jnp.repeat(starts, QBLK, total_repeat_length=rows_here)
    least_lower = jnp.min(lower)
    query_heads = queries.reshape(rows_here, heads_here, HD)
    cot_heads = attn_cot.reshape(rows_here, heads_here, HD)
    key_heads = keys_values[0].reshape(rows_here, heads_here, HD)
    value_heads = keys_values[1].reshape(rows_here, heads_here, HD)
    zeros = jnp.zeros((rows_here, heads_here, HD), jnp.float32)
    piece = lax.all_gather(keys_values, "ctx", axis=1, tiled=True)

    def key_one_block(inner_loop, offset):
        sub = math.gcd(piece.shape[1], 1024)
        key_first = offset
        live = (key_first <= local_first + rows_here - 1) & (key_first + sub - 1 >= least_lower)

        def key_working(values):
            part = lax.dynamic_slice_in_dim(piece, offset, sub, 1)
            key_part = part[0].reshape(sub, heads_here, HD)
            value_part = part[1].reshape(sub, heads_here, HD)
            key_places = key_first + jnp.arange(sub, dtype=jnp.int32)
            scores, squash, seen = pair_scores(
                query_heads, key_part, local_places, lower, key_places
            )
            dscore = score_grads(scores, squash, seen, cot_heads, value_part, seq_len)
            return values + jnp.einsum(
                "hij,jhd->ihd", dscore, key_part, preferred_element_type=jnp.float32
            )

        return lax.cond(live, key_working, lambda values: values, inner_loop)

    query_grad = over_blocks(piece.shape[1], key_one_block, zeros)
    query_piece = (
        lax.all_gather(queries, "ctx", axis=0, tiled=True),
        lax.all_gather(attn_cot, "ctx", axis=0, tiled=True),
        lax.all_gather(lower, "ctx", axis=0, tiled=True),
    )

    def query_one_block(inner_loop, offset):
        sub = math.gcd(query_piece[0].shape[0], 1024)
        query_first = offset
        query_lower = lax.dynamic_slice_in_dim(query_piece[2], offset, sub, 0)
        live = (local_first <= query_first + sub - 1) & (
            local_first + rows_here - 1 >= jnp.min(query_lower)
        )

        def query_working(values):
            query_part = lax.dynamic_slice_in_dim(query_piece[0], offset, sub, 0).reshape(
                sub, heads_here, HD
            )
            cotangent_piece = lax.dynamic_slice_in_dim(query_piece[1], offset, sub, 0).reshape(
                sub, heads_here, HD
            )
            query_places = query_first + jnp.arange(sub, dtype=jnp.int32)
            scores, squash, seen = pair_scores(
                query_part, key_heads, query_places, query_lower, local_places
            )
            weights = score_weights(scores, squash, seen, seq_len)
            dscore = score_grads(scores, squash, seen, cotangent_piece, value_heads, seq_len)
            key_add = jnp.einsum(
                "hij,ihd->jhd", dscore, query_part, preferred_element_type=jnp.float32
            )
            value_add = jnp.einsum(
                "hij,ihd->jhd", weights, cotangent_piece, preferred_element_type=jnp.float32
            )
            return (values[0] + key_add, values[1] + value_add)

        return lax.cond(live, query_working, lambda values: values, inner_loop)

    key_grad, value_grad = over_blocks(query_piece[0].shape[0], query_one_block, (zeros, zeros))
    head_grads = (
        jnp.stack([query_grad * scale, key_grad * scale, value_grad])
        .astype(jnp.bfloat16)
        .reshape(3, rows_here, feature_cols)
    )
    partial_grad = jnp.einsum(
        "mtc,mdc->td", head_grads, qkv_weight, preferred_element_type=jnp.float32
    )
    head_cols = adapter.shape[1]
    first_col = lax.axis_index("head") * head_cols
    layer_grad = lax.psum(partial_grad.astype(jnp.bfloat16), "head").astype(jnp.float32)
    layer_grad_b = layer_grad.astype(jnp.bfloat16)
    own_grad = lax.dynamic_slice_in_dim(layer_grad, first_col, head_cols, 1)
    row_grads = own_grad + jnp.dot(layer_grad_b, adapter, preferred_element_type=jnp.float32)
    own_rows = lax.dynamic_slice_in_dim(event_rows, first_col, head_cols, 1)
    adapter_grad = lax.psum_scatter(
        lax.dot_general(
            layer_grad_b, own_rows, (((0,), (0,)), ((), ())), preferred_element_type=jnp.float32
        ),
        "ctx",
        scatter_dimension=0,
        tiled=True,
    )
    capacity = max(2, 2 * rows_here // n_ctx)
    target = owners[:, 0]
    onehot = (target[:, None] == jnp.arange(n_ctx, dtype=jnp.int32)[None, :]).astype(jnp.int32)
    prior_blocks = jnp.cumsum(onehot, axis=0) - onehot
    ranking = jnp.sum(prior_blocks * onehot, axis=1)
    cell_index = target * capacity + ranking
    placing = cell_index[:, None] == jnp.arange(n_ctx * capacity, dtype=jnp.int32)[None, :]
    send_rows = lax.dot_general(
        placing.astype(jnp.float32),
        row_grads,
        (((0,), (0,)), ((), ())),
        precision=lax.Precision.HIGHEST,
    ).reshape(n_ctx, capacity, head_cols)
    send_slots = (jnp.sum(jnp.where(placing, slots[:, None] + 1, 0), axis=0) - 1).reshape(
        n_ctx, capacity
    )
    got_rows, got_slots = (
        lax.all_to_all(
            send_rows.astype(jnp.bfloat16), "ctx", split_axis=0, concat_axis=0, tiled=True
        ).astype(send_rows.dtype),
        lax.all_to_all(send_slots, "ctx", split_axis=0, concat_axis=0, tiled=True),
    )
    table_rows = table.shape[0]
    landing = got_slots.reshape(-1)[None, :] == jnp.arange(table_rows, dtype=jnp.int32)[:, None]
    summed = jnp.dot(
        landing.astype(jnp.float32),
        got_rows.reshape(n_ctx * capacity, head_cols),
        precision=lax.Precision.HIGHEST,
    )
    touched = jnp.sum(landing.astype(jnp.int32), axis=1) > 0
    new_table, new_m, new_v = adam_rows(summed, touched, table, moment_m, moment_v)
    return (adapter_grad, new_table, new_m, new_v)


BLOCK = 128
PAIR = 2 * BLOCK
META = 16
PART = PAIR + META
FAR_PART = PART + META
ACROSS_Y = [(i, i ^ 2) for i in range(16)]
FAR_OUT = [(i * 2, (i + 8) * 2) for i in range(8)] + [((i + 8) * 2 + 1, i * 2 + 1) for i in range(8)]
FAR_BACK = [(b, a) for a, b in FAR_OUT]
SWAP = [(0, 1), (1, 0)]
ROUNDS = (8, 4, 1, 2)
F32 = jnp.float32
BF16 = jnp.bfloat16
VMEM = pl.BlockSpec(memory_space=pltpu.VMEM)
SMEM = pl.BlockSpec(memory_space=pltpu.SMEM)


def dot(a, b, axis_a, axis_b):
    return lax.dot_general(a, b, (((axis_a,), (axis_b,)), ((), ())), preferred_element_type=F32)


def spot_of(me):
    return me // 4 % 2 * 2 + me % 2


def kernel_call(body, out_shape, operands, name, flops=0, in_bytes=0):
    specs = [SMEM if o.dtype == jnp.int32 and o.ndim == 1 else VMEM for o in operands]
    return pl.pallas_call(
        body,
        out_shape=out_shape,
        in_specs=specs,
        out_specs=jax.tree.map(lambda _: VMEM, out_shape),
        compiler_params=pltpu.CompilerParams(vmem_limit_bytes=12 * 1024 * 1024),
        cost_estimate=pl.CostEstimate(flops=flops, bytes_accessed=in_bytes, transcendentals=0),
        name=name,
    )(*operands)


def deal_body(starts, queries, keys_values, cot, rows, own, by_x, by_zl, by_both, held_rows, sems):
    core, me = lax.axis_index("head"), lax.axis_index("ctx")
    outs = (own, by_x, by_zl, by_both)
    start = starts[0]
    row = lax.broadcasted_iota(jnp.int32, (META, BLOCK), 0)
    meta = jnp.where(row == 0, start // BLOCK, jnp.where(row == 1, start % BLOCK, 0)).astype(F32).astype(BF16)
    cols = held_rows.shape[1]

    def copies(near, far, half):
        moves = []
        for flip, out in enumerate(outs):
            head = jnp.bitwise_xor(spot_of(me), flip)
            lanes = pl.ds(pl.multiple_of(head * BLOCK, BLOCK), BLOCK)
            for base, pair in ((0, near), (PART, far)):
                for at, source in enumerate(pair):
                    moves.append((source.at[:, lanes], out.at[base + at * BLOCK : base + (at + 1) * BLOCK, :]))
        moves.append((rows.at[:, half * cols : (half + 1) * cols], held_rows.at[:BLOCK, :]))
        moves = [pltpu.make_async_copy(a, b, sems.at[k]) for k, (a, b) in enumerate(moves)]
        for move in moves:
            move.start()
        held_rows[BLOCK:, :] = jnp.zeros((META, cols), BF16)
        for out in outs:
            out[PAIR:PART, :] = meta
            out[PART + PAIR : PART + PART, :] = meta
            out[PART + PART :, :] = jnp.zeros((META, BLOCK), BF16)
        for move in moves:
            move.wait()

    asks = (queries, cot)
    gives = (keys_values.at[0], keys_values.at[1])

    @pl.when(core == 0)
    def _():
        copies(asks, gives, 0)

    @pl.when(core == 1)
    def _():
        copies(gives, asks, 1)


def gather_body(own, rows_1, by_x, by_zl, by_both, rows_2, far, near, two):
    for flip, part in enumerate((own, by_x, by_zl, by_both)):
        near[flip] = part[:PART, :]
        far[flip] = part[PART:, :]
    count = two.shape[0] // 2
    two[:count, :] = rows_1[:count, :]
    two[count:, :] = rows_2[:count, :]


def lower_of(meta):
    meta = meta.astype(F32)
    return (meta[0:1] * BLOCK + meta[1:2]).astype(jnp.int32)


def attend(scale, role_q, crossing, nears, far, far_1, far_2, near_1_sum, near_2_sum, put_far_1, put_far_2):
    me = lax.axis_index("ctx")
    zh, y = me // 8, me // 2 % 2
    spots = [jnp.bitwise_xor(spot_of(me), flip) for flip in range(4)]
    places = [spot // 2 * 4 + spot % 2 for spot in spots]
    lane = lax.broadcasted_iota(jnp.int32, (1, BLOCK), 1)
    row_in = lax.broadcasted_iota(jnp.int32, (BLOCK, 4 * BLOCK), 0)
    never = 1 << 20
    far_zh = 1 - zh if crossing else zh
    place = jnp.concatenate([lane + (far_zh * 8 + y * 2 + s) * BLOCK for s in places], axis=1)
    base_1, base_2 = far_1[...], far_2[...]
    if not role_q:
        low = jnp.concatenate([lower_of(far[s, PAIR:PART, :]) for s in range(4)], axis=1)
    dscores, weights, firsts, seconds = [], [], [], []
    for chunk in range(4):
        rows = slice(chunk * PAIR, (chunk + 1) * PAIR)
        near_ref, near_y = nears[chunk // 2], (y, 1 - y)[chunk // 2]
        pair = (chunk % 2 * 2, chunk % 2 * 2 + 1)
        first = jnp.concatenate([near_ref[s, :BLOCK, :] for s in pair], axis=0)
        second = jnp.concatenate([near_ref[s, BLOCK:PAIR, :] for s in pair], axis=0)
        half = dot(first, base_1, 1, 1) * (0.5 * scale)
        dprod = dot(second, base_2, 1, 1)
        seen = []
        for s in pair:
            start = (zh * 8 + near_y * 2 + places[s]) * BLOCK
            if role_q:
                low = jnp.concatenate([lower_of(near_ref[s, PAIR:PART, :])] * 4, axis=1)
                seen.append(row_in >= jnp.where(place >= low, place - start, never))
            else:
                seen.append((row_in >= low - start) & (row_in <= place - start))
        seen = jnp.concatenate(seen, axis=0)
        tanh = jnp.tanh(half)
        twice = 1.0 + tanh
        weight = half * twice
        dscore = (dprod * twice) * (1.0 + half * (1.0 - tanh))
        weight = jnp.where(seen, weight, 0.0).astype(BF16)
        dscore = jnp.where(seen, dscore, 0.0).astype(BF16)
        grad_1 = dot(dscore, base_1, 1, 0)
        near_1_sum[rows, :] = near_1_sum[rows, :] + grad_1 if crossing else grad_1
        if not role_q:
            grad_2 = dot(weight, base_2, 1, 0)
            near_2_sum[rows, :] = near_2_sum[rows, :] + grad_2 if crossing else grad_2
        dscores.append(dscore)
        weights.append(weight)
        firsts.append(first)
        seconds.append(second)
    put_far_1(dot(jnp.concatenate(dscores, axis=0), jnp.concatenate(firsts, axis=0), 0, 0))
    if role_q:
        put_far_2(dot(jnp.concatenate(weights, axis=0), jnp.concatenate(seconds, axis=0), 0, 0))


def gather_far(far, far_1, far_2):
    for spot in range(4):
        rows = slice(spot * BLOCK, (spot + 1) * BLOCK)
        far_1[rows, :] = far[spot, :BLOCK, :]
        far_2[rows, :] = far[spot, BLOCK:PAIR, :]


def attend_own_body(scale, near_own, far_own, near_in, near_1_sum, near_2_sum, far_sum, far_1, far_2):
    gather_far(far_own, far_1, far_2)
    core = lax.axis_index("head")

    def put(at):
        def store(value):
            far_sum[at] = value

        return store

    rest = ((near_own, near_in), far_own, far_1, far_2, near_1_sum, near_2_sum, put(0), put(1))

    @pl.when(core == 0)
    def _():
        near_2_sum[...] = jnp.zeros_like(near_2_sum)
        attend(scale, True, False, *rest)

    @pl.when(core == 1)
    def _():
        far_sum[1] = jnp.zeros((4 * BLOCK, BLOCK), F32)
        attend(scale, False, False, *rest)


def attend_far_body(scale, seq_len, near_own, near_in, far_in, _1, _2, near_1_sum, near_2_sum, far_out, far_1, far_2):
    core, zh = lax.axis_index("head"), lax.axis_index("ctx") // 8
    far_out[...] = jnp.zeros_like(far_out)

    def put(at, factor):
        def store(value):
            for spot in range(4):
                far_out[spot, at * BLOCK : (at + 1) * BLOCK, :] = (value[spot * BLOCK : (spot + 1) * BLOCK] * factor).astype(BF16)

        return store

    puts = (put(0, scale * 0.5 / seq_len), put(1, 1.0 / seq_len))
    rest = ((near_own, near_in), far_in, far_1, far_2, near_1_sum, near_2_sum, *puts)

    @pl.when((core == 0) & (zh == 1))
    def _():
        gather_far(far_in, far_1, far_2)
        attend(scale, True, True, *rest)

    @pl.when((core == 1) & (zh == 0))
    def _():
        gather_far(far_in, far_1, far_2)
        attend(scale, False, True, *rest)


def near_body(scale, seq_len, near_1_sum, near_2_sum, out):
    for spot in range(4):
        rows = slice((4 + spot) * BLOCK, (5 + spot) * BLOCK)
        out[spot, 0] = (near_1_sum[rows, :] * (scale * 0.5 / seq_len)).astype(BF16)
        out[spot, 1] = (near_2_sum[rows, :] * (1.0 / seq_len)).astype(BF16)


def project_body(by_both, by_zl, by_x, own, weight, partial, sent, held):
    core, me = lax.axis_index("head"), lax.axis_index("ctx")
    for flip, part in enumerate((own, by_x, by_zl, by_both)):
        head = jnp.bitwise_xor(spot_of(me), flip)
        for slot in range(3):
            held[slot, :, pl.ds(pl.multiple_of(head * BLOCK, BLOCK), BLOCK)] = part[slot]
    total = dot(held[1], weight[2], 1, 1)
    total = total + dot(held[0], weight[core], 1, 1)
    total = total + dot(held[2], weight[1 - core], 1, 1)
    partial[...] = total
    sent[...] = total.astype(BF16)


def pack_body(own, other, adapter, placing, slots, out, grad, turned):
    core = lax.axis_index("head")
    n_ctx = out.shape[0]
    head_cols = adapter.shape[1]
    capacity = placing.shape[1] // n_ctx
    tiles = head_cols // BLOCK
    share = own.shape[1] // n_ctx // 2
    total = own[...] + other[...].astype(F32)
    grad[...] = total
    rounded = total.astype(BF16)
    turned[...] = jnp.transpose(rounded)
    rows = grad[:, pl.ds(pl.multiple_of(core * head_cols, head_cols), head_cols)]
    rows = rows + dot(rounded, adapter[...], 1, 0)
    rows = jnp.concatenate([rows.astype(BF16), slots[...]], axis=1)
    cells = dot(placing[...], rows, 0, 0).astype(BF16)
    for p in range(n_ctx):
        for tile in range(tiles + 1):
            out[p, tile * capacity : (tile + 1) * capacity, :] = cells[
                p * capacity : (p + 1) * capacity, tile * BLOCK : (tile + 1) * BLOCK
            ]
        first = pl.multiple_of(p * 2 * share + core * share, share)
        out[p, (tiles + 1) * capacity :, :] = turned[pl.ds(first, share), :]


def place_body(owners, slots, placing, marks):
    count = owners.shape[1]
    capacity = placing.shape[1] // 16
    lane = lax.broadcasted_iota(jnp.int32, (count, BLOCK), 1)
    row = lax.broadcasted_iota(jnp.int32, (count, BLOCK), 0)
    owner_row = jnp.broadcast_to(owners[...].astype(F32), (count, BLOCK))
    owner = jnp.transpose(owner_row)
    same = jnp.where((owner == owner_row) & (lane < row), 1.0, 0.0)
    ranking = jnp.sum(same, axis=1, keepdims=True)
    cell = owner * capacity + ranking
    for tile in range(placing.shape[1] // BLOCK):
        hit = cell == (lane + tile * BLOCK).astype(F32)
        placing[:, tile * BLOCK : (tile + 1) * BLOCK] = hit.astype(F32).astype(BF16)
    mark = jnp.broadcast_to(slots[...] + 1, (count, BLOCK)).astype(F32)
    marks[...] = jnp.transpose(mark).astype(BF16)


def merge_body(flips, scale, seq_len, far, near, near_1_sum, near_2_sum, far_sum, *outs):
    grad_scale, weight_scale = scale * 0.5 / seq_len, 1.0 / seq_len
    for flip, out in zip(flips, outs):
        rows = slice(flip * BLOCK, (flip + 1) * BLOCK)
        out[0] = (near_1_sum[rows, :] * grad_scale + near[flip, 0].astype(F32)).astype(BF16)
        both = (near_2_sum[rows, :] + far_sum[1, rows, :]) * weight_scale
        out[1] = (both + near[flip, 1].astype(F32) + far[flip, BLOCK:PAIR, :].astype(F32)).astype(BF16)
        out[2] = (far_sum[0, rows, :] * grad_scale + far[flip, :BLOCK, :].astype(F32)).astype(BF16)


def finish_body(got, other, *refs):
    pieces, held, grad, targets = refs[:8], refs[8:11], refs[11], refs[12:15]
    made, rows_held, in_sems, out_sems = refs[15:18], refs[18], refs[19], refs[20]
    chunks = out_sems.shape[1]
    span = held[0].shape[0] // chunks

    def rows_of(c):
        return slice(c * span, (c + 1) * span)

    stores = [
        [pltpu.make_async_copy(a.at[rows_of(c), :], b.at[rows_of(c), :], out_sems.at[k, c]) for k, (a, b) in enumerate(zip(made, targets))]
        for c in range(chunks)
    ]
    part = rows_held.shape[0] // 8
    loads = [pltpu.make_async_copy(p, rows_held.at[k * part : (k + 1) * part, :], in_sems.at[k]) for k, p in enumerate(pieces)]
    for move in loads:
        move.start()
    core, me = lax.axis_index("head"), lax.axis_index("ctx")
    share = other.shape[1]
    tiles = held[0].shape[1] // BLOCK
    table_rows = held[0].shape[0]
    n_ctx = got.shape[0]
    capacity = (got.shape[1] - share) // (tiles + 1)
    marks = got[:, tiles * capacity : (tiles + 1) * capacity, :].reshape(n_ctx * capacity, BLOCK).astype(F32)
    lane = lax.broadcasted_iota(jnp.int32, marks.shape, 1)
    landing = [(marks == (lane + (at * BLOCK + 1)).astype(F32)).astype(F32) for at in range(table_rows // BLOCK)]
    landing = jnp.concatenate(landing, axis=1).astype(BF16)
    cells = [got[:, tile * capacity : (tile + 1) * capacity, :].reshape(n_ctx * capacity, BLOCK) for tile in range(tiles)]
    cells = jnp.concatenate(cells + [jnp.ones(marks.shape, BF16)], axis=1)
    summed_all = dot(landing, cells, 0, 0)
    for c in range(chunks):
        rows = rows_of(c)
        summed = summed_all[rows, : tiles * BLOCK]
        touched = jnp.concatenate([summed_all[rows, tiles * BLOCK :]] * tiles, axis=1) > 0.0
        old, m, v = [ref[rows, :] for ref in held]
        fresh_m = beta_first * m + (1.0 - beta_first) * summed
        fresh_v = beta_second * v + (1.0 - beta_second) * summed * summed
        update = learn_rate * (fresh_m / first_fix) / (jnp.sqrt(fresh_v / second_fix) + epsilon)
        made[0][rows, :] = jnp.where(touched, old - update, old)
        made[1][rows, :] = jnp.where(touched, fresh_m, m)
        made[2][rows, :] = jnp.where(touched, fresh_v, v)
        for move in stores[c]:
            move.start()
    masks = [0]
    for bit in ROUNDS:
        masks = masks + [mask ^ bit for mask in masks]
    senders = [jnp.bitwise_xor(me, mask) for mask in masks]
    width = (tiles + 1) * capacity
    mine_t = jnp.concatenate([got[s, width:, :] for s in senders], axis=1)
    other_t = jnp.concatenate([other[s] for s in senders], axis=1)
    both_t = jnp.concatenate([mine_t, other_t], axis=0)
    for move in loads:
        move.wait()
    both = dot(both_t, rows_held[...], 1, 0)
    grad[pl.ds(pl.multiple_of(core * share, share), share), :] = both[:share]
    grad[pl.ds(pl.multiple_of((1 - core) * share, share), share), :] = both[share:]
    for store in stores:
        for move in store:
            move.wait()


def dealt_device(
    queries,
    keys_values,
    attn_cot,
    event_rows,
    adapter,
    qkv_weight,
    starts,
    owners,
    slots,
    table,
    moment_m,
    moment_v,
):
    shape = jax.ShapeDtypeStruct
    n_ctx = lax.axis_size("ctx")
    rows_here = queries.shape[0]
    seq_len = rows_here * n_ctx
    head_cols = adapter.shape[1]
    width = event_rows.shape[1]
    capacity = max(2, 2 * rows_here // n_ctx)
    dealt = shape((PART + FAR_PART, BLOCK), BF16)
    *dealt, own_rows = pl.pallas_call(
        deal_body,
        out_shape=(dealt,) * 4 + (shape((rows_here + META, head_cols), BF16),),
        in_specs=[SMEM] + [pl.BlockSpec(memory_space=pltpu.HBM)] * 4,
        out_specs=(VMEM,) * 5,
        scratch_shapes=[pltpu.SemaphoreType.DMA((17,))],
        compiler_params=pltpu.CompilerParams(vmem_limit_bytes=12 * 1024 * 1024),
        name="deal",
    )(starts, queries, keys_values, attn_cot, event_rows)

    def exchange(sent, bit):
        return lax.ppermute(sent, "ctx", [(i, i ^ bit) for i in range(16)])

    zh_rows = exchange(own_rows, ROUNDS[0])
    both, by_zl, by_x = [exchange(part, bit) for part, bit in zip(dealt[:0:-1], (5, 4, 1))]
    zh_rows, both, by_zl, by_x = lax.optimization_barrier((zh_rows, both, by_zl, by_x))
    far_own, near_own, two = kernel_call(
        gather_body,
        (shape((4, FAR_PART, BLOCK), BF16), shape((4, PART, BLOCK), BF16), shape((2 * rows_here, head_cols), BF16)),
        (dealt[0], own_rows, by_x, by_zl, both, zh_rows),
        "gather",
    )
    far_in = lax.ppermute(far_own, ("ctx", "head"), FAR_OUT)
    near_in = lax.ppermute(near_own, "ctx", ACROSS_Y)
    zl_rows, x_rows = [exchange(two, bit) for bit in ROUNDS[1:3]]
    scales = (1.0 / math.sqrt(HD), float(seq_len))
    side_scratch = [pltpu.VMEM((4 * BLOCK, BLOCK), BF16)] * 2
    near_sum = shape((8 * BLOCK, BLOCK), F32)
    cost = pl.CostEstimate(flops=10**9, bytes_accessed=2**20, transcendentals=0)
    near_1, near_2, far_sum = pl.pallas_call(
        functools.partial(attend_own_body, scales[0]),
        out_shape=(near_sum, near_sum, shape((2, 4 * BLOCK, BLOCK), F32)),
        in_specs=[VMEM] * 3,
        out_specs=(VMEM,) * 3,
        scratch_shapes=side_scratch,
        compiler_params=pltpu.CompilerParams(vmem_limit_bytes=12 * 1024 * 1024),
        cost_estimate=cost,
        name="attend_own",
    )(near_own, far_own, near_in)
    near_1, near_2, two_y = lax.optimization_barrier((near_1, near_2, two))
    y_rows = exchange(two_y, ROUNDS[3])
    near_1, near_2, far_out = pl.pallas_call(
        functools.partial(attend_far_body, *scales),
        out_shape=(near_sum, near_sum, shape((4, PART, BLOCK), BF16)),
        in_specs=[VMEM] * 5,
        out_specs=(VMEM,) * 3,
        scratch_shapes=side_scratch,
        input_output_aliases={3: 0, 4: 1},
        compiler_params=pltpu.CompilerParams(vmem_limit_bytes=12 * 1024 * 1024),
        cost_estimate=cost,
        name="attend_far",
    )(near_own, near_in, far_in, near_1, near_2)
    near_1, near_2, far_out, zl_rows, x_rows, y_rows = lax.optimization_barrier(
        (near_1, near_2, far_out, zl_rows, x_rows, y_rows)
    )
    near_out = kernel_call(
        functools.partial(near_body, *scales), shape((4, 2, BLOCK, BLOCK), BF16), (near_1, near_2), "near"
    )
    zl_x_rows = exchange(zl_rows, ROUNDS[2])
    zl_y_rows = exchange(zl_rows, ROUNDS[3])
    far_back = lax.ppermute(far_out, ("ctx", "head"), FAR_BACK)
    near_back = lax.ppermute(near_out, "ctx", ACROSS_Y)
    sums = (far_back, near_back, near_1, near_2, far_sum)
    part = shape((3, BLOCK, BLOCK), BF16)
    (both,) = kernel_call(functools.partial(merge_body, (3,), *scales), (part,), sums, "merge_both")
    both, *sums = lax.optimization_barrier((both, *sums))
    own, *parts = kernel_call(functools.partial(merge_body, (0, 1, 2), *scales), (part,) * 3, sums, "merge")
    both, *parts, zl_x_rows = lax.optimization_barrier((both, *parts, zl_x_rows))
    x_y_rows, zl_x_y_rows = exchange(y_rows, ROUNDS[2]), exchange(zl_x_rows, ROUNDS[3])
    both, by_zl, by_x = [exchange(part, bit) for part, bit in zip((both, parts[1], parts[0]), (5, 4, 1))]
    both, by_zl, by_x, zl_y_rows, zl_x_y_rows = lax.optimization_barrier((both, by_zl, by_x, zl_y_rows, zl_x_y_rows))
    partial, sent = pl.pallas_call(
        project_body,
        out_shape=(shape((rows_here, width), F32), shape((rows_here, width), BF16)),
        in_specs=[VMEM] * 5,
        out_specs=(VMEM, VMEM),
        scratch_shapes=[pltpu.VMEM((3, rows_here, queries.shape[1]), BF16)],
        compiler_params=pltpu.CompilerParams(vmem_limit_bytes=12 * 1024 * 1024),
        name="project",
    )(both, by_zl, by_x, own, qkv_weight)
    sent, owners, slots = lax.optimization_barrier((sent, owners, slots))
    placing, marks = kernel_call(
        place_body,
        (shape((rows_here, n_ctx * capacity), BF16), shape((rows_here, BLOCK), BF16)),
        (owners.reshape(1, rows_here), slots.reshape(1, rows_here)),
        "place",
    )
    other = lax.ppermute(sent, "head", SWAP)
    other, x_y_rows = lax.optimization_barrier((other, x_y_rows))
    share = width // n_ctx // 2
    packed_rows = capacity * (head_cols // BLOCK + 1)
    packed = pl.pallas_call(
        pack_body,
        out_shape=shape((n_ctx, packed_rows + share, BLOCK), BF16),
        in_specs=[VMEM] * 5,
        out_specs=VMEM,
        scratch_shapes=[pltpu.VMEM((rows_here, width), F32), pltpu.VMEM((width, rows_here), BF16)],
        compiler_params=pltpu.CompilerParams(vmem_limit_bytes=12 * 1024 * 1024),
        name="pack",
    )(partial, other, adapter, placing, marks)
    got = lax.all_to_all(packed, "ctx", 0, 0, tiled=True)
    other_share = lax.ppermute(got[:, packed_rows:], "head", SWAP)
    held = shape(table.shape, F32)
    pieces = (two, zl_rows, x_rows, zl_x_rows, y_rows, zl_y_rows, x_y_rows, zl_x_y_rows)
    return pl.pallas_call(
        finish_body,
        out_shape=(shape((width // n_ctx, head_cols), F32), held, held, held),
        in_specs=[VMEM] * 2 + [pl.BlockSpec(memory_space=pl.ANY)] * len(pieces) + [VMEM] * 3,
        out_specs=(VMEM,) + (pl.BlockSpec(memory_space=pl.ANY),) * 3,
        scratch_shapes=[pltpu.VMEM(table.shape, F32)] * 3
        + [
            pltpu.VMEM((n_ctx * rows_here, head_cols), BF16),
            pltpu.SemaphoreType.DMA((len(pieces),)),
            pltpu.SemaphoreType.DMA((3, 4)),
        ],
        compiler_params=pltpu.CompilerParams(vmem_limit_bytes=12 * 1024 * 1024),
        name="finish",
    )(got, other_share, *pieces, table, moment_m, moment_v)


def per_device(*arrays):
    rows_here, cols_here = arrays[0].shape
    fits = lax.axis_size("ctx") == 16 and lax.axis_size("head") == 2
    if fits and rows_here == BLOCK and cols_here == 4 * HD and arrays[9].shape[0] == 2 * BLOCK:
        return dealt_device(*arrays)
    return plain_device(*arrays)


def solution(mesh):
    placed = (
        P("ctx", "head"),
        P(None, "ctx", "head"),
        P("ctx", "head"),
        P("ctx", None),
        P(None, "head"),
        P(None, None, "head"),
        P("ctx"),
        P("ctx", None),
        P("ctx"),
        P("ctx", "head"),
        P("ctx", "head"),
        P("ctx", "head"),
    )
    return jax.shard_map(
        per_device,
        mesh=mesh,
        in_specs=placed,
        out_specs=(P("ctx", "head"), P("ctx", "head"), P("ctx", "head"), P("ctx", "head")),
        check_vma=False,
    )
```
